32 devices in a mesh: expert: 8 (over y, x, core), fsdp: 4 (over z).
Axes of the slice: x: 2, y: 2, z: 4, core: 2. Of those that a mesh axis runs over, the one named last changes fastest.
Arguments:
- tokens: bfloat16 [12288, 2048], P(('expert', 'fsdp')), may hold values from -6 to 6
- routes: int32 [12288, 4], P(('expert', 'fsdp')), may hold values from 0 to 7, all different within a row; in each aligned block of 384 rows (0 to 383, 384 to 767, ...) at most 256 rows name the same one
- seq_lengths: int32 [8, 3], P('expert'), may hold values from 1 to 1024, 1536 in all within a row
- cotangent: bfloat16 [12288, 2048], P(('expert', 'fsdp')), may hold values from -6 to 6
- norm1_gain: bfloat16 [2048], replicated, may hold values from 0.5 to 1.5
- query_weight: bfloat16 [2048, 2048], P(None, 'fsdp'), may hold values from -0.125 to 0.125
- query_bias: bfloat16 [2048], P('fsdp'), may hold values from -1.25 to 1.25
- key_weight: bfloat16 [2048, 2048], P(None, 'fsdp'), may hold values from -0.125 to 0.125
- key_bias: bfloat16 [2048], P('fsdp'), may hold values from -1.25 to 1.25
- value_weight: bfloat16 [2048, 2048], P(None, 'fsdp'), may hold values from -0.125 to 0.125
- value_bias: bfloat16 [2048], P('fsdp'), may hold values from -1.25 to 1.25
- out_weight: bfloat16 [2048, 2048], P('fsdp'), may hold values from -1 to 1
- norm2_gain: bfloat16 [2048], replicated, may hold values from 0.5 to 1.5
- router_weight: bfloat16 [2048, 8], replicated, may hold values from -0.0625 to 0.0625
- shared_switch: bfloat16 [2048], replicated, may hold values from -0.125 to 0.125
- shared_gate: bfloat16 [2048, 5632], P(None, 'fsdp'), may hold values from -0.125 to 0.125
- shared_up: bfloat16 [2048, 5632], P(None, 'fsdp'), may hold values from -0.125 to 0.125
- shared_down: bfloat16 [5632, 2048], P('fsdp'), may hold values from -0.078125 to 0.078125
- expert_gate: bfloat16 [8, 2048, 1408], P('expert', 'fsdp'), may hold values from -0.125 to 0.125
- expert_up: bfloat16 [8, 2048, 1408], P('expert', 'fsdp'), may hold values from -0.125 to 0.125
- expert_down: bfloat16 [8, 1408, 2048], P('expert', None, 'fsdp'), may hold values from -0.625 to 0.625
Outputs:
- block_out: bfloat16 [12288, 2048], P(('expert', 'fsdp'))
- grad_tokens: float32 [12288, 2048], P(('expert', 'fsdp'))
- grad_norm1_gain: float32 [2048], replicated
- grad_query_weight: float32 [2048, 2048], P(None, 'fsdp')
- grad_query_bias: float32 [2048], P('fsdp')
- grad_key_weight: float32 [2048, 2048], P(None, 'fsdp')
- grad_key_bias: float32 [2048], P('fsdp')
- grad_value_weight: float32 [2048, 2048], P(None, 'fsdp')
- grad_value_bias: float32 [2048], P('fsdp')
- grad_out_weight: float32 [2048, 2048], P('fsdp')
- grad_norm2_gain: float32 [2048], replicated
- grad_router_weight: float32 [2048, 8], replicated
- grad_shared_switch: float32 [2048], replicated
- grad_shared_gate: float32 [2048, 5632], P(None, 'fsdp')
- grad_shared_up: float32 [2048, 5632], P(None, 'fsdp')
- grad_shared_down: float32 [5632, 2048], P('fsdp')
- grad_expert_gate: float32 [8, 2048, 1408], P('expert', 'fsdp')
- grad_expert_up: float32 [8, 2048, 1408], P('expert', 'fsdp')
- grad_expert_down: float32 [8, 1408, 2048], P('expert', None, 'fsdp')
The draws below stay inside these ranges and needn't reach their ends.
Inputs may be any that keep to these rules, and one draw needn't show every extreme that they name: `routes`: A token names 4 different experts. In the rows of one device (384 consecutive rows) no expert is named by more than 256 rows, a bound that some block reaches. `seq_lengths`: each row sums to 1536, and its largest length is exactly 1024.
All inputs are finite; a program needn't handle non-finite values.
Results may differ from the reference program's by a relative error of at most 0.025.
Values may be sent and summed in bfloat16 or wider, within the bound.
A program may use at most 448 MiB of HBM per device.

```python
import math
import jax
import jax.numpy as jnp
import numpy as np
from jax import lax

D = 2048
HEADS = 16
HEAD_DIM = 128
SFF = 5632
EFF = 1408
TOP = 4
LONGEST = 1024
GROUP = 1536
TOK_DEV = 384
SEQS = 3
EXPERTS = 8
CAP = 256
TOKENS = 12288
N_EXPERT = 8
N_FSDP = 4


def block_levels(own_key, dims, cuts, least, largest):
    def one(dim, shards_of):
        draws = jax.random.uniform(jax.random.fold_in(jax.random.fold_in(own_key, 6), dim), (shards_of,), jnp.float32, least / len(cuts), largest / len(cuts))
        return jnp.repeat(jnp.exp(draws), dims[dim] // shards_of).reshape((-1,) + (1,) * (len(dims) - dim - 1))

    factor_of = one(*cuts[0])
    for cut in cuts[1:]:
        factor_of = factor_of * one(*cut)
    return factor_of


def profile(number_of, total, bound, skew):
    weights = [(1 << 20) // math.isqrt(standing ** skew) + 1 for standing in range(2, number_of + 1)]
    rest, counts = total - bound - (number_of - 1), [1] * (number_of - 1)
    while rest > 0:
        movable = [i for i in range(number_of - 1) if counts[i] < bound]
        whole, left = sum([weights[i] for i in movable]), rest
        for i in movable:
            addition = min(bound - counts[i], max(1, left * weights[i] // whole), rest)
            counts[i] = counts[i] + addition
            rest = rest - addition
    return np.array([bound] + counts)


def uneven(own_key, number_of, total, bound, lean):
    if number_of == 2:
        one = jax.random.randint(own_key, (), max(1, total - bound), min(bound, total - 1) + 1)
        return jnp.stack([one, total - one])
    sizes = jnp.asarray(profile(number_of, total, bound, lean), jnp.int32)
    pairs = (number_of - 1) // 2
    giver, receiver = sizes[1:1 + 2 * pairs:2], sizes[2:2 + 2 * pairs:2]
    room = jnp.minimum(giver - 1, bound - receiver)
    moved = jax.random.randint(jax.random.fold_in(own_key, 1), (pairs,), 0, 1 << 20) % (room + 1)
    sizes = sizes.at[1:1 + 2 * pairs:2].set(giver - moved).at[2:2 + 2 * pairs:2].set(receiver + moved)
    return sizes[jax.random.permutation(jax.random.fold_in(own_key, 2), number_of)]


def deal_out(stream_key, own, number, rows, amount, top, most, lean):
    ranking = jax.random.permutation(stream_key, amount)
    packed, usual = shares(amount, rows * top, most, lean, True), shares(amount, rows * top, most, lean, False)
    places = jnp.arange(amount)

    def named(tallies, turn):
        used = int((tallies > 0).sum())
        fixed = max(1, used // 4)
        shifted = fixed + (places - fixed + turn * (used - fixed)) % max(1, amount - fixed)
        return jnp.zeros((amount,), jnp.int32).at[ranking[jnp.where(places < fixed, places, shifted)]].set(jnp.asarray(tallies, jnp.int32))

    tallies = jnp.where(number % 4 == 0, named(packed, number // 4), named(usual, number - number // 4 - 1))
    mixed = jax.random.permutation(jax.random.fold_in(own, 3), amount)
    giver, sink = mixed[0:amount // 2 * 2:2], mixed[1:amount // 2 * 2:2]
    slack = jnp.minimum(tallies[giver] - 1, most - tallies[sink]) // 2
    slack = jnp.where((giver == ranking[0]) | (sink == ranking[0]) | (tallies[sink] == 0), 0, jnp.maximum(slack, 0))
    shifted = jax.random.randint(jax.random.fold_in(own, 4), (amount // 2,), 0, 1 << 20) % (slack + 1)
    tallies = tallies.at[giver].add(-shifted).at[sink].add(shifted)
    labels = jnp.searchsorted(jnp.cumsum(tallies), jnp.arange(rows * top), side="right").astype(jnp.int32)
    table = labels.reshape(top, rows).T
    table = table[jax.random.permutation(jax.random.fold_in(own, 1), rows)]
    turn = jax.random.randint(jax.random.fold_in(own, 2), (rows, 1), 0, top)
    return jnp.take_along_axis(table, (jnp.arange(top)[None, :] + turn) % top, axis=1)


def shares(number_of, total, limit, lean, full):
    portions = [(1 << 20) // math.isqrt(rank ** lean) + 1 for rank in range(1, number_of + 1)]
    largest = limit if full else min(limit, max(-(-total // number_of), total * portions[0] // sum(portions)))
    least = 1 if total - largest >= number_of - 1 else 0
    holding, surplus = [largest] + [least] * (number_of - 1), total - largest - least * (number_of - 1)
    while surplus > 0:
        movable = [i for i in range(1, number_of) if holding[i] < largest] or [i for i in range(1, number_of) if holding[i] < limit]
        whole, budget = sum([portions[i] for i in movable]), surplus
        for i in movable:
            extra = min(limit - holding[i], max(1, budget * portions[i] // whole), surplus)
            holding[i] = holding[i] + extra
            surplus = surplus - extra
    return np.array(holding)


def scatter_about(key, extent, spread, reach, cuts=(), held_as=jnp.bfloat16):
    values = jax.random.normal(key, extent, jnp.float32) * spread
    if len(cuts) > 0:
        values = block_levels(key, extent, cuts, -0.22, 0.18) * values
    return jnp.clip(values, min=-reach, max=reach).astype(held_as)


def setup_inputs(seed: int = 0) -> dict:
    key_of = jax.random.split(jax.random.key(seed), 22)
    tokens = scatter_about(key_of[0], (TOKENS, D), 1.0, 6.0, ((0, 32),))
    routes_keys = jax.random.split(jax.random.fold_in(key_of[1], 1), TOKENS // TOK_DEV)
    routes_turns = jax.random.permutation(jax.random.fold_in(key_of[1], 3), TOKENS // TOK_DEV)
    routes = jax.vmap(lambda own, number: deal_out(jax.random.fold_in(key_of[1], 2), own, number, TOK_DEV, EXPERTS, TOP, CAP, 2))(routes_keys, routes_turns).reshape((TOKENS, TOP))
    seq_lengths = jax.vmap(lambda own: uneven(own, SEQS, GROUP, LONGEST, 2))(jax.random.split(key_of[2], N_EXPERT)).reshape((N_EXPERT, SEQS)).astype(jnp.int32)
    cotangent = scatter_about(key_of[3], (TOKENS, D), 1.0, 6.0, ((0, 32),))
    norm1_gain = jnp.clip(1.0 + 0.1 * jax.random.normal(key_of[4], (D,), jnp.float32), 0.5, 1.5).astype(jnp.bfloat16)
    query_weight = scatter_about(key_of[5], (D, D), D ** -0.5, 0.125, ((1, 4),))
    query_bias = scatter_about(key_of[6], (D,), 0.2, 1.25, ((0, 4),))
    key_weight = scatter_about(key_of[7], (D, D), D ** -0.5, 0.125, ((1, 4),))
    key_bias = scatter_about(key_of[8], (D,), 0.2, 1.25, ((0, 4),))
    value_weight = scatter_about(key_of[9], (D, D), D ** -0.5, 0.125, ((1, 4),))
    value_bias = scatter_about(key_of[10], (D,), 0.2, 1.25, ((0, 4),))
    out_weight = scatter_about(key_of[11], (D, D), (D // 64) ** -0.5, 1.0, ((0, 4),))
    norm2_gain = jnp.clip(1.0 + 0.1 * jax.random.normal(key_of[12], (D,), jnp.float32), 0.5, 1.5).astype(jnp.bfloat16)
    router_weight = scatter_about(key_of[13], (D, EXPERTS), (4 * D) ** -0.5, 0.0625)
    shared_switch = scatter_about(key_of[14], (D,), D ** -0.5, 0.125)
    shared_gate = scatter_about(key_of[15], (D, SFF), D ** -0.5, 0.125, ((1, 4),))
    shared_up = scatter_about(key_of[16], (D, SFF), D ** -0.5, 0.125, ((1, 4),))
    shared_down = scatter_about(key_of[17], (SFF, D), SFF ** -0.5, 0.078125, ((0, 4),))
    expert_gate = scatter_about(key_of[18], (EXPERTS, D, EFF), D ** -0.5, 0.125, ((0, 8), (1, 4)))
    expert_up = scatter_about(key_of[19], (EXPERTS, D, EFF), D ** -0.5, 0.125, ((0, 8), (1, 4)))
    expert_down = scatter_about(key_of[20], (EXPERTS, EFF, D), (EFF // 16) ** -0.5, 0.625, ((0, 8), (2, 4)))
    return {"tokens": tokens, "routes": routes, "seq_lengths": seq_lengths, "cotangent": cotangent, "norm1_gain": norm1_gain, "query_weight": query_weight, "query_bias": query_bias, "key_weight": key_weight, "key_bias": key_bias, "value_weight": value_weight, "value_bias": value_bias, "out_weight": out_weight, "norm2_gain": norm2_gain, "router_weight": router_weight, "shared_switch": shared_switch, "shared_gate": shared_gate, "shared_up": shared_up, "shared_down": shared_down, "expert_gate": expert_gate, "expert_up": expert_up, "expert_down": expert_down}


@jax.custom_vjp
def low(v):
    return lax.optimization_barrier(v.astype(jnp.bfloat16)).astype(jnp.float32)

@jax.custom_vjp
def low_back(v):
    return v

def low_keep(v):
    return (low(v), None)

def low_pass(kept, grad):
    return (grad,)

def back_keep(v):
    return (v, None)

def back_low(kept, grad):
    return (low(grad),)
low.defvjp(low_keep, low_pass)
low_back.defvjp(back_keep, back_low)
EPSILON = 1e-06
THETA = 1000000.0
MASKED = -1e+30
PRECISE = lax.Precision.HIGHEST

def product(left_matrix, right_matrix):
    return jnp.dot(left_matrix, right_matrix, precision=PRECISE, preferred_element_type=jnp.float32)

def rms_rate(values):
    return lax.rsqrt(lax.optimization_barrier(jnp.mean(values * values, axis=-1, keepdims=True)) + EPSILON)

def token_layout(lengths, count):
    ends = jnp.cumsum(lengths).astype(jnp.int32)
    places = jnp.arange(count, dtype=jnp.int32)
    passed = (places[:, None] >= ends[None, :]).astype(jnp.int32)
    segment = lax.optimization_barrier(jnp.sum(passed, axis=1)).astype(jnp.int32)
    start = lax.optimization_barrier(jnp.sum(passed * lengths[None, :], axis=1)).astype(jnp.int32)
    return (segment, places - start)

def rotary_tables(positions, width):
    half_width = width // 2
    inverse = THETA ** (-2.0 * jnp.arange(half_width, dtype=jnp.float32) / width)
    angle = positions.astype(jnp.float32)[:, None] * inverse[None, :]
    return (jnp.cos(angle)[:, None, :], jnp.sin(angle)[:, None, :])

def rotate(values, cosine, sine):
    half_width = values.shape[-1] // 2
    first_half = values[..., :half_width]
    second_half = values[..., half_width:]
    return jnp.concatenate([first_half * cosine - second_half * sine, second_half * cosine + first_half * sine], axis=-1)

def attend(queries, keys_all, values_all, segment, positions):
    count = queries.shape[0]
    block_rows = math.gcd(count, 512)
    factor = 1.0 / math.sqrt(queries.shape[-1])

    def one_block(block_index):
        start = block_index * block_rows
        query_rows = lax.dynamic_slice_in_dim(queries, start, block_rows, 0)
        segment_rows = lax.dynamic_slice_in_dim(segment, start, block_rows, 0)
        position_rows = lax.dynamic_slice_in_dim(positions, start, block_rows, 0)
        scores = jnp.einsum('qhd,khd->hqk', query_rows, keys_all, precision=PRECISE) * factor
        scores = low_back(scores)
        allowed = (segment_rows[:, None] == segment[None, :]) & (position_rows[:, None] >= positions[None, :])
        scores = jnp.where(allowed[None], scores, MASKED)
        soft_weights = jax.nn.softmax(scores, axis=-1)
        return jnp.einsum('hqk,khd->qhd', low(soft_weights), values_all, precision=PRECISE)
    blocks = lax.map(jax.checkpoint(one_block), jnp.arange(count // block_rows, dtype=jnp.int32))
    return blocks.reshape(count, -1)

def expert_mix(normed_second, routes, gates, expert_gate, expert_up, expert_down):
    count = normed_second.shape[0]
    pair_count = count * TOP
    flat_routes = routes.reshape(pair_count)
    flat_gates = gates.reshape(pair_count)
    padded = jnp.concatenate([normed_second, jnp.zeros((1, normed_second.shape[1]), normed_second.dtype)], 0)
    most_rows = N_FSDP * CAP

    def one_expert(total, stack):
        which, gate_mat, up_mat, down_mat = stack
        picked = jnp.nonzero(flat_routes == which, size=most_rows, fill_value=pair_count)[0].astype(jnp.int32)
        valid = picked < pair_count
        token_index = jnp.where(valid, picked // TOP, count).astype(jnp.int32)
        gate_of = jnp.where(valid, jnp.take(flat_gates, jnp.minimum(picked, pair_count - 1)), 0.0)
        sent_rows = low_back(padded[token_index])
        gate_pre = low_back(product(sent_rows, gate_mat))
        up_pre = low_back(product(sent_rows, up_mat))
        middle = low(jax.nn.silu(gate_pre) * up_pre)
        result = low(low_back(product(middle, down_mat)))
        return (total.at[token_index].add(gate_of[:, None] * result), None)
    total, unused = lax.scan(jax.checkpoint(one_expert), jnp.zeros_like(padded), (jnp.arange(EXPERTS, dtype=jnp.int32), expert_gate, expert_up, expert_down))
    return total[:count]

def group_forward(weights, group_tokens, group_routes, group_lengths):
    norm1_gain, query_weight, query_bias, key_weight, key_bias, value_weight, value_bias, out_weight, norm2_gain, router_weight, shared_switch, shared_gate, shared_up, shared_down, expert_gate, expert_up, expert_down = weights
    count = group_tokens.shape[0]
    segment, positions = token_layout(group_lengths, count)
    cosine, sine = rotary_tables(positions, HEAD_DIM)
    normed_first = low(group_tokens * rms_rate(group_tokens) * norm1_gain)
    query_pre = low_back(product(normed_first, query_weight) + query_bias)
    key_pre = low_back(product(normed_first, key_weight) + key_bias)
    value_pre = low_back(product(normed_first, value_weight) + value_bias)
    queries = low(rotate(query_pre.reshape(count, HEADS, HEAD_DIM), cosine, sine))
    keys_all = low(rotate(key_pre.reshape(count, HEADS, HEAD_DIM), cosine, sine))
    values_all = low(value_pre.reshape(count, HEADS, HEAD_DIM))
    attended = low(low_back(attend(queries, keys_all, values_all, segment, positions)))
    attn_out = low_back(product(attended, out_weight))
    resid_mid = group_tokens + attn_out
    normed_second = low(resid_mid * rms_rate(resid_mid) * norm2_gain)
    router_probs = jax.nn.softmax(product(normed_second, router_weight), axis=-1)
    gates = jnp.take_along_axis(router_probs, group_routes, axis=1)
    shared_mid = low(jax.nn.silu(low_back(product(normed_second, shared_gate))) * low_back(product(normed_second, shared_up)))
    shared_out = low_back(product(shared_mid, shared_down))
    switch = jax.nn.sigmoid(product(normed_second, shared_switch[:, None]))
    experts_out = expert_mix(normed_second, group_routes, gates, expert_gate, expert_up, expert_down)
    return resid_mid + switch * shared_out + experts_out

def reference(tokens, routes, seq_lengths, cotangent, norm1_gain, query_weight, query_bias, key_weight, key_bias, value_weight, value_bias, out_weight, norm2_gain, router_weight, shared_switch, shared_gate, shared_up, shared_down, expert_gate, expert_up, expert_down):
    weights = tuple((item.astype(jnp.float32) for item in (norm1_gain, query_weight, query_bias, key_weight, key_bias, value_weight, value_bias, out_weight, norm2_gain, router_weight, shared_switch, shared_gate, shared_up, shared_down, expert_gate, expert_up, expert_down)))
    tokens_wide = tokens.astype(jnp.float32)

    def forward(weight_tuple, token_values):

        def step(carry, stack):
            part_tokens, part_routes, part_lengths = stack
            return (carry, jax.checkpoint(group_forward)(weight_tuple, part_tokens, part_routes, part_lengths))
        unused, outputs = lax.scan(step, jnp.zeros((), jnp.float32), (token_values.reshape(N_EXPERT, GROUP, D), routes.reshape(N_EXPERT, GROUP, TOP), seq_lengths))
        return outputs.reshape(TOKENS, D)
    block_out, pullback = jax.vjp(forward, weights, tokens_wide)
    grads, grad_tokens = pullback(cotangent.astype(jnp.float32))
    return (block_out.astype(jnp.bfloat16), grad_tokens, grads[0], grads[1], grads[2], grads[3], grads[4], grads[5], grads[6], grads[7], grads[8], grads[9], grads[10], grads[11], grads[12], grads[13], grads[14], grads[15], grads[16])
```

```python
import math

import jax
import jax.numpy as jnp
from jax import lax
from jax.sharding import PartitionSpec as P

HEAD_DIM = 128
TOP = 4


EPSILON = 1e-06
THETA = 1000000.0
MASKED = -1e30
PRECISE = lax.Precision.HIGHEST


def rms_rate(values):
    return lax.rsqrt(jnp.mean(values * values, axis=-1, keepdims=True) + EPSILON)


def token_layout(lengths, count):
    ends = jnp.cumsum(lengths)
    places = jnp.arange(count, dtype=jnp.int32)
    passed = (places[:, None] >= ends[None, :]).astype(jnp.int32)
    segment = jnp.sum(passed, axis=1)
    start = jnp.sum(passed * lengths[None, :], axis=1)
    return (segment, places - start)


def rotary_tables(positions, width):
    half_width = width // 2
    inverse = THETA ** (-2.0 * jnp.arange(half_width, dtype=jnp.float32) / width)
    angle = positions.astype(jnp.float32)[:, None] * inverse[None, :]
    return (jnp.cos(angle)[:, None, :], jnp.sin(angle)[:, None, :])


def rotate(values, cosine, sine):
    half_width = values.shape[-1] // 2
    first_half = values[..., :half_width]
    second_half = values[..., half_width:]
    return jnp.concatenate(
        [first_half * cosine - second_half * sine, second_half * cosine + first_half * sine],
        axis=-1,
    )


def rotate_back(grads, cosine, sine):
    half_width = grads.shape[-1] // 2
    first_half = grads[..., :half_width]
    second_half = grads[..., half_width:]
    return jnp.concatenate(
        [first_half * cosine + second_half * sine, second_half * cosine - first_half * sine],
        axis=-1,
    )


def matmul(left_matrix, right_matrix):
    return jnp.dot(left_matrix, right_matrix, preferred_element_type=jnp.float32)


def matmul_tn(left_matrix, right_matrix):
    return lax.dot_general(
        left_matrix, right_matrix, (((0,), (0,)), ((), ())), preferred_element_type=jnp.float32
    )


def matmul_nt(left_matrix, right_matrix):
    return lax.dot_general(
        left_matrix, right_matrix, (((1,), (1,)), ((), ())), preferred_element_type=jnp.float32
    )


def silu_parts(pre_values):
    sigma_values = jax.nn.sigmoid(pre_values)
    return (pre_values * sigma_values, sigma_values * (1.0 + pre_values * (1.0 - sigma_values)))


def norm_back(upstream, dh_values, values, rate, gain):
    gained = dh_values * gain
    return (
        upstream
        + rate * gained
        - values * rate**3 * jnp.mean(gained * values, axis=-1, keepdims=True)
    )


def shards(
    tokens,
    routes,
    seq_lengths,
    cotangent,
    norm1_gain,
    query_weight,
    query_bias,
    key_weight,
    key_bias,
    value_weight,
    value_bias,
    out_weight,
    norm2_gain,
    router_weight,
    shared_switch,
    shared_gate,
    shared_up,
    shared_down,
    expert_gate,
    expert_up,
    expert_down,
):
    own_count = tokens.shape[0]
    width = tokens.shape[1]
    members = lax.axis_size("fsdp")
    columns = lax.axis_size("expert")
    member = lax.axis_index("fsdp")
    own_start = member * own_count
    count = own_count * members
    experts_count = router_weight.shape[1]
    local_experts = experts_count // members
    capacity = 4 * own_count * TOP // (3 * experts_count)

    def own_rows(values):
        return lax.dynamic_slice_in_dim(values, own_start, own_count, 0)

    def over_members(pieces):
        return lax.all_to_all(pieces, "fsdp", split_axis=0, concat_axis=0, tiled=True)

    def over_columns(pieces):
        return lax.all_to_all(pieces, "expert", split_axis=0, concat_axis=0, tiled=True)

    def weights_in(chunk):
        rows, cols = chunk.shape
        mixed = over_columns(chunk.reshape(columns, rows // columns, cols))
        crossed = over_members(mixed.reshape(members, local_experts, rows // columns, cols))
        return lax.all_gather(crossed, "expert", axis=0, tiled=False)

    def grads_out(parts):
        merged = parts.reshape((columns * members,) + parts.shape[2:])
        summed_part = lax.psum_scatter(merged, "expert", scatter_dimension=0, tiled=True)
        crossed = over_members(summed_part)
        rows, cols = crossed.shape[2:]
        mixed = over_columns(crossed.reshape(experts_count, rows, cols))
        return mixed.reshape(1, columns * rows, cols).astype(jnp.float32)

    def rows_full(gathered):
        return gathered.transpose(2, 1, 0, 3, 4).reshape(local_experts, width, -1)

    def cols_full(gathered):
        return gathered.transpose(2, 0, 3, 1, 4).reshape(local_experts, -1, width)

    group_tokens = lax.all_gather(tokens, "fsdp", axis=0, tiled=True)
    group_routes = lax.all_gather(routes, "fsdp", axis=0, tiled=True)
    column = lax.axis_index("expert")
    out_piece_rows = out_weight.shape[0] // columns
    out_piece = lax.dynamic_slice_in_dim(out_weight, column * out_piece_rows, out_piece_rows, 0)
    out_full = lax.all_gather(out_piece, ("fsdp", "expert"), axis=0, tiled=True)
    gate_mats = rows_full(weights_in(expert_gate[0]))
    up_mats = rows_full(weights_in(expert_up[0]))
    down_mats = cols_full(weights_in(expert_down[0]))
    group_cot = lax.all_gather(cotangent, "fsdp", axis=0, tiled=True)

    local_heads = query_weight.shape[1] // HEAD_DIM
    segment, positions = token_layout(seq_lengths[0], count)
    cosine, sine = rotary_tables(positions, HEAD_DIM)
    tokens_wide = group_tokens.astype(jnp.float32)
    tokens_own_wide = tokens.astype(jnp.float32)
    rate_first = rms_rate(tokens_wide)
    gain_first = norm1_gain.astype(jnp.float32)
    normed_first = (tokens_wide * rate_first * gain_first).astype(jnp.bfloat16)
    query_pre = matmul(normed_first, query_weight) + query_bias.astype(jnp.float32)
    key_pre = matmul(normed_first, key_weight) + key_bias.astype(jnp.float32)
    value_pre = matmul(normed_first, value_weight) + value_bias.astype(jnp.float32)
    queries = rotate(query_pre.reshape(count, local_heads, HEAD_DIM), cosine, sine).astype(
        jnp.bfloat16
    )
    keys_all = rotate(key_pre.reshape(count, local_heads, HEAD_DIM), cosine, sine).astype(
        jnp.bfloat16
    )
    values_all = value_pre.reshape(count, local_heads, HEAD_DIM).astype(jnp.bfloat16)
    block_rows = math.gcd(count, 512)
    block_count = count // block_rows
    factor = 1.0 / math.sqrt(HEAD_DIM)

    def block_scores(start):
        query_rows = lax.dynamic_slice_in_dim(queries, start, block_rows, 0)
        segment_rows = lax.dynamic_slice_in_dim(segment, start, block_rows, 0)
        position_rows = lax.dynamic_slice_in_dim(positions, start, block_rows, 0)
        allowed = (segment_rows[:, None] == segment[None, :]) & (
            position_rows[:, None] >= positions[None, :]
        )
        scores = (
            jnp.einsum("qhd,khd->hqk", query_rows, keys_all, preferred_element_type=jnp.float32)
            * factor
        )
        return (query_rows, jnp.where(allowed[None], scores, MASKED))

    def forward_block(block_index):
        query_rows, scores = block_scores(block_index * block_rows)
        peak = jnp.max(scores, axis=-1, keepdims=True)
        raised = jnp.exp(scores - peak)
        total_mass = jnp.sum(raised, axis=-1, keepdims=True)
        soft_low = (raised / total_mass).astype(jnp.bfloat16)
        context = jnp.einsum(
            "hqk,khd->qhd", soft_low, values_all, preferred_element_type=jnp.float32
        )
        return (context, (peak + jnp.log(total_mass))[..., 0])

    contexts, log_mass = lax.map(forward_block, jnp.arange(block_count, dtype=jnp.int32))
    attended = contexts.reshape(count, local_heads * HEAD_DIM).astype(jnp.bfloat16)
    attended_full = lax.all_gather(attended, "fsdp", axis=1, tiled=True)
    resid_mid = tokens_wide + matmul(attended_full, out_full)
    gain_second = norm2_gain.astype(jnp.float32)
    rate_second = rms_rate(resid_mid)
    normed_second = (resid_mid * rate_second * gain_second).astype(jnp.bfloat16)
    resid_own = own_rows(resid_mid)
    rate_own = own_rows(rate_second)

    small_weight = jnp.concatenate([router_weight, shared_switch[:, None]], axis=1)
    small_pre = matmul(normed_second, small_weight)
    router_probs = jax.nn.softmax(small_pre[:, :experts_count], axis=-1)
    switch_all = jax.nn.sigmoid(small_pre[:, experts_count:])
    own_ids = member * local_experts + jnp.arange(local_experts, dtype=jnp.int32)
    gates = lax.dynamic_slice_in_dim(router_probs, member * local_experts, local_experts, 1)
    hot = jnp.sum(
        (group_routes[:, :, None] == own_ids[None, None, :]).astype(jnp.float32), axis=1
    ).reshape(members, own_count, local_experts)
    places = jnp.arange(own_count, dtype=jnp.int32)
    before = (places[:, None] > places[None, :]).astype(jnp.bfloat16)
    ranks = jnp.einsum(
        "ut,btj->bju", before, hot.astype(jnp.bfloat16), preferred_element_type=jnp.float32
    ).astype(jnp.int32)
    slots = jnp.arange(capacity, dtype=jnp.int32)
    picks = (ranks[:, :, None, :] == slots[None, None, :, None]) & (
        hot.transpose(0, 2, 1)[:, :, None, :] > 0.0
    )
    picks_low = picks.astype(jnp.bfloat16)
    gates_by_block = gates.reshape(members, own_count, local_experts).transpose(0, 2, 1)
    slot_gates = jnp.sum(jnp.where(picks, gates_by_block[:, :, None, :], 0.0), axis=-1)

    def dispatch(values, which):
        return (
            jnp.einsum(
                "bst,btd->bsd",
                picks_low[:, which],
                values.reshape(members, own_count, width),
                preferred_element_type=jnp.float32,
            )
            .astype(jnp.bfloat16)
            .reshape(members * capacity, width)
        )

    def collect(values, which):
        return jnp.einsum(
            "bst,bsd->btd",
            picks_low[:, which],
            values.reshape(members, capacity, width),
            preferred_element_type=jnp.float32,
        ).reshape(count, width)

    shared_gate_pre = matmul(normed_second, shared_gate)
    shared_up_pre = matmul(normed_second, shared_up)
    shared_silu, shared_slope = silu_parts(shared_gate_pre)
    shared_mid = (shared_silu * shared_up_pre).astype(jnp.bfloat16)
    shared_out = matmul(shared_mid, shared_down)
    grad_wide = group_cot.astype(jnp.float32)
    block_part = switch_all * shared_out
    switch_logit = (
        jnp.sum(grad_wide * shared_out, axis=-1, keepdims=True) * switch_all * (1.0 - switch_all)
    )

    d_shared_out = (switch_all * grad_wide).astype(jnp.bfloat16)
    d_shared_mid = matmul_nt(d_shared_out, shared_down)
    d_shared_gate = (d_shared_mid * shared_up_pre * shared_slope).astype(jnp.bfloat16)
    d_shared_up = (d_shared_mid * shared_silu).astype(jnp.bfloat16)
    dh_partial = matmul_nt(d_shared_gate, shared_gate) + matmul_nt(d_shared_up, shared_up)

    expert_parts = []
    d_gate_columns = []
    for which in range(local_experts):
        gate_mat, up_mat, down_mat = gate_mats[which], up_mats[which], down_mats[which]
        rows = dispatch(normed_second, which)
        expert_gate_pre = matmul(rows, gate_mat)
        expert_up_pre = matmul(rows, up_mat)
        expert_silu, expert_slope = silu_parts(expert_gate_pre)
        expert_mid = (expert_silu * expert_up_pre).astype(jnp.bfloat16)
        result = matmul(expert_mid, down_mat).astype(jnp.bfloat16)
        row_gates = slot_gates[:, which].reshape(members * capacity, 1)
        result_wide = result.astype(jnp.float32)
        block_part = block_part + collect((row_gates * result_wide).astype(jnp.bfloat16), which)
        grad_rows = dispatch(group_cot, which).astype(jnp.float32)
        d_slot_gates = jnp.sum(grad_rows * result_wide, axis=-1).reshape(members, capacity)
        d_gate_columns.append(
            jnp.sum(jnp.where(picks[:, which], d_slot_gates[:, :, None], 0.0), axis=1).reshape(count)
        )
        d_rows = (row_gates * grad_rows).astype(jnp.bfloat16)
        d_expert_mid = matmul_nt(d_rows, down_mat)
        d_expert_gate = (d_expert_mid * expert_up_pre * expert_slope).astype(jnp.bfloat16)
        d_expert_up = (d_expert_mid * expert_silu).astype(jnp.bfloat16)
        d_in = (matmul_nt(d_expert_gate, gate_mat) + matmul_nt(d_expert_up, up_mat)).astype(
            jnp.bfloat16
        )
        dh_partial = dh_partial + collect(d_in, which)
        expert_parts.append((rows, d_expert_gate, d_expert_up, expert_mid, d_rows))

    d_gates = jnp.stack(d_gate_columns, axis=1)
    d_choice = lax.dynamic_update_slice_in_dim(
        jnp.zeros_like(router_probs), d_gates, member * local_experts, 1
    )
    d_logits = router_probs * (d_choice - jnp.sum(gates * d_gates, axis=-1, keepdims=True))
    d_small = jnp.concatenate([d_logits, switch_logit], axis=1)
    d_small_high = d_small.astype(jnp.bfloat16)
    d_small_low = (d_small - d_small_high.astype(jnp.float32)).astype(jnp.bfloat16)
    d_small_both = jnp.concatenate([d_small_high, d_small_low], axis=1)
    small_both = jnp.concatenate([small_weight, small_weight], axis=1)
    dh_partial = dh_partial + matmul_nt(d_small_both, small_both)
    small_part = matmul_tn(normed_second, d_small_both)
    small_part = small_part[:, : experts_count + 1] + small_part[:, experts_count + 1 :]

    block_own = lax.psum_scatter(
        block_part.astype(jnp.bfloat16), "fsdp", scatter_dimension=0, tiled=True
    ).astype(jnp.float32)
    block_out = (resid_own + block_own).astype(jnp.bfloat16)
    dh_second_own = lax.psum_scatter(
        dh_partial.astype(jnp.bfloat16), "fsdp", scatter_dimension=0, tiled=True
    ).astype(jnp.float32)

    def pieces_rows(grads):
        return (
            jnp.stack(grads)
            .astype(jnp.bfloat16)
            .reshape(local_experts, members, columns, -1, grads[0].shape[1])
            .transpose(2, 1, 0, 3, 4)
        )

    def pieces_cols(grads):
        return (
            jnp.stack(grads)
            .astype(jnp.bfloat16)
            .reshape(local_experts, columns, -1, members, width // members)
            .transpose(1, 3, 0, 2, 4)
        )

    expert_gate_grad = grads_out(pieces_rows([matmul_tn(p[0], p[1]) for p in expert_parts]))
    expert_up_grad = grads_out(pieces_rows([matmul_tn(p[0], p[2]) for p in expert_parts]))
    expert_down_grad = grads_out(pieces_cols([matmul_tn(p[3], p[4]) for p in expert_parts]))
    shared_down_grad = matmul_tn(shared_mid, d_shared_out)
    shared_gate_grad = matmul_tn(normed_second, d_shared_gate)
    shared_up_grad = matmul_tn(normed_second, d_shared_up)

    grad_own = cotangent.astype(jnp.float32)
    d_resid_own = norm_back(grad_own, dh_second_own, resid_own, rate_own, gain_second)
    d_attn_own = d_resid_own.astype(jnp.bfloat16)
    norm2_part = jnp.sum(dh_second_own * resid_own * rate_own, axis=0)
    d_attended_own = matmul_nt(d_attn_own, out_full).astype(jnp.bfloat16)
    d_context = over_members(
        d_attended_own.reshape(own_count, members, -1).transpose(1, 0, 2)
    ).reshape(count, local_heads, HEAD_DIM)
    d_attn_out = lax.all_gather(d_attn_own, "fsdp", axis=0, tiled=True)
    out_grad = matmul_tn(attended, d_attn_out)

    def backward_block(carry, block_index):
        key_acc, value_acc = carry
        start = block_index * block_rows
        query_rows, scores = block_scores(start)
        grad_rows = lax.dynamic_slice_in_dim(d_context, start, block_rows, 0)
        soft_weights = jnp.exp(scores - log_mass[block_index][..., None])
        d_soft = jnp.einsum(
            "qhd,khd->hqk", grad_rows, values_all, preferred_element_type=jnp.float32
        )
        inner = jnp.sum(soft_weights * d_soft, axis=-1, keepdims=True)
        d_scores = (soft_weights * (d_soft - inner)).astype(jnp.bfloat16)
        d_query = (
            jnp.einsum("hqk,khd->qhd", d_scores, keys_all, preferred_element_type=jnp.float32)
            * factor
        )
        key_acc = (
            key_acc
            + jnp.einsum("hqk,qhd->khd", d_scores, query_rows, preferred_element_type=jnp.float32)
            * factor
        )
        value_acc = value_acc + jnp.einsum(
            "hqk,qhd->khd",
            soft_weights.astype(jnp.bfloat16),
            grad_rows,
            preferred_element_type=jnp.float32,
        )
        return ((key_acc, value_acc), d_query)

    zero_heads = jnp.zeros((count, local_heads, HEAD_DIM), jnp.float32)
    (key_grad, value_grad), query_blocks = lax.scan(
        backward_block, (zero_heads, zero_heads), jnp.arange(block_count, dtype=jnp.int32)
    )
    query_grad = query_blocks.reshape(count, local_heads, HEAD_DIM)
    d_query_pre = (
        rotate_back(query_grad, cosine, sine)
        .astype(jnp.bfloat16)
        .reshape(count, local_heads * HEAD_DIM)
    )
    d_key_pre = (
        rotate_back(key_grad, cosine, sine)
        .astype(jnp.bfloat16)
        .reshape(count, local_heads * HEAD_DIM)
    )
    d_value_pre = value_grad.astype(jnp.bfloat16).reshape(count, local_heads * HEAD_DIM)
    dh_first_part = (
        matmul_nt(d_query_pre, query_weight)
        + matmul_nt(d_key_pre, key_weight)
        + matmul_nt(d_value_pre, value_weight)
    )
    norm1_part = jnp.sum(dh_first_part * (tokens_wide * rate_first), axis=0)
    dh_first_own = lax.psum_scatter(
        dh_first_part.astype(jnp.bfloat16), "fsdp", scatter_dimension=0, tiled=True
    ).astype(jnp.float32)
    grad_tokens = norm_back(
        d_resid_own, dh_first_own, tokens_own_wide, own_rows(rate_first), gain_first
    )

    biases = jnp.concatenate(
        [
            jnp.sum(d_pre.astype(jnp.float32), axis=0)
            for d_pre in (d_query_pre, d_key_pre, d_value_pre)
        ]
    )
    all_biases = lax.dynamic_update_slice_in_dim(
        jnp.zeros((members, biases.shape[0]), jnp.float32), biases[None], member, 0
    )
    stats = lax.psum(
        jnp.concatenate(
            [norm1_part, norm2_part, small_part.T.reshape(-1), all_biases.reshape(-1)]
        ),
        ("expert", "fsdp"),
    )
    small_sum = stats[2 * width : (3 + experts_count) * width].reshape(-1, width)
    bias_sums = lax.dynamic_index_in_dim(
        stats[(3 + experts_count) * width :].reshape(members, 3, -1), member, 0, keepdims=False
    )

    def over_groups(grad):
        return lax.psum(grad.astype(jnp.bfloat16), "expert").astype(jnp.float32)

    return (
        block_out,
        grad_tokens,
        stats[:width],
        over_groups(matmul_tn(normed_first, d_query_pre)),
        bias_sums[0],
        over_groups(matmul_tn(normed_first, d_key_pre)),
        bias_sums[1],
        over_groups(matmul_tn(normed_first, d_value_pre)),
        bias_sums[2],
        over_groups(out_grad),
        stats[width : 2 * width],
        small_sum[:experts_count].T,
        small_sum[experts_count],
        over_groups(shared_gate_grad),
        over_groups(shared_up_grad),
        over_groups(shared_down_grad),
        expert_gate_grad,
        expert_up_grad,
        expert_down_grad,
    )


def solution(mesh):
    placed = (
        P(("expert", "fsdp"), None),
        P(("expert", "fsdp"), None),
        P("expert", None),
        P(("expert", "fsdp"), None),
        P(),
        P(None, "fsdp"),
        P("fsdp"),
        P(None, "fsdp"),
        P("fsdp"),
        P(None, "fsdp"),
        P("fsdp"),
        P("fsdp", None),
        P(),
        P(),
        P(),
        P(None, "fsdp"),
        P(None, "fsdp"),
        P("fsdp", None),
        P("expert", "fsdp", None),
        P("expert", "fsdp", None),
        P("expert", None, "fsdp"),
    )
    return jax.shard_map(
        shards,
        mesh=mesh,
        in_specs=placed,
        out_specs=(
            P(("expert", "fsdp"), None),
            P(("expert", "fsdp"), None),
            P(),
            P(None, "fsdp"),
            P("fsdp"),
            P(None, "fsdp"),
            P("fsdp"),
            P(None, "fsdp"),
            P("fsdp"),
            P("fsdp", None),
            P(),
            P(),
            P(),
            P(None, "fsdp"),
            P(None, "fsdp"),
            P("fsdp", None),
            P("expert", "fsdp", None),
            P("expert", "fsdp", None),
            P("expert", None, "fsdp"),
        ),
        check_vma=False,
    )
```

```python
import functools
import math

import jax
import jax.numpy as jnp
from jax import lax
from jax.experimental import pallas as pl
from jax.experimental.pallas import tpu as pltpu
from jax.sharding import PartitionSpec as P

HEAD_DIM = 128
TOP = 4


EPSILON = 1e-06
THETA = 1000000.0
MASKED = -1e30
KERNEL_VMEM = 40 * 1024 * 1024
BIG_VMEM = 58 * 1024 * 1024
NO_COST = pl.CostEstimate(flops=0, bytes_accessed=0, transcendentals=0)


def rms_rate(values):
    return lax.rsqrt(jnp.mean(values * values, axis=-1, keepdims=True) + EPSILON)


def token_layout(lengths, count):
    ends = jnp.cumsum(lengths)
    places = jnp.arange(count, dtype=jnp.int32)
    passed = (places[:, None] >= ends[None, :]).astype(jnp.int32)
    segment = jnp.sum(passed, axis=1)
    start = jnp.sum(passed * lengths[None, :], axis=1)
    return (segment, places - start)


def rotary_tables(positions, width):
    half_width = width // 2
    inverse = THETA ** (-2.0 * jnp.arange(half_width, dtype=jnp.float32) / width)
    angle = positions.astype(jnp.float32)[:, None] * inverse[None, :]
    cosine, sine = jnp.cos(angle), jnp.sin(angle)
    return (
        jnp.concatenate([cosine, cosine], axis=1),
        jnp.concatenate([-sine, sine], axis=1),
    )


def matmul(left_matrix, right_matrix):
    return jnp.dot(left_matrix, right_matrix, preferred_element_type=jnp.float32)


def matmul_tn(left_matrix, right_matrix):
    return lax.dot_general(
        left_matrix, right_matrix, (((0,), (0,)), ((), ())), preferred_element_type=jnp.float32
    )


def matmul_nt(left_matrix, right_matrix):
    return lax.dot_general(
        left_matrix, right_matrix, (((1,), (1,)), ((), ())), preferred_element_type=jnp.float32
    )


def silu_parts(pre_values):
    sigma_values = jax.nn.sigmoid(pre_values)
    return (pre_values * sigma_values, sigma_values * (1.0 + pre_values * (1.0 - sigma_values)))


def norm_back(upstream, dh_values, values, rate, gain):
    gained = dh_values * gain
    return (
        upstream
        + rate * gained
        - values * rate**3 * jnp.mean(gained * values, axis=-1, keepdims=True)
    )


def lane_turn(values):
    return pltpu.roll(values, HEAD_DIM // 2, 1)


def project_body(tokens_ref, gain_ref, weight_refs, bias_refs, cos_ref, sin_ref, outs):
    normed_ref, rate_ref, query_ref, key_ref, value_ref = outs
    wide = tokens_ref[...].astype(jnp.float32)
    rate = rms_rate(wide)
    normed = (wide * rate * gain_ref[...]).astype(jnp.bfloat16)
    normed_ref[...] = normed
    rate_ref[...] = rate
    cosine, sine = cos_ref[...], sin_ref[...]
    for place, out_ref in enumerate((query_ref, key_ref, value_ref)):
        pre = (
            jnp.dot(normed, weight_refs[place][...], preferred_element_type=jnp.float32)
            + bias_refs[place][...]
        )
        if place == 2:
            out_ref[...] = pre.astype(jnp.bfloat16)
            continue
        for head in range(pre.shape[1] // HEAD_DIM):
            part = pre[:, head * HEAD_DIM : (head + 1) * HEAD_DIM]
            turned = part * cosine + lane_turn(part) * sine
            out_ref[:, head * HEAD_DIM : (head + 1) * HEAD_DIM] = turned.astype(jnp.bfloat16)


def project(tokens, gain, weights, biases, cosine, sine, rows):
    count, width = tokens.shape
    features = weights[0].shape[1]

    def body(t, g, w0, w1, w2, b0, b1, b2, c, s, *outs):
        project_body(t, g, (w0, w1, w2), (b0, b1, b2), c, s, outs)

    def by_rows(cols):
        return pl.BlockSpec((rows, cols), lambda i: (i, 0))

    def whole(*shape):
        return pl.BlockSpec(shape, lambda i: (0, 0))

    return pl.pallas_call(
        body,
        grid=(count // rows,),
        in_specs=[by_rows(width), whole(1, width)]
        + [whole(width, features)] * 3
        + [whole(1, features)] * 3
        + [by_rows(HEAD_DIM)] * 2,
        out_specs=[by_rows(width), by_rows(1)] + [by_rows(features)] * 3,
        out_shape=[
            jax.ShapeDtypeStruct((count, width), jnp.bfloat16),
            jax.ShapeDtypeStruct((count, 1), jnp.float32),
        ]
        + [jax.ShapeDtypeStruct((count, features), jnp.bfloat16)] * 3,
        compiler_params=pltpu.CompilerParams(vmem_limit_bytes=KERNEL_VMEM),
        cost_estimate=pl.CostEstimate(
            flops=6 * count * width * features,
            bytes_accessed=4 * count * width + 6 * (count + width) * features,
            transcendentals=0,
        ),
        name="project",
    )(tokens, gain, *weights, *biases, cosine, sine)


def scores_of(lows_ref, starts_ref, query, key_ref, wide, block):
    index = pl.program_id(1)
    low = lows_ref[index]
    rows = pl.ds(pl.multiple_of(low * block, block), wide * block)
    keys = key_ref[rows, :]
    scores = lax.dot_general(
        keys, query, (((1,), (1,)), ((), ())), preferred_element_type=jnp.float32
    ) * (1.0 / math.sqrt(HEAD_DIM))
    key_place = low * block + lax.broadcasted_iota(jnp.int32, scores.shape, 0)
    query_place = index * block + lax.broadcasted_iota(jnp.int32, scores.shape, 1)
    allowed = (key_place <= query_place) & (key_place >= starts_ref[...])
    return rows, keys, jnp.where(allowed, scores, MASKED)


def attend_body(lows_ref, starts_ref, query_ref, key_ref, value_ref, out_ref, mass_ref):
    block = query_ref.shape[0]
    index = pl.program_id(1)

    def run(wide):
        rows, _, scores = scores_of(lows_ref, starts_ref, query_ref[...], key_ref, wide, block)
        peak = jnp.max(scores, axis=0, keepdims=True)
        raised = jnp.exp(scores - peak)
        total = jnp.sum(raised, axis=0, keepdims=True)
        soft = (raised * (1.0 / total)).astype(jnp.bfloat16)
        mixed = lax.dot_general(
            value_ref[rows, :], soft, (((0,), (0,)), ((), ())), preferred_element_type=jnp.float32
        )
        out_ref[...] = mixed.T.astype(jnp.bfloat16)
        mass_ref[0] = peak + jnp.log(total)

    for wide in range(1, key_ref.shape[0] // block + 1):
        pl.when(index - lows_ref[index] + 1 == wide)(functools.partial(run, wide))


def attend(lows, starts, queries, keys, values, block):
    count, features = queries.shape
    heads = features // HEAD_DIM
    by_block = pl.BlockSpec((block, HEAD_DIM), lambda h, i, *_: (i, h))
    by_head = pl.BlockSpec((count, HEAD_DIM), lambda h, i, *_: (0, h))
    return pl.pallas_call(
        attend_body,
        grid_spec=pltpu.PrefetchScalarGridSpec(
            num_scalar_prefetch=1,
            grid=(heads, count // block),
            in_specs=[
                pl.BlockSpec((1, block), lambda h, i, *_: (0, i)),
                by_block,
                by_head,
                by_head,
            ],
            out_specs=[by_block, pl.BlockSpec((1, 1, block), lambda h, i, *_: (h, 0, i))],
        ),
        out_shape=[
            jax.ShapeDtypeStruct((count, features), jnp.bfloat16),
            jax.ShapeDtypeStruct((heads, 1, count), jnp.float32),
        ],
        compiler_params=pltpu.CompilerParams(vmem_limit_bytes=KERNEL_VMEM),
        cost_estimate=pl.CostEstimate(
            flops=2 * count * count * features,
            bytes_accessed=8 * count * features,
            transcendentals=count * count * heads // 2,
        ),
        name="attend",
    )(lows, starts, queries, keys, values)


def attend_back_body(
    lows_ref, starts_ref, query_ref, key_ref, value_ref, grad_ref, mass_ref, *rest
):
    cos_ref, sin_ref, d_query_ref, d_key_ref, d_value_ref, key_sum, value_sum = rest
    block = query_ref.shape[0]
    index = pl.program_id(1)
    blocks = key_ref.shape[0] // block
    factor = 1.0 / math.sqrt(HEAD_DIM)

    def rope_back(values, rows):
        return (
            values * cos_ref[rows, :] + lane_turn(values) * -sin_ref[rows, :]
        ).astype(jnp.bfloat16)

    @pl.when(index == 0)
    def _():
        key_sum[...] = jnp.zeros_like(key_sum)
        value_sum[...] = jnp.zeros_like(value_sum)

    def run(wide):
        query, grad = query_ref[...], grad_ref[...]
        rows, keys, scores = scores_of(lows_ref, starts_ref, query, key_ref, wide, block)
        soft = jnp.exp(scores - mass_ref[0])
        d_soft = lax.dot_general(
            value_ref[rows, :], grad, (((1,), (1,)), ((), ())), preferred_element_type=jnp.float32
        )
        inner = jnp.sum(soft * d_soft, axis=0, keepdims=True)
        d_scores = (soft * (d_soft - inner)).astype(jnp.bfloat16)
        value_sum[rows, :] += jnp.dot(
            soft.astype(jnp.bfloat16), grad, preferred_element_type=jnp.float32
        )
        key_sum[rows, :] += jnp.dot(d_scores, query, preferred_element_type=jnp.float32) * factor
        d_query = lax.dot_general(
            keys, d_scores, (((0,), (0,)), ((), ())), preferred_element_type=jnp.float32
        ).T * factor
        here = pl.ds(pl.multiple_of(index * block, block), block)
        d_query_ref[...] = rope_back(d_query, here)

    for wide in range(1, blocks + 1):
        pl.when(index - lows_ref[index] + 1 == wide)(functools.partial(run, wide))

    @pl.when(index == blocks - 1)
    def _():
        d_key_ref[...] = rope_back(key_sum[...], slice(None))
        d_value_ref[...] = value_sum[...].astype(jnp.bfloat16)


def attend_back(lows, starts, queries, keys, values, grads, mass, cosine, sine, block):
    count, features = queries.shape
    heads = features // HEAD_DIM
    by_block = pl.BlockSpec((block, HEAD_DIM), lambda h, i, *_: (i, h))
    by_head = pl.BlockSpec((count, HEAD_DIM), lambda h, i, *_: (0, h))
    whole = pl.BlockSpec((count, HEAD_DIM), lambda h, i, *_: (0, 0))
    return pl.pallas_call(
        attend_back_body,
        grid_spec=pltpu.PrefetchScalarGridSpec(
            num_scalar_prefetch=1,
            grid=(heads, count // block),
            in_specs=[
                pl.BlockSpec((1, block), lambda h, i, *_: (0, i)),
                by_block,
                by_head,
                by_head,
                by_block,
                pl.BlockSpec((1, 1, block), lambda h, i, *_: (h, 0, i)),
                whole,
                whole,
            ],
            out_specs=[by_block, by_head, by_head],
            scratch_shapes=[pltpu.VMEM((count, HEAD_DIM), jnp.float32)] * 2,
        ),
        out_shape=[jax.ShapeDtypeStruct((count, features), jnp.bfloat16)] * 3,
        compiler_params=pltpu.CompilerParams(vmem_limit_bytes=KERNEL_VMEM),
        cost_estimate=NO_COST,
        name="attend_back",
    )(lows, starts, queries, keys, values, grads, mass, cosine, sine)


def settle_body(tokens_ref, attended_ref, weight_ref, gain_ref, small_ref, *outs):
    resid_ref, rate_ref, normed_ref, logit_ref = outs
    total = tokens_ref[...].astype(jnp.float32)
    members, _, features = attended_ref.shape
    for member in range(members):
        total = total + jnp.dot(
            attended_ref[member],
            weight_ref[member * features : (member + 1) * features, :],
            preferred_element_type=jnp.float32,
        )
    rate = rms_rate(total)
    normed = (total * rate * gain_ref[...]).astype(jnp.bfloat16)
    resid_ref[...] = total
    rate_ref[...] = rate
    normed_ref[...] = normed
    logit_ref[...] = jnp.dot(normed, small_ref[...], preferred_element_type=jnp.float32)


def settle(tokens, attended, weight, gain, small, rows):
    count, width = tokens.shape
    members, _, features = attended.shape

    def by_rows(cols):
        return pl.BlockSpec((rows, cols), lambda i: (i, 0))

    def whole(*shape):
        return pl.BlockSpec(shape, lambda i: (0,) * len(shape))

    return pl.pallas_call(
        settle_body,
        grid=(count // rows,),
        in_specs=[
            by_rows(width),
            pl.BlockSpec((members, rows, features), lambda i: (0, i, 0)),
            whole(width, width),
            whole(1, width),
            whole(*small.shape),
        ],
        out_specs=[by_rows(width), by_rows(1), by_rows(width), by_rows(small.shape[1])],
        out_shape=[
            jax.ShapeDtypeStruct((count, width), jnp.float32),
            jax.ShapeDtypeStruct((count, 1), jnp.float32),
            jax.ShapeDtypeStruct((count, width), jnp.bfloat16),
            jax.ShapeDtypeStruct((count, small.shape[1]), jnp.float32),
        ],
        compiler_params=pltpu.CompilerParams(vmem_limit_bytes=KERNEL_VMEM),
        cost_estimate=pl.CostEstimate(
            flops=2 * count * width * width, bytes_accessed=12 * count * width, transcendentals=0
        ),
        name="settle",
    )(tokens, attended, weight, gain, small)


def mixed_places(members, rows):
    for z in range(members):
        for q in range(members):
            yield (z * members + q) * rows, (q * members + z) * rows


def dispatch_body(members, places_ref, source_ref, target_ref):
    slots = target_ref.shape[2]
    quarter = source_ref.shape[1] // members // members
    for which in range(target_ref.shape[0]):
        place = places_ref[0, which : which + 1, :]
        picks = lax.broadcasted_iota(jnp.int32, (slots, place.shape[1]), 0) == place
        picks = picks.astype(jnp.float32).astype(jnp.bfloat16)
        values = jnp.dot(picks, source_ref[...], preferred_element_type=jnp.float32).astype(
            jnp.bfloat16
        )
        for plain, mixed in mixed_places(members, quarter):
            target_ref[which, 0, :, mixed : mixed + quarter] = values[:, plain : plain + quarter]


def dispatch(places, source, slots, members):
    experts, width = places.shape[1], source.shape[1]
    own = source.shape[0] // members
    return pl.pallas_call(
        functools.partial(dispatch_body, members),
        grid=(members,),
        in_specs=[
            pl.BlockSpec((1, experts, own), lambda b: (b, 0, 0)),
            pl.BlockSpec((own, width), lambda b: (b, 0)),
        ],
        out_specs=pl.BlockSpec((experts, 1, slots, width), lambda b: (0, b, 0, 0)),
        out_shape=jax.ShapeDtypeStruct((experts, members, slots, width), jnp.bfloat16),
        compiler_params=pltpu.CompilerParams(vmem_limit_bytes=KERNEL_VMEM),
        cost_estimate=NO_COST,
        name="dispatch",
    )(places, source).reshape(experts, members * slots, width)


def collect_body(members, scaled, places_ref, values_ref, extra_ref, *rest):
    *rest, out_ref = rest
    slots = values_ref.shape[2]
    total = 0.0
    for which in range(values_ref.shape[0]):
        place = places_ref[:, which : which + 1]
        picks = lax.broadcasted_iota(jnp.int32, (place.shape[0], slots), 1) == place
        total = total + jnp.dot(
            picks.astype(jnp.float32).astype(jnp.bfloat16),
            values_ref[which, 0],
            preferred_element_type=jnp.float32,
        )
    extra = extra_ref[...]
    if scaled:
        extra = extra * rest[0][...]
    else:
        extra = extra + jnp.dot(rest[0][...], rest[1][...], preferred_element_type=jnp.float32)
    quarter = extra.shape[1] // members // members
    for plain, mixed in mixed_places(members, quarter):
        out_ref[:, plain : plain + quarter] = (
            extra[:, plain : plain + quarter] + total[:, mixed : mixed + quarter]
        ).astype(out_ref.dtype)


def collect(places, values, extra, members, left, right=None):
    experts, _, slots, width = values.shape
    own = extra.shape[0] // members
    by_block = pl.BlockSpec((own, width), lambda b: (b, 0))
    operands = [places, values, extra]
    in_specs = [
        pl.BlockSpec((own, experts), lambda b: (b, 0)),
        pl.BlockSpec((experts, 1, slots, width), lambda b: (0, b, 0, 0)),
        by_block,
    ]
    operands.append(left)
    in_specs.append(pl.BlockSpec((own, left.shape[1]), lambda b: (b, 0)))
    if right is not None:
        operands.append(right)
        in_specs.append(pl.BlockSpec(right.shape, lambda b: (0, 0)))
    return pl.pallas_call(
        functools.partial(collect_body, members, right is None),
        grid=(members,),
        in_specs=in_specs,
        out_specs=by_block,
        out_shape=jax.ShapeDtypeStruct(extra.shape, jnp.bfloat16),
        compiler_params=pltpu.CompilerParams(vmem_limit_bytes=KERNEL_VMEM),
        cost_estimate=NO_COST,
        name="collect",
    )(*operands)


def expert_specs(experts, count, width, features, rows):
    def by_rows(cols):
        return pl.BlockSpec((1, rows, cols), lambda e, i: (e, i, 0))

    def whole(array):
        return pl.BlockSpec(
            (1,) + array.shape[1:], lambda e, i: (e, 0, 0), pipeline_mode=pl.Buffered(1)
        )

    def out(cols, kind):
        return jax.ShapeDtypeStruct((experts, count, cols), kind)

    return by_rows, whole, out


def expert_body(turned, values_ref, scale_ref, gate_ref, up_ref, down_ref, *outs):
    result_ref, mid_ref, silu_ref, up_slope_ref, *scaled_ref = outs
    values = values_ref[0]
    gate_pre = jnp.dot(values, gate_ref[0], preferred_element_type=jnp.float32)
    up_pre = jnp.dot(values, up_ref[0], preferred_element_type=jnp.float32)
    silu, slope = silu_parts(gate_pre)
    mid = (silu * up_pre).astype(jnp.bfloat16)
    mid_ref[0] = mid
    silu_ref[0] = silu
    up_slope_ref[0] = up_pre * slope
    if turned:
        result = matmul_nt(mid, down_ref[0]).astype(jnp.bfloat16)
        scaled_ref[0][0] = (scale_ref[0] * result.astype(jnp.float32)).astype(jnp.bfloat16)
    else:
        result = matmul(mid, down_ref[0])
    result_ref[0] = result


def expert(values, scales, gate, up, down, turned, rows):
    experts, count, width = values.shape
    features = gate.shape[2]
    by_rows, whole, out = expert_specs(experts, count, width, features, rows)
    low, wide = jnp.bfloat16, jnp.float32
    cols = (width, features, features, features) + (width,) * turned
    kinds = (low if turned else wide, low, wide, wide) + (low,) * turned
    return pl.pallas_call(
        functools.partial(expert_body, turned),
        grid=(experts, count // rows),
        in_specs=[by_rows(width), by_rows(1), whole(gate), whole(up), whole(down)],
        out_specs=[by_rows(c) for c in cols],
        out_shape=[out(c, kind) for c, kind in zip(cols, kinds)],
        compiler_params=pltpu.CompilerParams(vmem_limit_bytes=BIG_VMEM),
        cost_estimate=pl.CostEstimate(
            flops=6 * experts * count * width * features,
            bytes_accessed=6 * experts * (count + width) * features,
            transcendentals=experts * count * features,
        ),
        name="expert",
    )(values, scales, gate, up, down)


def expert_back_body(turned, grad_ref, result_ref, scale_ref, silu_ref, up_slope_ref, *rest):
    gate_ref, up_ref, down_ref, dot_ref, d_out_ref, d_gate_ref, d_up_ref, d_in_ref = rest
    grad = grad_ref[0].astype(jnp.float32)
    dot_ref[0] = jnp.sum(grad * result_ref[0].astype(jnp.float32), axis=1, keepdims=True)
    d_out = (scale_ref[0] * grad).astype(jnp.bfloat16)
    d_out_ref[0] = d_out
    d_mid = (matmul if turned else matmul_nt)(d_out, down_ref[0])
    d_gate = (d_mid * up_slope_ref[0]).astype(jnp.bfloat16)
    d_up = (d_mid * silu_ref[0]).astype(jnp.bfloat16)
    d_gate_ref[0] = d_gate
    d_up_ref[0] = d_up
    d_in_ref[0] = (matmul_nt(d_gate, gate_ref[0]) + matmul_nt(d_up, up_ref[0])).astype(
        d_in_ref.dtype
    )


def expert_back(grads, results, scales, silu, up_slope, gate, up, down, turned, rows):
    experts, count, width = grads.shape
    features = gate.shape[2]
    by_rows, whole, out = expert_specs(experts, count, width, features, rows)
    low = jnp.bfloat16
    return pl.pallas_call(
        functools.partial(expert_back_body, turned),
        grid=(experts, count // rows),
        in_specs=[by_rows(width), by_rows(width), by_rows(1), by_rows(features), by_rows(features)]
        + [whole(gate), whole(up), whole(down)],
        out_specs=[by_rows(c) for c in (1, width, features, features, width)],
        out_shape=[
            out(1, jnp.float32),
            out(width, low),
            out(features, low),
            out(features, low),
            out(width, results.dtype),
        ],
        compiler_params=pltpu.CompilerParams(vmem_limit_bytes=BIG_VMEM),
        cost_estimate=NO_COST,
        name="expert_back",
    )(grads, results, scales, silu, up_slope, gate, up, down)


def weight_grads_body(rows_ref, d_out_ref, d_gate_ref, d_up_ref, mid_ref, out_ref):
    rows = rows_ref[0].T
    out_ref[0, 0, 0] = matmul(rows, d_gate_ref[0]).astype(jnp.bfloat16)
    out_ref[0, 0, 1] = matmul(rows, d_up_ref[0]).astype(jnp.bfloat16)
    out_ref[0, 0, 2] = matmul(d_out_ref[0].T, mid_ref[0]).astype(jnp.bfloat16)


def weight_grads(rows, d_out, d_gate, d_up, mid, members):
    experts, count, width = rows.shape
    features = mid.shape[2]
    cut = width // members
    by_cols = pl.BlockSpec((1, count, cut), lambda e, i: (e, 0, i))
    whole = pl.BlockSpec((1, count, features), lambda e, i: (e, 0, 0))
    return pl.pallas_call(
        weight_grads_body,
        grid=(experts, members),
        in_specs=[by_cols, by_cols, whole, whole, whole],
        out_specs=pl.BlockSpec((1, 1, 3, cut, features), lambda e, i: (e, i, 0, 0, 0)),
        out_shape=jax.ShapeDtypeStruct((experts, members, 3, cut, features), jnp.bfloat16),
        compiler_params=pltpu.CompilerParams(vmem_limit_bytes=KERNEL_VMEM),
        cost_estimate=NO_COST,
        name="weight_grads",
    )(rows, d_out, d_gate, d_up, mid)


MESH = pl.DeviceIdType.MESH


class Line:
    def __init__(self, source, out, send_sems, recv_sems, pieces):
        self.source, self.out = source, out
        self.send_sems, self.recv_sems = send_sems, recv_sems
        self.members, self.rows, self.pieces = out.shape[0], out.shape[1] // pieces, pieces
        self.member = lax.axis_index("fsdp")

    def origin(self, step, way):
        return self.member - step if way == 0 else self.member + step

    def inside(self, place):
        return (place >= 0) & (place < self.members)

    def target(self, way):
        return self.member + 1 if way == 0 else self.member - 1

    def sends(self, step, way):
        return self.inside(self.origin(step - 1, way)) & self.inside(self.target(way))

    def copy(self, origin, step, way, piece, first):
        rows = pl.ds(piece * self.rows, self.rows)
        return pltpu.make_async_remote_copy(
            src_ref=self.source.at[rows] if first else self.out.at[origin, rows],
            dst_ref=self.out.at[origin, rows],
            send_sem=self.send_sems.at[way, step - 1, piece],
            recv_sem=self.recv_sems.at[way, step - 1, piece],
            device_id={"fsdp": self.target(way)},
            device_id_type=MESH,
        )

    def send(self, step, way, piece):
        copy = self.copy(self.origin(step - 1, way), step, way, piece, step == 1)
        pl.when(self.sends(step, way))(copy.start)

    def start(self):
        for piece in range(self.pieces):
            for way in range(2):
                self.send(1, way, piece)

    def hand_on(self, step):
        for piece in range(self.pieces):
            for way in range(2):
                origin = self.origin(step, way)
                came = self.copy(origin, step, way, piece, False)
                pl.when(self.inside(origin))(came.wait_recv)
                if step < self.members - 1:
                    self.send(step + 1, way, piece)

    def finish(self):
        for step in range(1, self.members):
            for piece in range(self.pieces):
                for way in range(2):
                    copy = self.copy(self.origin(step - 1, way), step, way, piece, step == 1)
                    pl.when(self.sends(step, way))(copy.wait_send)


def arrive_body(members, local_experts, pieces, *refs):
    tokens_ref, routes_ref, *refs = refs
    chunk_refs, refs = refs[:3], refs[3:]
    group_ref, routes_out, *refs = refs
    mixed_refs, crossed_refs, refs = refs[:3], refs[3:6], refs[6:]
    line_send, line_recv, routes_send, routes_recv, mix_send, mix_recv, refs = *refs[:6], refs[6:]
    cross_send, cross_recv, own_sems = refs
    columns = members * local_experts
    column, member = lax.axis_index("expert"), lax.axis_index("fsdp")
    plane, j = column // local_experts, column % local_experts
    rows = chunk_refs[0].shape[0] // members

    barrier = pltpu.get_barrier_semaphore()
    for other in range(1, columns):
        pl.semaphore_signal(
            barrier, inc=1, device_id={"expert": (column + other) % columns}, device_id_type=MESH
        )
    for other in range(1, members):
        pl.semaphore_signal(
            barrier, inc=1, device_id={"fsdp": (member + other) % members}, device_id_type=MESH
        )
    pl.semaphore_wait(barrier, columns + members - 2)

    line = Line(tokens_ref, group_ref, line_send, line_recv, pieces)
    line.start()
    own_copies = [
        pltpu.make_async_copy(tokens_ref, group_ref.at[member], own_sems.at[0]),
        pltpu.make_async_copy(routes_ref, routes_out.at[member], own_sems.at[1]),
    ]
    for copy in own_copies:
        copy.start()

    def mix(turn, kind):
        part = (plane + turn) % members
        target = j * members + part
        source = chunk_refs[kind].at[pl.ds(pl.multiple_of(part * rows, rows), rows)]
        remote = pltpu.make_async_remote_copy(
            src_ref=source,
            dst_ref=mixed_refs[kind].at[plane],
            send_sem=mix_send.at[turn, kind],
            recv_sem=mix_recv.at[turn, kind],
            device_id={"expert": target},
            device_id_type=MESH,
        )
        local = pltpu.make_async_copy(
            source, mixed_refs[kind].at[plane], mix_send.at[turn, kind]
        )
        return target == column, remote, local

    turns = [(turn, kind) for turn in range(members) for kind in range(3)]
    for turn, kind in turns:
        here, remote, local = mix(turn, kind)
        pl.when(here)(local.start)
        pl.when(jnp.logical_not(here))(remote.start)

    def route(other):
        return pltpu.make_async_remote_copy(
            src_ref=routes_ref,
            dst_ref=routes_out.at[member],
            send_sem=routes_send.at[other - 1],
            recv_sem=routes_recv.at[other - 1],
            device_id={"fsdp": (member + other) % members},
            device_id_type=MESH,
        )

    for other in range(1, members):
        route(other).start()
    for step in range(1, members - 1):
        line.hand_on(step)
    for turn, kind in turns:
        here, remote, local = mix(turn, kind)
        pl.when(here)(local.wait)
        pl.when(jnp.logical_not(here))(remote.wait)

    def cross(other, kind):
        target = (member + other) % members
        return pltpu.make_async_remote_copy(
            src_ref=mixed_refs[kind].at[target],
            dst_ref=crossed_refs[kind].at[member],
            send_sem=cross_send.at[other - 1, kind],
            recv_sem=cross_recv.at[other - 1, kind],
            device_id={"fsdp": target},
            device_id_type=MESH,
        )

    for kind in range(3):
        own_copies.append(
            pltpu.make_async_copy(
                mixed_refs[kind].at[member], crossed_refs[kind].at[member], own_sems.at[2 + kind]
            )
        )
        own_copies[-1].start()
        for other in range(1, members):
            cross(other, kind).start()
    line.hand_on(members - 1)
    line.finish()
    for other in range(1, members):
        route(other).wait()
        for kind in range(3):
            cross(other, kind).wait()
    for copy in own_copies:
        copy.wait()


def arrive(tokens, routes, chunks, members, local_experts):
    own, width = tokens.shape
    pieces = 3 if own % 48 == 0 else 1
    rows, cols = chunks[0].shape
    piece = jax.ShapeDtypeStruct((members, rows // members, cols), jnp.bfloat16)
    anywhere = pl.BlockSpec(memory_space=pl.ANY)
    sems = pltpu.SemaphoreType.DMA
    out_shape = [
        jax.ShapeDtypeStruct((members, own, width), jnp.bfloat16),
        jax.ShapeDtypeStruct((members,) + routes.shape, jnp.int32),
    ] + [piece] * 6
    group, group_routes, *rest = pl.pallas_call(
        functools.partial(arrive_body, members, local_experts, pieces),
        in_specs=[anywhere] * 5,
        out_specs=[anywhere] * len(out_shape),
        out_shape=out_shape,
        scratch_shapes=[sems((2, members - 1, pieces))] * 2
        + [sems((members - 1,))] * 2
        + [sems((members, 3))] * 2
        + [sems((members - 1, 3))] * 2
        + [sems((5,))],
        compiler_params=pltpu.CompilerParams(collective_id=0, has_side_effects=True),
        name="arrive",
    )(tokens, routes, *chunks)
    return group.reshape(members * own, width), group_routes, rest[3:]


def greet(members):
    member = lax.axis_index("fsdp")
    barrier = pltpu.get_barrier_semaphore()
    for other in range(1, members):
        pl.semaphore_signal(
            barrier, inc=1, device_id={"fsdp": (member + other) % members}, device_id_type=MESH
        )
    pl.semaphore_wait(barrier, members - 1)


def gather_body(pieces, block_ref, out_ref, send_sems, recv_sems, own_sem):
    members = out_ref.shape[0]
    member = lax.axis_index("fsdp")
    greet(members)
    line = Line(block_ref, out_ref, send_sems, recv_sems, pieces)
    line.start()
    own = pltpu.make_async_copy(block_ref, out_ref.at[member], own_sem)
    own.start()
    for step in range(1, members):
        line.hand_on(step)
    line.finish()
    own.wait()


def gather(block, members, pieces, collective_id):
    sems = pltpu.SemaphoreType.DMA
    return pl.pallas_call(
        functools.partial(gather_body, pieces),
        in_specs=[pl.BlockSpec(memory_space=pl.ANY)],
        out_specs=pl.BlockSpec(memory_space=pl.ANY),
        out_shape=jax.ShapeDtypeStruct((members,) + block.shape, block.dtype),
        scratch_shapes=[sems((2, members - 1, pieces))] * 2 + [sems],
        compiler_params=pltpu.CompilerParams(collective_id=collective_id, has_side_effects=True),
        name="gather",
    )(block)


def scatter_body(pieces, parts_ref, out_ref, came, send_sems, recv_sems):
    members, rows = parts_ref.shape[0], parts_ref.shape[1] // pieces
    member = lax.axis_index("fsdp")
    greet(members)

    def copy(way, block, piece, first):
        here = pl.ds(piece * rows, rows)
        source = parts_ref.at[block, here] if first else came.at[way, block, here]
        return pltpu.make_async_remote_copy(
            src_ref=source,
            dst_ref=came.at[way, block, here],
            send_sem=send_sems.at[way, block, piece],
            recv_sem=recv_sems.at[way, block, piece],
            device_id={"fsdp": member + 1 if way == 0 else member - 1},
            device_id_type=MESH,
        )

    def passes(way, block):
        starts = (member == 0) & (block > 0) if way == 0 else (member == members - 1)
        if way == 0:
            return starts, (member > 0) & (block > member), (member > 0) & (block == member)
        starts = starts & (block < members - 1)
        last = member < members - 1
        return starts, last & (block < member), last & (block == member)

    turns = [
        (way, members - 1 - turn if way == 0 else turn, piece)
        for turn in range(members)
        for piece in range(pieces)
        for way in range(2)
    ]
    for way, block, piece in turns:
        starts, hands_on, ends = passes(way, block)
        pl.when(starts)(copy(way, block, piece, True).start)

        @pl.when(hands_on)
        def _():
            copy(way, block, piece, False).wait_recv()
            here = pl.ds(piece * rows, rows)
            came[way, block, here] = (
                came[way, block, here].astype(jnp.float32)
                + parts_ref[block, here].astype(jnp.float32)
            ).astype(came.dtype)
            copy(way, block, piece, False).start()

    for way, block, piece in turns:
        pl.when(passes(way, block)[2])(copy(way, block, piece, False).wait_recv)

    for block in range(members):

        @pl.when(member == block)
        def _():
            total = parts_ref[block].astype(jnp.float32)
            if block > 0:
                total = total + came[0, block].astype(jnp.float32)
            if block < members - 1:
                total = total + came[1, block].astype(jnp.float32)
            out_ref[...] = total

    for way, block, piece in turns:
        starts, hands_on, _ = passes(way, block)
        pl.when(starts)(copy(way, block, piece, True).wait_send)
        pl.when(hands_on)(copy(way, block, piece, False).wait_send)


def scatter(parts, members, collective_id):
    count, width = parts.shape
    own = count // members
    pieces = 6 if own % 96 == 0 else 1
    sems = pltpu.SemaphoreType.DMA((2, members, pieces))
    return pl.pallas_call(
        functools.partial(scatter_body, pieces),
        in_specs=[pl.BlockSpec(memory_space=pltpu.VMEM)],
        out_specs=pl.BlockSpec(memory_space=pltpu.VMEM),
        out_shape=jax.ShapeDtypeStruct((own, width), jnp.float32),
        scratch_shapes=[pltpu.VMEM((2, members, own, width), parts.dtype), sems, sems],
        compiler_params=pltpu.CompilerParams(
            collective_id=collective_id, has_side_effects=True, vmem_limit_bytes=KERNEL_VMEM
        ),
        name="scatter",
    )(parts.reshape(members, own, width))


def unproject_body(*refs):
    grad_refs, weight_refs, refs = refs[:3], refs[3:6], refs[6:]
    tokens_ref, rate_ref, out_ref, sum_ref = refs
    total = 0.0
    for grad_ref, weight_ref in zip(grad_refs, weight_refs):
        total = total + matmul_nt(grad_ref[...], weight_ref[...])
    out_ref[...] = total.astype(jnp.bfloat16)
    part = total * (tokens_ref[...].astype(jnp.float32) * rate_ref[...])

    @pl.when(pl.program_id(0) == 0)
    def _():
        sum_ref[...] = jnp.zeros_like(sum_ref)

    sum_ref[...] += jnp.sum(part, axis=0, keepdims=True)


def unproject(grads, weights, tokens, rates, rows):
    count, width = tokens.shape
    features = grads[0].shape[1]

    def by_rows(cols):
        return pl.BlockSpec((rows, cols), lambda i: (i, 0))

    def whole(*shape):
        return pl.BlockSpec(shape, lambda i: (0, 0))

    return pl.pallas_call(
        unproject_body,
        grid=(count // rows,),
        in_specs=[by_rows(features)] * 3
        + [whole(width, features)] * 3
        + [by_rows(width), by_rows(1)],
        out_specs=[by_rows(width), whole(1, width)],
        out_shape=[
            jax.ShapeDtypeStruct((count, width), jnp.bfloat16),
            jax.ShapeDtypeStruct((1, width), jnp.float32),
        ],
        compiler_params=pltpu.CompilerParams(vmem_limit_bytes=KERNEL_VMEM),
        cost_estimate=NO_COST,
        name="unproject",
    )(*grads, *weights, tokens, rates)


def turn_body(piece_ref, out_ref):
    out_ref[...] = piece_ref[0].astype(jnp.float32).T


def turn(pieces):
    members, rows, features = pieces.shape
    if rows % 128:
        return pieces.reshape(members * rows, features).astype(jnp.float32).T
    return pl.pallas_call(
        turn_body,
        grid=(members,),
        in_specs=[pl.BlockSpec((1, rows, features), lambda i: (i, 0, 0))],
        out_specs=pl.BlockSpec((features, rows), lambda i: (0, i)),
        out_shape=jax.ShapeDtypeStruct((features, members * rows), jnp.float32),
        compiler_params=pltpu.CompilerParams(vmem_limit_bytes=KERNEL_VMEM),
        name="turn",
    )(pieces)


def shards(
    tokens,
    routes,
    seq_lengths,
    cotangent,
    norm1_gain,
    query_weight,
    query_bias,
    key_weight,
    key_bias,
    value_weight,
    value_bias,
    out_weight,
    norm2_gain,
    router_weight,
    shared_switch,
    shared_gate,
    shared_up,
    shared_down,
    expert_gate,
    expert_up,
    expert_down,
):
    own_count = tokens.shape[0]
    width = tokens.shape[1]
    members = lax.axis_size("fsdp")
    columns = lax.axis_size("expert")
    member = lax.axis_index("fsdp")
    own_start = member * own_count
    count = own_count * members
    experts_count = router_weight.shape[1]
    local_experts = experts_count // members
    capacity = 4 * own_count * TOP // (3 * experts_count)

    def own_rows(values):
        return lax.dynamic_slice_in_dim(values, own_start, own_count, 0)

    def take(pieces, place):
        return lax.dynamic_index_in_dim(pieces, place, 0, keepdims=False)

    def put(pieces, piece, place):
        return lax.dynamic_update_index_in_dim(pieces, piece, place, 0)

    def after(value, other):
        return lax.optimization_barrier((value, other))[0]

    def exchange(pieces):
        result = pieces
        for step in range(1, members):
            sent = take(pieces, (member + step) % members)
            came = lax.ppermute(sent, "fsdp", [(m, (m + step) % members) for m in range(members)])
            result = put(result, came, (member - step) % members)
        return result

    def line_gather(block, ties=(), last=()):
        from_low, from_high = [block], [block]
        for step in range(1, members):
            if step > 1 and ties:
                from_low[-1], from_high[-1] = after(
                    (from_low[-1], from_high[-1]), ties[min(step - 2, len(ties) - 1)]
                )
            upward = [(m, m + 1) for m in range(step - 1, members - 1)]
            downward = [(members - 1 - m, members - 2 - m) for m in range(step - 1, members - 1)]
            from_low.append(lax.ppermute(from_low[-1], "fsdp", upward))
            from_high.append(lax.ppermute(from_high[-1], "fsdp", downward))
        from_low[-1], from_high[-1] = after((from_low[-1], from_high[-1]), last)
        window = jnp.concatenate(from_low[:0:-1] + [block] + from_high[1:], axis=0)
        size = block.shape[0]
        return lax.dynamic_slice_in_dim(window, (members - 1 - member) * size, members * size, 0)

    def line_scatter(parts, ties=()):
        blocks = parts.reshape((members, -1) + parts.shape[1:])
        up_sum = down_sum = None
        for step in range(1, members):
            up_block = take(blocks, jnp.minimum(members - step + member, members - 1))
            down_block = take(blocks, jnp.maximum(member - (members - step), 0))
            if up_sum is not None:
                if ties:
                    up_sum, down_sum = after(
                        (up_sum, down_sum), ties[min(step - 2, len(ties) - 1)]
                    )
                up_block = (up_block.astype(jnp.float32) + up_sum.astype(jnp.float32)).astype(
                    parts.dtype
                )
                down_block = (down_block.astype(jnp.float32) + down_sum.astype(jnp.float32)).astype(
                    parts.dtype
                )
            up_sum = lax.ppermute(up_block, "fsdp", [(m, m + 1) for m in range(step)])
            down_sum = lax.ppermute(
                down_block, "fsdp", [(members - 1 - m, members - 2 - m) for m in range(step)]
            )
        if ties:
            up_sum, down_sum = after((up_sum, down_sum), ties[-1])
        own = take(blocks, member).astype(jnp.float32)
        return own + up_sum.astype(jnp.float32) + down_sum.astype(jnp.float32)

    column = lax.axis_index("expert")
    plane_of, j_of = column // local_experts, column % local_experts
    quarter_of = column % members

    def pairs_to_quarters(turn):
        return [
            (plane * local_experts + j, j * members + (plane + turn) % members)
            for plane in range(members)
            for j in range(local_experts)
        ]

    def weights_whole(piece):
        gathered = lax.all_gather(piece, "expert", axis=0, tiled=False)
        return gathered.reshape(local_experts, width, -1)

    def grads_out(crossed, tie):
        came = [
            lax.ppermute(
                take(crossed, (quarter_of - turn) % members),
                "expert",
                [(b, a) for a, b in pairs_to_quarters(turn)],
            )
            for turn in range(members)
        ]
        mixed = jnp.zeros_like(crossed)
        for turn, piece in enumerate(after(came, tie)):
            mixed = put(mixed, piece, (plane_of + turn) % members)
        return lax.optimization_barrier([mixed[:, kind] for kind in range(3)])

    group_tokens, group_routes, crossed = arrive(
        tokens,
        routes.T,
        (expert_gate[0], expert_up[0], expert_down[0].T),
        members,
        local_experts,
    )
    out_piece_rows = out_weight.shape[0] // columns
    out_piece = lax.dynamic_slice_in_dim(out_weight, column * out_piece_rows, out_piece_rows, 0)
    out_full = lax.all_gather(out_piece, ("fsdp", "expert"), axis=0, tiled=True)
    gate_mats, up_mats, down_mats = (weights_whole(piece) for piece in crossed)

    segment, positions = token_layout(seq_lengths[0], count)
    block = math.gcd(count, 256)
    starts = jnp.arange(count, dtype=jnp.int32) - positions
    lows = starts[::block] // block
    starts = starts[None]
    cosine, sine = rotary_tables(positions, HEAD_DIM)
    tokens_own_wide = tokens.astype(jnp.float32)
    gain_first = norm1_gain.astype(jnp.float32)
    normed_first, rate_first, queries, keys_all, values_all = project(
        group_tokens,
        gain_first[None],
        (query_weight, key_weight, value_weight),
        [bias.astype(jnp.float32)[None] for bias in (query_bias, key_bias, value_bias)],
        cosine,
        sine,
        block,
    )
    attended, log_mass = attend(lows, starts, queries, keys_all, values_all, block)
    attended_by_member = gather(attended, members, math.gcd(count // 16, 4), 1)
    tokens_wide = group_tokens.astype(jnp.float32)
    gain_second = norm2_gain.astype(jnp.float32)
    small_count = experts_count + 1
    small_weight = jnp.concatenate([router_weight, shared_switch[:, None]], axis=1)
    small_wide = jnp.pad(small_weight, ((0, 0), (0, 128 - small_count)))
    resid_mid, rate_second, normed_second, small_pre = settle(
        group_tokens, attended_by_member, out_full, gain_second[None], small_wide, block
    )
    resid_own = own_rows(resid_mid)
    rate_own = own_rows(rate_second)

    router_probs = jax.nn.softmax(small_pre[:, :experts_count], axis=-1)
    switch_all = jax.nn.sigmoid(small_pre[:, experts_count:small_count])
    own_ids = member * local_experts + jnp.arange(local_experts, dtype=jnp.int32)
    gates = lax.dynamic_slice_in_dim(router_probs, member * local_experts, local_experts, 1)
    hot = jnp.sum(
        (group_routes[:, :, None, :] == own_ids[None, None, :, None]).astype(jnp.float32), axis=1
    )
    order = jnp.arange(own_count, dtype=jnp.int32)
    before = (order[:, None] > order[None, :]).astype(jnp.bfloat16)
    ranks = jnp.einsum(
        "ut,bjt->bju", before, hot.astype(jnp.bfloat16), preferred_element_type=jnp.float32
    ).astype(jnp.int32)
    places_turned = jnp.where(hot > 0.0, ranks, -1)
    places = places_turned.transpose(0, 2, 1)
    slots = jnp.arange(capacity, dtype=jnp.int32)
    picks = places_turned[:, :, None, :] == slots[None, None, :, None]
    gates_turned = gates.reshape(members, own_count, local_experts).transpose(0, 2, 1)
    slot_gates = jnp.sum(jnp.where(picks, gates_turned[:, :, None, :], 0.0), axis=-1)
    slot_gates = slot_gates.transpose(1, 0, 2).reshape(local_experts, members * capacity, 1)
    places = places.reshape(count, local_experts)

    shared_weights = (shared_gate[None], shared_up[None], shared_down[None])
    shared_out, shared_mid, shared_silu, shared_slope = expert(
        normed_second[None], switch_all[None], *shared_weights, False, block
    )
    row_count = members * capacity
    row_block = math.gcd(row_count, 256)
    rows = dispatch(places_turned, after(normed_second, shared_mid), capacity, members)
    result, expert_mid, expert_silu, expert_slope, scaled = expert(
        rows, slot_gates, gate_mats, up_mats, down_mats, True, row_block
    )
    by_block = (local_experts, members, capacity, width)
    block_low = collect(places, scaled.reshape(by_block), shared_out[0], members, switch_all)

    group_cot = line_gather(
        after(cotangent, attended_by_member), (normed_second, shared_mid), block_low
    )

    grad_wide = group_cot.astype(jnp.float32)
    down_grad = matmul_tn(shared_mid[0], (switch_all * grad_wide).astype(jnp.bfloat16)).astype(
        jnp.bfloat16
    )
    down_sum = lax.psum(down_grad, "expert")
    slot_dot, d_rows, d_expert_gate, d_expert_up, d_in = expert_back(
        dispatch(places_turned, after(group_cot, down_grad), capacity, members),
        result,
        slot_gates,
        expert_silu,
        expert_slope,
        gate_mats,
        up_mats,
        down_mats,
        True,
        row_block,
    )
    expert_grads = weight_grads(rows, d_rows, d_expert_gate, d_expert_up, expert_mid, members)
    expert_pieces = lax.psum_scatter(
        expert_grads.reshape((columns, 3) + expert_grads.shape[3:]),
        "expert",
        scatter_dimension=0,
        tiled=True,
    ).reshape(3, members, -1, expert_grads.shape[-1])
    switch_dot, _, d_shared_gate, d_shared_up, dh_shared = expert_back(
        after(group_cot, (expert_grads, down_sum))[None],
        shared_out,
        switch_all[None],
        shared_silu,
        shared_slope,
        *shared_weights,
        False,
        block,
    )
    switch_logit = switch_dot[0] * switch_all * (1.0 - switch_all)
    shared_grads = tuple(
        grad.astype(jnp.bfloat16)
        for grad in (
            matmul_tn(normed_second, d_shared_gate[0]),
            matmul_tn(normed_second, d_shared_up[0]),
        )
    )
    shared_sums = lax.psum(shared_grads, "expert")
    slot_dots = slot_dot.reshape(local_experts, members, capacity).transpose(1, 0, 2)
    d_gates = jnp.sum(jnp.where(picks, slot_dots[:, :, :, None], 0.0), axis=2)
    d_gates = d_gates.transpose(0, 2, 1).reshape(count, local_experts)
    d_choice = lax.dynamic_update_slice_in_dim(
        jnp.zeros_like(router_probs), d_gates, member * local_experts, 1
    )
    d_logits = router_probs * (d_choice - jnp.sum(gates * d_gates, axis=-1, keepdims=True))
    d_small = jnp.concatenate([d_logits, switch_logit], axis=1)
    d_small_high = d_small.astype(jnp.bfloat16)
    d_small_low = (d_small - d_small_high.astype(jnp.float32)).astype(jnp.bfloat16)
    d_small_both = jnp.pad(
        jnp.concatenate([d_small_high, d_small_low], axis=1),
        ((0, 0), (0, 128 - 2 * small_count)),
    )
    small_both = jnp.pad(
        jnp.concatenate([small_weight.T, small_weight.T], axis=0),
        ((0, 128 - 2 * small_count), (0, 0)),
    )
    dh_low = collect(
        places, d_in.reshape(by_block), dh_shared[0], members, d_small_both, small_both
    )
    small_part = matmul_tn(normed_second, d_small_both)
    small_part = small_part[:, :small_count] + small_part[:, small_count : 2 * small_count]

    block_own = line_scatter(block_low, (d_in, dh_shared, shared_grads))
    block_out = (resid_own + block_own).astype(jnp.bfloat16)
    dh_second_own = scatter(after(dh_low, shared_grads), members, 2)

    grad_own = cotangent.astype(jnp.float32)
    d_resid_own = norm_back(grad_own, dh_second_own, resid_own, rate_own, gain_second)
    d_attn_own = d_resid_own.astype(jnp.bfloat16)
    norm2_part = jnp.sum(dh_second_own * resid_own * rate_own, axis=0)
    d_attn_out = gather(d_attn_own, members, 3 if own_count % 48 == 0 else 1, 3)
    d_attn_out = d_attn_out.reshape(count, width)
    d_context = matmul_nt(d_attn_out, out_weight).astype(jnp.bfloat16)
    d_query_pre, d_key_pre, d_value_pre = attend_back(
        lows,
        starts,
        queries,
        keys_all,
        values_all,
        d_context,
        log_mass,
        cosine,
        sine,
        block,
    )

    d_query_pre, d_key_pre, d_value_pre = after(
        (d_query_pre, d_key_pre, d_value_pre), shared_sums
    )
    dh_first_low, norm1_part = unproject(
        (d_query_pre, d_key_pre, d_value_pre),
        (query_weight, key_weight, value_weight),
        group_tokens,
        rate_first,
        block,
    )
    norm1_part = norm1_part[0]
    attn_grads = tuple(
        matmul_tn(normed_first, d_pre).astype(jnp.bfloat16)
        for d_pre in (d_query_pre, d_key_pre, d_value_pre)
    ) + (matmul_tn(attended, d_attn_out).astype(jnp.bfloat16),)
    crossed_grads = exchange(after(expert_pieces, d_attn_out).transpose(1, 0, 2, 3))
    dh_first_own = scatter(
        after(dh_first_low, (attn_grads, crossed_grads)), members, 4
    )
    grad_tokens = norm_back(
        d_resid_own, dh_first_own, tokens_own_wide, own_rows(rate_first), gain_first
    )

    def pair_sum(values, axis, size):
        if size & (size - 1):
            return lax.psum(values, axis)
        for bit in range(size.bit_length() - 1):
            pairs = [(place, place ^ (1 << bit)) for place in range(size)]
            values = values + lax.ppermute(values, axis, pairs)
        return values

    biases = [
        jnp.sum(d_pre.astype(jnp.float32), axis=0)
        for d_pre in (d_query_pre, d_key_pre, d_value_pre)
    ]
    stats = pair_sum(
        jnp.concatenate([norm1_part, norm2_part, small_part.T.reshape(-1)]), "fsdp", members
    )
    stats = pair_sum(jnp.concatenate([stats] + biases), "expert", columns)
    small_sum = stats[2 * width : (2 + small_count) * width].reshape(-1, width)
    bias_sums = stats[(2 + small_count) * width :].reshape(3, -1)

    attn_sums = lax.psum(attn_grads, "expert")
    expert_sums = grads_out(crossed_grads, dh_first_own)

    return (
        block_out,
        grad_tokens,
        stats[:width],
        attn_sums[0].astype(jnp.float32),
        bias_sums[0],
        attn_sums[1].astype(jnp.float32),
        bias_sums[1],
        attn_sums[2].astype(jnp.float32),
        bias_sums[2],
        attn_sums[3].astype(jnp.float32),
        stats[width : 2 * width],
        small_sum[:experts_count].T,
        small_sum[experts_count],
        shared_sums[0].astype(jnp.float32),
        shared_sums[1].astype(jnp.float32),
        down_sum.astype(jnp.float32),
        expert_sums[0].reshape(1, width // members, -1).astype(jnp.float32),
        expert_sums[1].reshape(1, width // members, -1).astype(jnp.float32),
        turn(expert_sums[2])[None],
    )


def solution(mesh):
    placed = (
        P(("expert", "fsdp"), None),
        P(("expert", "fsdp"), None),
        P("expert", None),
        P(("expert", "fsdp"), None),
        P(),
        P(None, "fsdp"),
        P("fsdp"),
        P(None, "fsdp"),
        P("fsdp"),
        P(None, "fsdp"),
        P("fsdp"),
        P("fsdp", None),
        P(),
        P(),
        P(),
        P(None, "fsdp"),
        P(None, "fsdp"),
        P("fsdp", None),
        P("expert", "fsdp", None),
        P("expert", "fsdp", None),
        P("expert", None, "fsdp"),
    )
    return jax.shard_map(
        shards,
        mesh=mesh,
        in_specs=placed,
        out_specs=(
            P(("expert", "fsdp"), None),
            P(("expert", "fsdp"), None),
            P(),
            P(None, "fsdp"),
            P("fsdp"),
            P(None, "fsdp"),
            P("fsdp"),
            P(None, "fsdp"),
            P("fsdp"),
            P("fsdp", None),
            P(),
            P(),
            P(),
            P(None, "fsdp"),
            P(None, "fsdp"),
            P("fsdp", None),
            P("expert", "fsdp", None),
            P("expert", "fsdp", None),
            P("expert", None, "fsdp"),
        ),
        check_vma=False,
    )
```

```python
import functools
import math

import jax
import jax.numpy as jnp
from jax import lax
from jax.experimental import pallas as pl
from jax.experimental.pallas import tpu as pltpu
from jax.sharding import PartitionSpec as P

HEAD_DIM = 128
TOP = 4


EPSILON = 1e-06
THETA = 1000000.0
MASKED = -1e30
KERNEL_VMEM = 40 * 1024 * 1024
BIG_VMEM = 58 * 1024 * 1024
NO_COST = pl.CostEstimate(flops=0, bytes_accessed=0, transcendentals=0)
LONG_COST = pl.CostEstimate(flops=10**11, bytes_accessed=0, transcendentals=0)


def rms_rate(values):
    return lax.rsqrt(jnp.mean(values * values, axis=-1, keepdims=True) + EPSILON)


def token_layout(lengths, count):
    ends = jnp.cumsum(lengths)
    places = jnp.arange(count, dtype=jnp.int32)
    passed = (places[:, None] >= ends[None, :]).astype(jnp.int32)
    segment = jnp.sum(passed, axis=1)
    start = jnp.sum(passed * lengths[None, :], axis=1)
    return (segment, places - start)


def rotary_tables(positions, width):
    half_width = width // 2
    inverse = THETA ** (-2.0 * jnp.arange(half_width, dtype=jnp.float32) / width)
    angle = positions.astype(jnp.float32)[:, None] * inverse[None, :]
    cosine, sine = jnp.cos(angle), jnp.sin(angle)
    return (
        jnp.concatenate([cosine, cosine], axis=1),
        jnp.concatenate([-sine, sine], axis=1),
    )


def matmul(left_matrix, right_matrix):
    return jnp.dot(left_matrix, right_matrix, preferred_element_type=jnp.float32)


def matmul_tn(left_matrix, right_matrix):
    return lax.dot_general(
        left_matrix, right_matrix, (((0,), (0,)), ((), ())), preferred_element_type=jnp.float32
    )


def matmul_nt(left_matrix, right_matrix):
    return lax.dot_general(
        left_matrix, right_matrix, (((1,), (1,)), ((), ())), preferred_element_type=jnp.float32
    )


def silu_parts(pre_values):
    sigma_values = jax.nn.sigmoid(pre_values)
    return (pre_values * sigma_values, sigma_values * (1.0 + pre_values * (1.0 - sigma_values)))


def norm_back(upstream, dh_values, values, rate, gain):
    gained = dh_values * gain
    return (
        upstream
        + rate * gained
        - values * rate**3 * jnp.mean(gained * values, axis=-1, keepdims=True)
    )


def lane_turn(values):
    return pltpu.roll(values, HEAD_DIM // 2, 1)


def project_body(tokens_ref, gain_ref, weight_refs, bias_refs, cos_ref, sin_ref, outs):
    normed_ref, rate_ref, query_ref, key_ref, value_ref = outs
    wide = tokens_ref[...].astype(jnp.float32)
    rate = rms_rate(wide)
    normed = (wide * rate * gain_ref[...]).astype(jnp.bfloat16)
    normed_ref[...] = normed
    rate_ref[...] = rate
    cosine, sine = cos_ref[...], sin_ref[...]
    for place, out_ref in enumerate((query_ref, key_ref, value_ref)):
        pre = (
            jnp.dot(normed, weight_refs[place][...], preferred_element_type=jnp.float32)
            + bias_refs[place][...]
        )
        if place == 2:
            out_ref[...] = pre.astype(jnp.bfloat16)
            continue
        for head in range(pre.shape[1] // HEAD_DIM):
            part = pre[:, head * HEAD_DIM : (head + 1) * HEAD_DIM]
            turned = part * cosine + lane_turn(part) * sine
            out_ref[:, head * HEAD_DIM : (head + 1) * HEAD_DIM] = turned.astype(jnp.bfloat16)


def project(tokens, gain, weights, biases, cosine, sine, rows):
    count, width = tokens.shape
    features = weights[0].shape[1]

    def body(t, g, w0, w1, w2, b0, b1, b2, c, s, *outs):
        project_body(t, g, (w0, w1, w2), (b0, b1, b2), c, s, outs)

    def by_rows(cols):
        return pl.BlockSpec((rows, cols), lambda i: (i, 0))

    def whole(*shape):
        return pl.BlockSpec(shape, lambda i: (0, 0))

    return pl.pallas_call(
        body,
        grid=(count // rows,),
        in_specs=[by_rows(width), whole(1, width)]
        + [whole(width, features)] * 3
        + [whole(1, features)] * 3
        + [by_rows(HEAD_DIM)] * 2,
        out_specs=[by_rows(width), by_rows(1)] + [by_rows(features)] * 3,
        out_shape=[
            jax.ShapeDtypeStruct((count, width), jnp.bfloat16),
            jax.ShapeDtypeStruct((count, 1), jnp.float32),
        ]
        + [jax.ShapeDtypeStruct((count, features), jnp.bfloat16)] * 3,
        compiler_params=pltpu.CompilerParams(vmem_limit_bytes=KERNEL_VMEM),
        cost_estimate=NO_COST,
        name="project",
    )(tokens, gain, *weights, *biases, cosine, sine)


def scores_of(lows_ref, starts_ref, query, key_ref, wide, block):
    index = pl.program_id(1)
    low = lows_ref[index]
    rows = pl.ds(pl.multiple_of(low * block, block), wide * block)
    keys = key_ref[rows, :]
    scores = lax.dot_general(
        keys, query, (((1,), (1,)), ((), ())), preferred_element_type=jnp.float32
    ) * (1.0 / math.sqrt(HEAD_DIM))
    key_place = low * block + lax.broadcasted_iota(jnp.int32, scores.shape, 0)
    query_place = index * block + lax.broadcasted_iota(jnp.int32, scores.shape, 1)
    allowed = (key_place <= query_place) & (key_place >= starts_ref[...])
    return rows, keys, jnp.where(allowed, scores, MASKED)


def attend_body(lows_ref, starts_ref, query_ref, key_ref, value_ref, out_ref, mass_ref):
    block = query_ref.shape[0]
    index = pl.program_id(1)

    def run(wide):
        rows, _, scores = scores_of(lows_ref, starts_ref, query_ref[...], key_ref, wide, block)
        peak = jnp.max(scores, axis=0, keepdims=True)
        raised = jnp.exp(scores - peak)
        total = jnp.sum(raised, axis=0, keepdims=True)
        soft = (raised * (1.0 / total)).astype(jnp.bfloat16)
        mixed = lax.dot_general(
            value_ref[rows, :], soft, (((0,), (0,)), ((), ())), preferred_element_type=jnp.float32
        )
        out_ref[...] = mixed.T.astype(jnp.bfloat16)
        mass_ref[0] = peak + jnp.log(total)

    for wide in range(1, key_ref.shape[0] // block + 1):
        pl.when(index - lows_ref[index] + 1 == wide)(functools.partial(run, wide))


def attend(lows, starts, queries, keys, values, block):
    count, features = queries.shape
    heads = features // HEAD_DIM
    by_block = pl.BlockSpec((block, HEAD_DIM), lambda h, i, *_: (i, h))
    by_head = pl.BlockSpec((count, HEAD_DIM), lambda h, i, *_: (0, h))
    return pl.pallas_call(
        attend_body,
        grid_spec=pltpu.PrefetchScalarGridSpec(
            num_scalar_prefetch=1,
            grid=(heads, count // block),
            in_specs=[
                pl.BlockSpec((1, block), lambda h, i, *_: (0, i)),
                by_block,
                by_head,
                by_head,
            ],
            out_specs=[by_block, pl.BlockSpec((1, 1, block), lambda h, i, *_: (h, 0, i))],
        ),
        out_shape=[
            jax.ShapeDtypeStruct((count, features), jnp.bfloat16),
            jax.ShapeDtypeStruct((heads, 1, count), jnp.float32),
        ],
        compiler_params=pltpu.CompilerParams(vmem_limit_bytes=KERNEL_VMEM),
        cost_estimate=NO_COST,
        name="attend",
    )(lows, starts, queries, keys, values)


def attend_back_body(
    lows_ref, starts_ref, query_ref, key_ref, value_ref, grad_ref, mass_ref, *rest
):
    cos_ref, sin_ref, d_query_ref, d_key_ref, d_value_ref, key_sum, value_sum = rest
    block = query_ref.shape[0]
    index = pl.program_id(1)
    blocks = key_ref.shape[0] // block
    factor = 1.0 / math.sqrt(HEAD_DIM)

    def rope_back(values, rows):
        return (
            values * cos_ref[rows, :] + lane_turn(values) * -sin_ref[rows, :]
        ).astype(jnp.bfloat16)

    @pl.when(index == 0)
    def _():
        key_sum[...] = jnp.zeros_like(key_sum)
        value_sum[...] = jnp.zeros_like(value_sum)

    def run(wide):
        query, grad = query_ref[...], grad_ref[...]
        rows, keys, scores = scores_of(lows_ref, starts_ref, query, key_ref, wide, block)
        soft = jnp.exp(scores - mass_ref[0])
        d_soft = lax.dot_general(
            value_ref[rows, :], grad, (((1,), (1,)), ((), ())), preferred_element_type=jnp.float32
        )
        inner = jnp.sum(soft * d_soft, axis=0, keepdims=True)
        d_scores = (soft * (d_soft - inner)).astype(jnp.bfloat16)
        value_sum[rows, :] += jnp.dot(
            soft.astype(jnp.bfloat16), grad, preferred_element_type=jnp.float32
        )
        key_sum[rows, :] += jnp.dot(d_scores, query, preferred_element_type=jnp.float32) * factor
        d_query = lax.dot_general(
            keys, d_scores, (((0,), (0,)), ((), ())), preferred_element_type=jnp.float32
        ).T * factor
        here = pl.ds(pl.multiple_of(index * block, block), block)
        d_query_ref[...] = rope_back(d_query, here)

    for wide in range(1, blocks + 1):
        pl.when(index - lows_ref[index] + 1 == wide)(functools.partial(run, wide))

    @pl.when(index == blocks - 1)
    def _():
        d_key_ref[...] = rope_back(key_sum[...], slice(None))
        d_value_ref[...] = value_sum[...].astype(jnp.bfloat16)


def attend_back(lows, starts, queries, keys, values, grads, mass, cosine, sine, block):
    count, features = queries.shape
    heads = features // HEAD_DIM
    by_block = pl.BlockSpec((block, HEAD_DIM), lambda h, i, *_: (i, h))
    by_head = pl.BlockSpec((count, HEAD_DIM), lambda h, i, *_: (0, h))
    whole = pl.BlockSpec((count, HEAD_DIM), lambda h, i, *_: (0, 0))
    return pl.pallas_call(
        attend_back_body,
        grid_spec=pltpu.PrefetchScalarGridSpec(
            num_scalar_prefetch=1,
            grid=(heads, count // block),
            in_specs=[
                pl.BlockSpec((1, block), lambda h, i, *_: (0, i)),
                by_block,
                by_head,
                by_head,
                by_block,
                pl.BlockSpec((1, 1, block), lambda h, i, *_: (h, 0, i)),
                whole,
                whole,
            ],
            out_specs=[by_block, by_head, by_head],
            scratch_shapes=[pltpu.VMEM((count, HEAD_DIM), jnp.float32)] * 2,
        ),
        out_shape=[jax.ShapeDtypeStruct((count, features), jnp.bfloat16)] * 3,
        compiler_params=pltpu.CompilerParams(vmem_limit_bytes=KERNEL_VMEM),
        cost_estimate=NO_COST,
        name="attend_back",
    )(lows, starts, queries, keys, values, grads, mass, cosine, sine)


def settle_body(tokens_ref, attended_ref, weight_ref, gain_ref, small_ref, *outs):
    resid_ref, rate_ref, normed_ref, logit_ref = outs
    total = tokens_ref[...].astype(jnp.float32)
    members, _, features = attended_ref.shape
    for member in range(members):
        total = total + jnp.dot(
            attended_ref[member],
            weight_ref[member * features : (member + 1) * features, :],
            preferred_element_type=jnp.float32,
        )
    rate = rms_rate(total)
    normed = (total * rate * gain_ref[...]).astype(jnp.bfloat16)
    resid_ref[...] = total
    rate_ref[...] = rate
    normed_ref[...] = normed
    logit_ref[...] = jnp.dot(normed, small_ref[...], preferred_element_type=jnp.float32)


def settle(tokens, attended, weight, gain, small, rows):
    count, width = tokens.shape
    members, _, features = attended.shape

    def by_rows(cols):
        return pl.BlockSpec((rows, cols), lambda i: (i, 0))

    def whole(*shape):
        return pl.BlockSpec(shape, lambda i: (0,) * len(shape))

    return pl.pallas_call(
        settle_body,
        grid=(count // rows,),
        in_specs=[
            by_rows(width),
            pl.BlockSpec((members, rows, features), lambda i: (0, i, 0)),
            whole(width, width),
            whole(1, width),
            whole(*small.shape),
        ],
        out_specs=[by_rows(width), by_rows(1), by_rows(width), by_rows(small.shape[1])],
        out_shape=[
            jax.ShapeDtypeStruct((count, width), jnp.float32),
            jax.ShapeDtypeStruct((count, 1), jnp.float32),
            jax.ShapeDtypeStruct((count, width), jnp.bfloat16),
            jax.ShapeDtypeStruct((count, small.shape[1]), jnp.float32),
        ],
        compiler_params=pltpu.CompilerParams(vmem_limit_bytes=KERNEL_VMEM),
        cost_estimate=pl.CostEstimate(
            flops=2 * count * width * width, bytes_accessed=12 * count * width, transcendentals=0
        ),
        name="settle",
    )(tokens, attended, weight, gain, small)


def mixed_places(members, rows):
    for z in range(members):
        for q in range(members):
            yield (z * members + q) * rows, (q * members + z) * rows


def dispatch_body(members, places_ref, source_ref, target_ref):
    slots = target_ref.shape[2]
    quarter = source_ref.shape[1] // members // members
    for which in range(target_ref.shape[0]):
        place = places_ref[0, which : which + 1, :]
        picks = lax.broadcasted_iota(jnp.int32, (slots, place.shape[1]), 0) == place
        picks = picks.astype(jnp.float32).astype(jnp.bfloat16)
        values = jnp.dot(picks, source_ref[...], preferred_element_type=jnp.float32).astype(
            jnp.bfloat16
        )
        for plain, mixed in mixed_places(members, quarter):
            target_ref[which, 0, :, mixed : mixed + quarter] = values[:, plain : plain + quarter]


def dispatch(places, source, slots, members):
    experts, width = places.shape[1], source.shape[1]
    own = source.shape[0] // members
    return pl.pallas_call(
        functools.partial(dispatch_body, members),
        grid=(members,),
        in_specs=[
            pl.BlockSpec((1, experts, own), lambda b: (b, 0, 0)),
            pl.BlockSpec((own, width), lambda b: (b, 0)),
        ],
        out_specs=pl.BlockSpec((experts, 1, slots, width), lambda b: (0, b, 0, 0)),
        out_shape=jax.ShapeDtypeStruct((experts, members, slots, width), jnp.bfloat16),
        compiler_params=pltpu.CompilerParams(vmem_limit_bytes=KERNEL_VMEM),
        cost_estimate=NO_COST,
        name="dispatch",
    )(places, source).reshape(experts, members * slots, width)


def collect_body(members, scaled, places_ref, values_ref, extra_ref, *rest):
    *rest, out_ref = rest
    slots = values_ref.shape[2]
    total = 0.0
    for which in range(values_ref.shape[0]):
        place = places_ref[:, which : which + 1]
        picks = lax.broadcasted_iota(jnp.int32, (place.shape[0], slots), 1) == place
        total = total + jnp.dot(
            picks.astype(jnp.float32).astype(jnp.bfloat16),
            values_ref[which, 0],
            preferred_element_type=jnp.float32,
        )
    extra = extra_ref[...]
    if scaled:
        extra = extra * rest[0][...]
    else:
        extra = extra + jnp.dot(rest[0][...], rest[1][...], preferred_element_type=jnp.float32)
    quarter = extra.shape[1] // members // members
    for plain, mixed in mixed_places(members, quarter):
        out_ref[:, plain : plain + quarter] = (
            extra[:, plain : plain + quarter] + total[:, mixed : mixed + quarter]
        ).astype(out_ref.dtype)


def collect(places, values, extra, members, left, right=None):
    experts, _, slots, width = values.shape
    own = extra.shape[0] // members
    by_block = pl.BlockSpec((own, width), lambda b: (b, 0))
    operands = [places, values, extra]
    in_specs = [
        pl.BlockSpec((own, experts), lambda b: (b, 0)),
        pl.BlockSpec((experts, 1, slots, width), lambda b: (0, b, 0, 0)),
        by_block,
    ]
    operands.append(left)
    in_specs.append(pl.BlockSpec((own, left.shape[1]), lambda b: (b, 0)))
    if right is not None:
        operands.append(right)
        in_specs.append(pl.BlockSpec(right.shape, lambda b: (0, 0)))
    return pl.pallas_call(
        functools.partial(collect_body, members, right is None),
        grid=(members,),
        in_specs=in_specs,
        out_specs=by_block,
        out_shape=jax.ShapeDtypeStruct(extra.shape, jnp.bfloat16),
        compiler_params=pltpu.CompilerParams(vmem_limit_bytes=KERNEL_VMEM),
        cost_estimate=NO_COST,
        name="collect",
    )(*operands)


def expert_specs(experts, count, width, features, rows):
    def by_rows(cols):
        return pl.BlockSpec((1, rows, cols), lambda e, i: (e, i, 0))

    def whole(array):
        return pl.BlockSpec(
            (1,) + array.shape[1:], lambda e, i: (e, 0, 0), pipeline_mode=pl.Buffered(1)
        )

    def out(cols, kind):
        return jax.ShapeDtypeStruct((experts, count, cols), kind)

    return by_rows, whole, out


def expert_body(turned, values_ref, scale_ref, gate_ref, up_ref, down_ref, *outs):
    result_ref, mid_ref, silu_ref, up_slope_ref, *scaled_ref = outs
    values = values_ref[0]
    gate_pre = jnp.dot(values, gate_ref[0], preferred_element_type=jnp.float32)
    up_pre = jnp.dot(values, up_ref[0], preferred_element_type=jnp.float32)
    silu, slope = silu_parts(gate_pre)
    mid = (silu * up_pre).astype(jnp.bfloat16)
    mid_ref[0] = mid
    silu_ref[0] = silu
    up_slope_ref[0] = up_pre * slope
    if turned:
        result = matmul_nt(mid, down_ref[0]).astype(jnp.bfloat16)
        scaled_ref[0][0] = (scale_ref[0] * result.astype(jnp.float32)).astype(jnp.bfloat16)
    else:
        result = matmul(mid, down_ref[0])
    result_ref[0] = result


def expert(values, scales, gate, up, down, turned, rows):
    experts, count, width = values.shape
    features = gate.shape[2]
    by_rows, whole, out = expert_specs(experts, count, width, features, rows)
    low, wide = jnp.bfloat16, jnp.float32
    cols = (width, features, features, features) + (width,) * turned
    kinds = (low if turned else wide, low, wide, wide) + (low,) * turned
    return pl.pallas_call(
        functools.partial(expert_body, turned),
        grid=(experts, count // rows),
        in_specs=[by_rows(width), by_rows(1), whole(gate), whole(up), whole(down)],
        out_specs=[by_rows(c) for c in cols],
        out_shape=[out(c, kind) for c, kind in zip(cols, kinds)],
        compiler_params=pltpu.CompilerParams(vmem_limit_bytes=BIG_VMEM),
        cost_estimate=NO_COST if turned else None,
        name="expert",
    )(values, scales, gate, up, down)


def expert_back_body(turned, grad_ref, result_ref, scale_ref, silu_ref, up_slope_ref, *rest):
    gate_ref, up_ref, down_ref, dot_ref, d_out_ref, d_gate_ref, d_up_ref, d_in_ref = rest
    grad = grad_ref[0].astype(jnp.float32)
    dot_ref[0] = jnp.sum(grad * result_ref[0].astype(jnp.float32), axis=1, keepdims=True)
    d_out = (scale_ref[0] * grad).astype(jnp.bfloat16)
    d_out_ref[0] = d_out
    d_mid = (matmul if turned else matmul_nt)(d_out, down_ref[0])
    d_gate = (d_mid * up_slope_ref[0]).astype(jnp.bfloat16)
    d_up = (d_mid * silu_ref[0]).astype(jnp.bfloat16)
    d_gate_ref[0] = d_gate
    d_up_ref[0] = d_up
    d_in_ref[0] = (matmul_nt(d_gate, gate_ref[0]) + matmul_nt(d_up, up_ref[0])).astype(
        d_in_ref.dtype
    )


def expert_back(grads, results, scales, silu, up_slope, gate, up, down, turned, rows):
    experts, count, width = grads.shape
    features = gate.shape[2]
    by_rows, whole, out = expert_specs(experts, count, width, features, rows)
    low = jnp.bfloat16
    return pl.pallas_call(
        functools.partial(expert_back_body, turned),
        grid=(experts, count // rows),
        in_specs=[by_rows(width), by_rows(width), by_rows(1), by_rows(features), by_rows(features)]
        + [whole(gate), whole(up), whole(down)],
        out_specs=[by_rows(c) for c in (1, width, features, features, width)],
        out_shape=[
            out(1, jnp.float32),
            out(width, low),
            out(features, low),
            out(features, low),
            out(width, results.dtype),
        ],
        compiler_params=pltpu.CompilerParams(vmem_limit_bytes=BIG_VMEM),
        cost_estimate=NO_COST,
        name="expert_back",
    )(grads, results, scales, silu, up_slope, gate, up, down)


def weight_grads_body(rows_ref, d_out_ref, d_gate_ref, d_up_ref, mid_ref, out_ref):
    rows = rows_ref[0].T
    out_ref[0, 0, 0] = matmul(rows, d_gate_ref[0]).astype(jnp.bfloat16)
    out_ref[0, 0, 1] = matmul(rows, d_up_ref[0]).astype(jnp.bfloat16)
    out_ref[0, 0, 2] = matmul(d_out_ref[0].T, mid_ref[0]).astype(jnp.bfloat16)


def weight_grads(rows, d_out, d_gate, d_up, mid, members):
    experts, count, width = rows.shape
    features = mid.shape[2]
    cut = width // members
    by_cols = pl.BlockSpec((1, count, cut), lambda e, i: (e, 0, i))
    whole = pl.BlockSpec((1, count, features), lambda e, i: (e, 0, 0))
    return pl.pallas_call(
        weight_grads_body,
        grid=(experts, members),
        in_specs=[by_cols, by_cols, whole, whole, whole],
        out_specs=pl.BlockSpec((1, 1, 3, cut, features), lambda e, i: (e, i, 0, 0, 0)),
        out_shape=jax.ShapeDtypeStruct((experts, members, 3, cut, features), jnp.bfloat16),
        compiler_params=pltpu.CompilerParams(vmem_limit_bytes=KERNEL_VMEM),
        cost_estimate=NO_COST,
        name="weight_grads",
    )(rows, d_out, d_gate, d_up, mid)


def pair_grads_body(rows_ref, first_ref, second_ref, first_out, second_out):
    rows = rows_ref[...].T
    first_out[...] = matmul(rows, first_ref[...]).astype(jnp.bfloat16)
    second_out[...] = matmul(rows, second_ref[...]).astype(jnp.bfloat16)


def pair_grads(rows, first, second, cut):
    count, width = rows.shape
    features = first.shape[1]
    whole = pl.BlockSpec((count, features), lambda i: (0, 0))
    out = jax.ShapeDtypeStruct((width, features), jnp.bfloat16)
    return pl.pallas_call(
        pair_grads_body,
        grid=(width // cut,),
        in_specs=[pl.BlockSpec((count, cut), lambda i: (0, i)), whole, whole],
        out_specs=[pl.BlockSpec((cut, features), lambda i: (i, 0))] * 2,
        out_shape=[out, out],
        compiler_params=pltpu.CompilerParams(vmem_limit_bytes=KERNEL_VMEM),
        cost_estimate=NO_COST,
        name="pair_grads",
    )(rows, first, second)


MESH = pl.DeviceIdType.MESH


class Line:
    def __init__(self, source, out, send_sems, recv_sems, pieces):
        self.source, self.out = source, out
        self.send_sems, self.recv_sems = send_sems, recv_sems
        self.members, self.rows, self.pieces = out.shape[0], out.shape[1] // pieces, pieces
        self.member = lax.axis_index("fsdp")

    def origin(self, step, way):
        return self.member - step if way == 0 else self.member + step

    def inside(self, place):
        return (place >= 0) & (place < self.members)

    def target(self, way):
        return self.member + 1 if way == 0 else self.member - 1

    def sends(self, step, way):
        return self.inside(self.origin(step - 1, way)) & self.inside(self.target(way))

    def copy(self, origin, step, way, piece, first):
        rows = pl.ds(piece * self.rows, self.rows)
        return pltpu.make_async_remote_copy(
            src_ref=self.source.at[rows] if first else self.out.at[origin, rows],
            dst_ref=self.out.at[origin, rows],
            send_sem=self.send_sems.at[way, step - 1, piece],
            recv_sem=self.recv_sems.at[way, step - 1, piece],
            device_id={"fsdp": self.target(way)},
            device_id_type=MESH,
        )

    def send(self, step, way, piece):
        copy = self.copy(self.origin(step - 1, way), step, way, piece, step == 1)
        pl.when(self.sends(step, way))(copy.start)

    def start(self):
        for piece in range(self.pieces):
            for way in range(2):
                self.send(1, way, piece)

    def hand_on(self, step):
        for piece in range(self.pieces):
            self.hand_on_piece(step, piece)

    def hand_on_piece(self, step, piece):
        for way in range(2):
            origin = self.origin(step, way)
            came = self.copy(origin, step, way, piece, False)
            pl.when(self.inside(origin))(came.wait_recv)
            if step < self.members - 1:
                self.send(step + 1, way, piece)

    def finish(self):
        for step in range(1, self.members):
            for piece in range(self.pieces):
                for way in range(2):
                    copy = self.copy(self.origin(step - 1, way), step, way, piece, step == 1)
                    pl.when(self.sends(step, way))(copy.wait_send)


def arrive_body(members, local_experts, pieces, *refs):
    tokens_ref, routes_ref, *refs = refs
    chunk_refs, refs = refs[:3], refs[3:]
    group_ref, routes_out, *refs = refs
    mixed_refs, crossed_refs, refs = refs[:3], refs[3:6], refs[6:]
    line_send, line_recv, routes_send, routes_recv, mix_send, mix_recv, refs = *refs[:6], refs[6:]
    cross_send, cross_recv, own_sems = refs
    columns = members * local_experts
    column, member = lax.axis_index("expert"), lax.axis_index("fsdp")
    plane, j = column // local_experts, column % local_experts
    rows = chunk_refs[0].shape[0] // members

    barrier = pltpu.get_barrier_semaphore()
    for other in range(1, columns):
        pl.semaphore_signal(
            barrier, inc=1, device_id={"expert": (column + other) % columns}, device_id_type=MESH
        )
    for other in range(1, members):
        pl.semaphore_signal(
            barrier, inc=1, device_id={"fsdp": (member + other) % members}, device_id_type=MESH
        )
    pl.semaphore_wait(barrier, columns + members - 2)

    line = Line(tokens_ref, group_ref, line_send, line_recv, pieces)
    line.start()
    own_copies = [
        pltpu.make_async_copy(tokens_ref, group_ref.at[member], own_sems.at[0]),
        pltpu.make_async_copy(routes_ref, routes_out.at[member], own_sems.at[1]),
    ]
    for copy in own_copies:
        copy.start()

    def mix(turn, kind):
        part = (plane + turn) % members
        target = j * members + part
        source = chunk_refs[kind].at[pl.ds(pl.multiple_of(part * rows, rows), rows)]
        remote = pltpu.make_async_remote_copy(
            src_ref=source,
            dst_ref=mixed_refs[kind].at[plane],
            send_sem=mix_send.at[turn, kind],
            recv_sem=mix_recv.at[turn, kind],
            device_id={"expert": target},
            device_id_type=MESH,
        )
        local = pltpu.make_async_copy(
            source, mixed_refs[kind].at[plane], mix_send.at[turn, kind]
        )
        return target == column, remote, local

    turns = [(turn, kind) for turn in range(members) for kind in range(3)]
    for turn, kind in turns:
        here, remote, local = mix(turn, kind)
        pl.when(here)(local.start)
        pl.when(jnp.logical_not(here))(remote.start)

    def route(other):
        return pltpu.make_async_remote_copy(
            src_ref=routes_ref,
            dst_ref=routes_out.at[member],
            send_sem=routes_send.at[other - 1],
            recv_sem=routes_recv.at[other - 1],
            device_id={"fsdp": (member + other) % members},
            device_id_type=MESH,
        )

    for other in range(1, members):
        route(other).start()
    for step in range(1, members - 1):
        line.hand_on(step)
    for turn, kind in turns:
        here, remote, local = mix(turn, kind)
        pl.when(here)(local.wait)
        pl.when(jnp.logical_not(here))(remote.wait)

    def cross(other, kind):
        target = (member + other) % members
        return pltpu.make_async_remote_copy(
            src_ref=mixed_refs[kind].at[target],
            dst_ref=crossed_refs[kind].at[member],
            send_sem=cross_send.at[other - 1, kind],
            recv_sem=cross_recv.at[other - 1, kind],
            device_id={"fsdp": target},
            device_id_type=MESH,
        )

    for kind in range(3):
        own_copies.append(
            pltpu.make_async_copy(
                mixed_refs[kind].at[member], crossed_refs[kind].at[member], own_sems.at[2 + kind]
            )
        )
        own_copies[-1].start()
        for other in range(1, members):
            cross(other, kind).start()
    line.hand_on(members - 1)
    line.finish()
    for other in range(1, members):
        route(other).wait()
        for kind in range(3):
            cross(other, kind).wait()
    for copy in own_copies:
        copy.wait()


def arrive(tokens, routes, chunks, members, local_experts):
    own, width = tokens.shape
    pieces = 3 if own % 48 == 0 else 1
    rows, cols = chunks[0].shape
    piece = jax.ShapeDtypeStruct((members, rows // members, cols), jnp.bfloat16)
    anywhere = pl.BlockSpec(memory_space=pl.ANY)
    sems = pltpu.SemaphoreType.DMA
    out_shape = [
        jax.ShapeDtypeStruct((members, own, width), jnp.bfloat16),
        jax.ShapeDtypeStruct((members,) + routes.shape, jnp.int32),
    ] + [piece] * 6
    group, group_routes, *rest = pl.pallas_call(
        functools.partial(arrive_body, members, local_experts, pieces),
        in_specs=[anywhere] * 5,
        out_specs=[anywhere] * len(out_shape),
        out_shape=out_shape,
        scratch_shapes=[sems((2, members - 1, pieces))] * 2
        + [sems((members - 1,))] * 2
        + [sems((members, 3))] * 2
        + [sems((members - 1, 3))] * 2
        + [sems((5,))],
        compiler_params=pltpu.CompilerParams(collective_id=0, has_side_effects=True),
        name="arrive",
    )(tokens, routes, *chunks)
    return group.reshape(members * own, width), group_routes, rest[3:]


def greet(members):
    member = lax.axis_index("fsdp")
    barrier = pltpu.get_barrier_semaphore()
    for other in range(1, members):
        pl.semaphore_signal(
            barrier, inc=1, device_id={"fsdp": (member + other) % members}, device_id_type=MESH
        )
    pl.semaphore_wait(barrier, members - 1)


def gather_body(pieces, block_ref, out_ref, send_sems, recv_sems, own_sem):
    members = out_ref.shape[0]
    member = lax.axis_index("fsdp")
    greet(members)
    line = Line(block_ref, out_ref, send_sems, recv_sems, pieces)
    line.start()
    own = pltpu.make_async_copy(block_ref, out_ref.at[member], own_sem)
    own.start()
    for step in range(1, members):
        line.hand_on(step)
    line.finish()
    own.wait()


def gather(block, members, pieces, collective_id):
    sems = pltpu.SemaphoreType.DMA
    return pl.pallas_call(
        functools.partial(gather_body, pieces),
        in_specs=[pl.BlockSpec(memory_space=pl.ANY)],
        out_specs=pl.BlockSpec(memory_space=pl.ANY),
        out_shape=jax.ShapeDtypeStruct((members,) + block.shape, block.dtype),
        scratch_shapes=[sems((2, members - 1, pieces))] * 2 + [sems],
        compiler_params=pltpu.CompilerParams(collective_id=collective_id, has_side_effects=True),
        name="gather",
    )(block)


class Sums:
    def __init__(self, parts, came, send_sems, recv_sems, pieces):
        self.parts, self.came = parts, came
        self.send_sems, self.recv_sems = send_sems, recv_sems
        self.members, self.rows = parts.shape[0], parts.shape[1] // pieces
        self.member = lax.axis_index("fsdp")

    def clear(self):
        for way, end in ((0, 0), (1, self.members - 1)):

            @pl.when(self.member == end)
            def _():
                self.came[way, end] = jnp.zeros_like(self.came[way, end])

    def copy(self, way, block, piece, first):
        here = pl.ds(piece * self.rows, self.rows)
        source = self.parts.at[block, here] if first else self.came.at[way, block, here]
        return pltpu.make_async_remote_copy(
            src_ref=source,
            dst_ref=self.came.at[way, block, here],
            send_sem=self.send_sems.at[way, block, piece],
            recv_sem=self.recv_sems.at[way, block, piece],
            device_id={"fsdp": self.member + 1 if way == 0 else self.member - 1},
            device_id_type=MESH,
        )

    def passes(self, way, block):
        member, last = self.member, self.members - 1
        if way == 0:
            starts = (member == 0) & (block > 0)
            return starts, (member > 0) & (block > member), (member > 0) & (block == member)
        starts = (member == last) & (block < last)
        return starts, (member < last) & (block < member), (member < last) & (block == member)

    def turns(self):
        for turn in range(self.members):
            for way in range(2):
                yield way, self.members - 1 - turn if way == 0 else turn

    def hand_on(self, piece):
        here = pl.ds(piece * self.rows, self.rows)
        for way, block in self.turns():
            starts, hands_on, _ = self.passes(way, block)
            pl.when(starts)(self.copy(way, block, piece, True).start)

            @pl.when(hands_on)
            def _():
                self.copy(way, block, piece, False).wait_recv()
                self.came[way, block, here] = (
                    self.came[way, block, here].astype(jnp.float32)
                    + self.parts[block, here].astype(jnp.float32)
                ).astype(self.came.dtype)
                self.copy(way, block, piece, False).start()

    def total(self, piece):
        for way, block in self.turns():
            pl.when(self.passes(way, block)[2])(self.copy(way, block, piece, False).wait_recv)
        here = pl.ds(piece * self.rows, self.rows)
        return (
            self.parts[self.member, here].astype(jnp.float32)
            + self.came[0, self.member, here].astype(jnp.float32)
            + self.came[1, self.member, here].astype(jnp.float32)
        )

    def finish(self, piece):
        for way, block in self.turns():
            starts, hands_on, _ = self.passes(way, block)
            pl.when(starts)(self.copy(way, block, piece, True).wait_send)
            pl.when(hands_on)(self.copy(way, block, piece, False).wait_send)


def pair_stages(members, columns):
    for size, axis in ((members, "fsdp"), (columns, "expert")):
        for bit in range(size.bit_length() - 1):
            yield axis, 1 << bit


def scatter_body(pieces, columns, line_rows, parts_ref, stats_ref, crossed_ref, *refs):
    out_ref, stats_out, mixed_ref, came, levels, stats_came, send_sems, recv_sems, *refs = refs
    stats_send, stats_recv, mix_send, mix_recv = refs
    members = parts_ref.shape[0]
    stages = list(pair_stages(members, columns))
    member, column = lax.axis_index("fsdp"), lax.axis_index("expert")
    barrier = pltpu.get_barrier_semaphore()
    for other in range(1, members):
        pl.semaphore_signal(
            barrier, inc=1, device_id={"fsdp": (member + other) % members}, device_id_type=MESH
        )
    for other in range(1, columns):
        pl.semaphore_signal(
            barrier, inc=1, device_id={"expert": (column + other) % columns}, device_id_type=MESH
        )
    pl.semaphore_wait(barrier, members + columns - 2)

    def exchange(stage):
        axis, distance = stages[stage]
        place = member if axis == "fsdp" else column
        partner = place + distance - 2 * distance * ((place // distance) % 2)
        return pltpu.make_async_remote_copy(
            src_ref=levels.at[stage],
            dst_ref=stats_came.at[stage],
            send_sem=stats_send.at[stage],
            recv_sem=stats_recv.at[stage],
            device_id={axis: partner},
            device_id_type=MESH,
        )

    def settle_stage(stage):
        exchange(stage).wait_recv()
        value = levels[stage] + stats_came[stage]
        if stages[stage][0] == "fsdp":
            rows = lax.broadcasted_iota(jnp.int32, value.shape, 0)
            value = jnp.where(rows < line_rows, value, levels[stage])
        if stage + 1 < len(stages):
            levels[stage + 1] = value
            exchange(stage + 1).start()
        else:
            stats_out[...] = value

    def mix(turn):
        quarter, j = column % members, column // members
        plane = (quarter - turn + members) % members
        target = plane * (columns // members) + j
        remote = pltpu.make_async_remote_copy(
            src_ref=crossed_ref.at[plane],
            dst_ref=mixed_ref.at[quarter],
            send_sem=mix_send.at[turn],
            recv_sem=mix_recv.at[turn],
            device_id={"expert": target},
            device_id_type=MESH,
        )
        local = pltpu.make_async_copy(
            crossed_ref.at[plane], mixed_ref.at[quarter], mix_send.at[turn]
        )
        return target == column, remote, local

    for turn in range(members):
        here, remote, local = mix(turn)
        pl.when(here)(local.start)
        pl.when(jnp.logical_not(here))(remote.start)
    sums = Sums(parts_ref, came, send_sems, recv_sems, pieces)
    sums.clear()
    levels[0] = stats_ref[...]
    exchange(0).start()
    for piece in range(pieces):
        sums.hand_on(piece)
        if piece < len(stages):
            settle_stage(piece)
    for stage in range(pieces, len(stages)):
        settle_stage(stage)
    for piece in range(pieces):
        out_ref[piece * sums.rows : (piece + 1) * sums.rows, :] = sums.total(piece)
    for piece in range(pieces):
        sums.finish(piece)
    for stage in range(len(stages)):
        exchange(stage).wait_send()
    for turn in range(members):
        here, remote, local = mix(turn)
        pl.when(here)(local.wait)
        pl.when(jnp.logical_not(here))(remote.wait)


def scatter(parts, stats, crossed, line_rows, members, columns, collective_id, cost):
    count, width = parts.shape
    own = count // members
    pieces = 6 if own % 96 == 0 else 1
    stages = len(list(pair_stages(members, columns)))
    sems = pltpu.SemaphoreType.DMA
    in_vmem = pl.BlockSpec(memory_space=pltpu.VMEM)
    anywhere = pl.BlockSpec(memory_space=pl.ANY)
    return pl.pallas_call(
        functools.partial(scatter_body, pieces, columns, line_rows),
        in_specs=[in_vmem, in_vmem, anywhere],
        out_specs=[in_vmem, in_vmem, anywhere],
        out_shape=[
            jax.ShapeDtypeStruct((own, width), jnp.float32),
            jax.ShapeDtypeStruct(stats.shape, jnp.float32),
            jax.ShapeDtypeStruct(crossed.shape, crossed.dtype),
        ],
        scratch_shapes=[
            pltpu.VMEM((2, members, own, width), parts.dtype),
            pltpu.VMEM((stages,) + stats.shape, jnp.float32),
            pltpu.VMEM((stages,) + stats.shape, jnp.float32),
        ]
        + [sems((2, members, pieces))] * 2
        + [sems((stages,))] * 2
        + [sems((members,))] * 2,
        compiler_params=pltpu.CompilerParams(
            collective_id=collective_id, has_side_effects=True, vmem_limit_bytes=KERNEL_VMEM
        ),
        cost_estimate=cost,
        name="scatter",
    )(parts.reshape(members, own, width), stats, crossed)


def turnaround_body(pieces, *refs):
    parts_ref, resid_all, rate_all, grad_ref, gain_ref, d_resid_ref, sum_ref, out_ref, *refs = refs
    came, resid_ref, rate_ref, low, send_sems, recv_sems, line_send, line_recv, own_sems = refs
    members, own_rows = parts_ref.shape[:2]
    greet(members)
    here = pl.ds(pl.multiple_of(lax.axis_index("fsdp") * own_rows, own_rows), own_rows)
    reads = [
        pltpu.make_async_copy(resid_all.at[here], resid_ref, own_sems.at[1]),
        pltpu.make_async_copy(rate_all.at[here], rate_ref, own_sems.at[2]),
    ]
    for read in reads:
        read.start()
    sums = Sums(parts_ref, came, send_sems, recv_sems, pieces)
    sums.clear()
    line = Line(low, out_ref, line_send, line_recv, pieces)
    sum_ref[...] = jnp.zeros_like(sum_ref)
    for read in reads:
        read.wait()
    for phase in range(pieces + members - 1 + 1):
        if phase < pieces:
            sums.hand_on(phase)
        ready = phase - 1
        if 0 <= ready < pieces:
            here = slice(ready * sums.rows, (ready + 1) * sums.rows)
            dh = sums.total(ready)
            resid, rate = resid_ref[here, :], rate_ref[here, :]
            sum_ref[...] += jnp.sum(dh * resid * rate, axis=0, keepdims=True)
            d_resid = norm_back(
                grad_ref[here, :].astype(jnp.float32), dh, resid, rate, gain_ref[...]
            )
            d_resid_ref[here, :] = d_resid
            low[here, :] = d_resid.astype(low.dtype)
            for way in range(2):
                line.send(1, way, ready)
        for step in range(1, members):
            if 0 <= ready - step < pieces:
                line.hand_on_piece(step, ready - step)
    own = pltpu.make_async_copy(low, out_ref.at[line.member], own_sems.at[0])
    own.start()
    line.finish()
    for piece in range(pieces):
        sums.finish(piece)
    own.wait()


def turnaround(parts, resid, rate, grad, gain, members, collective_id):
    count, width = parts.shape
    own = count // members
    pieces = 12 if own % 192 == 0 else 1
    sems = pltpu.SemaphoreType.DMA
    in_vmem = pl.BlockSpec(memory_space=pltpu.VMEM)
    anywhere = pl.BlockSpec(memory_space=pl.ANY)
    d_resid, gain_part, d_attn = pl.pallas_call(
        functools.partial(turnaround_body, pieces),
        in_specs=[in_vmem, anywhere, anywhere, in_vmem, in_vmem],
        out_specs=[in_vmem, in_vmem, anywhere],
        out_shape=[
            jax.ShapeDtypeStruct((own, width), jnp.float32),
            jax.ShapeDtypeStruct((1, width), jnp.float32),
            jax.ShapeDtypeStruct((members, own, width), jnp.bfloat16),
        ],
        scratch_shapes=[
            pltpu.VMEM((2, members, own, width), parts.dtype),
            pltpu.VMEM((own, width), jnp.float32),
            pltpu.VMEM((own, 1), jnp.float32),
            pltpu.VMEM((own, width), jnp.bfloat16),
        ]
        + [sems((2, members, pieces))] * 2
        + [sems((2, members - 1, pieces))] * 2
        + [sems((3,))],
        compiler_params=pltpu.CompilerParams(
            collective_id=collective_id, has_side_effects=True, vmem_limit_bytes=KERNEL_VMEM
        ),
        name="turnaround",
    )(parts.reshape(members, own, width), resid, rate, grad, gain)
    return d_resid, gain_part[0], d_attn.reshape(count, width)


def unproject_body(*refs):
    grad_refs, weight_refs, refs = refs[:3], refs[3:6], refs[6:]
    tokens_ref, rate_ref, out_ref, sum_ref, *bias_refs = refs
    total = 0.0
    for grad_ref, weight_ref in zip(grad_refs, weight_refs):
        total = total + matmul_nt(grad_ref[...], weight_ref[...])
    out_ref[...] = total.astype(jnp.bfloat16)
    part = total * (tokens_ref[...].astype(jnp.float32) * rate_ref[...])

    @pl.when(pl.program_id(0) == 0)
    def _():
        for ref in (sum_ref, *bias_refs):
            ref[...] = jnp.zeros_like(ref)

    sum_ref[...] += jnp.sum(part, axis=0, keepdims=True)
    for grad_ref, bias_ref in zip(grad_refs, bias_refs):
        bias_ref[...] += jnp.sum(grad_ref[...].astype(jnp.float32), axis=0, keepdims=True)


def unproject(grads, weights, tokens, rates, rows):
    count, width = tokens.shape
    features = grads[0].shape[1]

    def by_rows(cols):
        return pl.BlockSpec((rows, cols), lambda i: (i, 0))

    def whole(*shape):
        return pl.BlockSpec(shape, lambda i: (0, 0))

    return pl.pallas_call(
        unproject_body,
        grid=(count // rows,),
        in_specs=[by_rows(features)] * 3
        + [whole(width, features)] * 3
        + [by_rows(width), by_rows(1)],
        out_specs=[by_rows(width), whole(1, width)] + [whole(1, features)] * 3,
        out_shape=[
            jax.ShapeDtypeStruct((count, width), jnp.bfloat16),
            jax.ShapeDtypeStruct((1, width), jnp.float32),
        ]
        + [jax.ShapeDtypeStruct((1, features), jnp.float32)] * 3,
        compiler_params=pltpu.CompilerParams(vmem_limit_bytes=KERNEL_VMEM),
        cost_estimate=NO_COST,
        name="unproject",
    )(*grads, *weights, tokens, rates)


def attend_grads_body(rows_ref, d_query, d_key, d_value, attended_ref, d_out_ref, *outs):
    rows = rows_ref[...].T
    for d_ref, out in zip((d_query, d_key, d_value), outs):
        out[...] = matmul(rows, d_ref[...]).astype(jnp.bfloat16)
    outs[3][...] = matmul(attended_ref[...].T, d_out_ref[...]).astype(jnp.bfloat16)


def attend_grads(rows, d_pres, attended, d_out, cut):
    count, width = rows.shape
    features = attended.shape[1]
    by_cols = pl.BlockSpec((count, cut), lambda i: (0, i))
    whole = pl.BlockSpec((count, features), lambda i: (0, 0))
    tall = pl.BlockSpec((cut, features), lambda i: (i, 0))
    return pl.pallas_call(
        attend_grads_body,
        grid=(width // cut,),
        in_specs=[by_cols] + [whole] * 4 + [by_cols],
        out_specs=[tall] * 3 + [pl.BlockSpec((features, cut), lambda i: (0, i))],
        out_shape=[jax.ShapeDtypeStruct((width, features), jnp.bfloat16)] * 3
        + [jax.ShapeDtypeStruct((features, width), jnp.bfloat16)],
        compiler_params=pltpu.CompilerParams(vmem_limit_bytes=KERNEL_VMEM),
        cost_estimate=NO_COST,
        name="attend_grads",
    )(rows, *d_pres, attended, d_out)


def turn_body(piece_ref, out_ref):
    out_ref[...] = piece_ref[0].astype(jnp.float32).T


def turn(pieces):
    members, rows, features = pieces.shape
    if rows % 128:
        return pieces.reshape(members * rows, features).astype(jnp.float32).T
    return pl.pallas_call(
        turn_body,
        grid=(members,),
        in_specs=[pl.BlockSpec((1, rows, features), lambda i: (i, 0, 0))],
        out_specs=pl.BlockSpec((features, rows), lambda i: (0, i)),
        out_shape=jax.ShapeDtypeStruct((features, members * rows), jnp.float32),
        compiler_params=pltpu.CompilerParams(vmem_limit_bytes=KERNEL_VMEM),
        name="turn",
    )(pieces)


def shards(
    tokens,
    routes,
    seq_lengths,
    cotangent,
    norm1_gain,
    query_weight,
    query_bias,
    key_weight,
    key_bias,
    value_weight,
    value_bias,
    out_weight,
    norm2_gain,
    router_weight,
    shared_switch,
    shared_gate,
    shared_up,
    shared_down,
    expert_gate,
    expert_up,
    expert_down,
):
    own_count = tokens.shape[0]
    width = tokens.shape[1]
    members = lax.axis_size("fsdp")
    columns = lax.axis_size("expert")
    member = lax.axis_index("fsdp")
    own_start = member * own_count
    count = own_count * members
    experts_count = router_weight.shape[1]
    local_experts = experts_count // members
    capacity = 4 * own_count * TOP // (3 * experts_count)

    def own_rows(values):
        return lax.dynamic_slice_in_dim(values, own_start, own_count, 0)

    def take(pieces, place):
        return lax.dynamic_index_in_dim(pieces, place, 0, keepdims=False)

    def put(pieces, piece, place):
        return lax.dynamic_update_index_in_dim(pieces, piece, place, 0)

    def after(value, other):
        return lax.optimization_barrier((value, other))[0]

    def exchange(pieces):
        result = pieces
        for step in range(1, members):
            sent = take(pieces, (member + step) % members)
            came = lax.ppermute(sent, "fsdp", [(m, (m + step) % members) for m in range(members)])
            result = put(result, came, (member - step) % members)
        return result

    def one_hop(low, high, step):
        upward = [(m, m + 1) for m in range(step - 1, members - 1)]
        downward = [(members - 1 - m, members - 2 - m) for m in range(step - 1, members - 1)]
        return lax.ppermute(low, "fsdp", upward), lax.ppermute(high, "fsdp", downward)

    def line_gather(block, first, ties, last):
        from_low, from_high = [block, first[0]], [block, first[1]]
        for step in range(2, members):
            from_low[-1], from_high[-1] = after(
                (from_low[-1], from_high[-1]), ties[min(step - 2, len(ties) - 1)]
            )
            low, high = one_hop(from_low[-1], from_high[-1], step)
            from_low.append(low)
            from_high.append(high)
        from_low[-1], from_high[-1] = after((from_low[-1], from_high[-1]), last)
        window = jnp.concatenate(from_low[:0:-1] + [block] + from_high[1:], axis=0)
        size = block.shape[0]
        return lax.dynamic_slice_in_dim(window, (members - 1 - member) * size, members * size, 0)

    def relay(parts, step, sums=None):
        blocks = parts.reshape((members, -1) + parts.shape[1:])
        up_block = take(blocks, jnp.minimum(members - step + member, members - 1))
        down_block = take(blocks, jnp.maximum(member - (members - step), 0))
        if sums is not None:
            up_block, down_block = (
                (block.astype(jnp.float32) + came.astype(jnp.float32)).astype(parts.dtype)
                for block, came in zip((up_block, down_block), sums)
            )
        up_pairs = [(m, m + 1) for m in range(step)]
        down_pairs = [(members - 1 - m, members - 2 - m) for m in range(step)]
        return (
            lax.ppermute(up_block, "fsdp", up_pairs),
            lax.ppermute(down_block, "fsdp", down_pairs),
        )

    column = lax.axis_index("expert")

    def weights_whole(piece):
        gathered = lax.all_gather(piece, "expert", axis=0, tiled=False)
        return gathered.reshape(local_experts, width, -1)

    group_tokens, group_routes, crossed = arrive(
        tokens,
        routes.T,
        (expert_gate[0], expert_up[0], expert_down[0].T),
        members,
        local_experts,
    )
    out_piece_rows = out_weight.shape[0] // columns
    out_piece = lax.dynamic_slice_in_dim(out_weight, column * out_piece_rows, out_piece_rows, 0)
    out_full = lax.all_gather(out_piece, ("fsdp", "expert"), axis=0, tiled=True)
    gate_mats, up_mats, down_mats = (weights_whole(piece) for piece in crossed)

    segment, positions = token_layout(seq_lengths[0], count)
    block = math.gcd(count, 256)
    starts = jnp.arange(count, dtype=jnp.int32) - positions
    lows = starts[::block] // block
    starts = starts[None]
    cosine, sine = rotary_tables(positions, HEAD_DIM)
    tokens_own_wide = tokens.astype(jnp.float32)
    gain_first = norm1_gain.astype(jnp.float32)
    normed_first, rate_first, queries, keys_all, values_all = project(
        group_tokens,
        gain_first[None],
        (query_weight, key_weight, value_weight),
        [bias.astype(jnp.float32)[None] for bias in (query_bias, key_bias, value_bias)],
        cosine,
        sine,
        block,
    )
    attended, log_mass = attend(lows, starts, queries, keys_all, values_all, block)
    cot_tied = after(cotangent, group_tokens)
    attended, cot_hop = lax.optimization_barrier((attended, one_hop(cot_tied, cot_tied, 1)))
    attended_by_member = gather(attended, members, math.gcd(count // 16, 4), 1)
    tokens_wide = group_tokens.astype(jnp.float32)
    gain_second = norm2_gain.astype(jnp.float32)
    small_count = experts_count + 1
    small_weight = jnp.concatenate([router_weight, shared_switch[:, None]], axis=1)
    small_wide = jnp.pad(small_weight, ((0, 0), (0, 128 - small_count)))
    resid_mid, rate_second, normed_second, small_pre = settle(
        group_tokens, attended_by_member, out_full, gain_second[None], small_wide, block
    )
    resid_own = own_rows(resid_mid)

    router_probs = jax.nn.softmax(small_pre[:, :experts_count], axis=-1)
    switch_all = jax.nn.sigmoid(small_pre[:, experts_count:small_count])
    own_ids = member * local_experts + jnp.arange(local_experts, dtype=jnp.int32)
    gates = lax.dynamic_slice_in_dim(router_probs, member * local_experts, local_experts, 1)
    hot = jnp.sum(
        (group_routes[:, :, None, :] == own_ids[None, None, :, None]).astype(jnp.float32), axis=1
    )
    order = jnp.arange(own_count, dtype=jnp.int32)
    before = (order[:, None] > order[None, :]).astype(jnp.bfloat16)
    ranks = jnp.einsum(
        "ut,bjt->bju", before, hot.astype(jnp.bfloat16), preferred_element_type=jnp.float32
    ).astype(jnp.int32)
    places_turned = jnp.where(hot > 0.0, ranks, -1)
    places = places_turned.transpose(0, 2, 1)
    slots = jnp.arange(capacity, dtype=jnp.int32)
    picks = places_turned[:, :, None, :] == slots[None, None, :, None]
    gates_turned = gates.reshape(members, own_count, local_experts).transpose(0, 2, 1)
    slot_gates = jnp.sum(jnp.where(picks, gates_turned[:, :, None, :], 0.0), axis=-1)
    slot_gates = slot_gates.transpose(1, 0, 2).reshape(local_experts, members * capacity, 1)
    places = places.reshape(count, local_experts)

    shared_weights = (shared_gate[None], shared_up[None], shared_down[None])
    shared_out, shared_mid, shared_silu, shared_slope = expert(
        normed_second[None], switch_all[None], *shared_weights, False, block
    )
    group_cot = line_gather(
        cotangent, cot_hop, (attended_by_member, normed_second), shared_mid
    )
    row_count = members * capacity
    row_block = math.gcd(row_count, 256)
    rows = dispatch(places_turned, after(normed_second, shared_mid), capacity, members)

    grad_wide = group_cot.astype(jnp.float32)
    down_grad = matmul_tn(shared_mid[0], (switch_all * grad_wide).astype(jnp.bfloat16)).astype(
        jnp.bfloat16
    )
    down_sum = lax.psum(down_grad, "expert")
    switch_dot, _, d_shared_gate, d_shared_up, dh_shared = expert_back(
        after(group_cot, down_grad)[None],
        shared_out,
        switch_all[None],
        shared_silu,
        shared_slope,
        *shared_weights,
        False,
        block,
    )
    switch_logit = switch_dot[0] * switch_all * (1.0 - switch_all)
    shared_grads = tuple(
        pair_grads(normed_second, d_shared_gate[0], d_shared_up[0], math.gcd(width, 512))
    )
    shared_sums = lax.psum(shared_grads, "expert")

    result, expert_mid, expert_silu, expert_slope, scaled = expert(
        after(rows, shared_grads), slot_gates, gate_mats, up_mats, down_mats, True, row_block
    )
    by_block = (local_experts, members, capacity, width)
    block_low = collect(places, scaled.reshape(by_block), shared_out[0], members, switch_all)
    slot_dot, d_rows, d_expert_gate, d_expert_up, d_in = expert_back(
        dispatch(places_turned, after(group_cot, block_low), capacity, members),
        result,
        slot_gates,
        expert_silu,
        expert_slope,
        gate_mats,
        up_mats,
        down_mats,
        True,
        row_block,
    )
    block_sums = relay(block_low, 1)
    expert_grads = weight_grads(
        after(rows, block_sums), d_rows, d_expert_gate, d_expert_up, expert_mid, members
    )
    block_sums = relay(block_low, 2, after(block_sums, d_in))
    slot_dot, block_sums, expert_grads = lax.optimization_barrier(
        (slot_dot, block_sums, expert_grads)
    )
    for step in range(3, members):
        block_sums = relay(block_low, step, block_sums)
    expert_pieces = lax.psum_scatter(
        expert_grads.reshape((columns, 3) + expert_grads.shape[3:]),
        "expert",
        scatter_dimension=0,
        tiled=True,
    ).reshape(3, members, -1, expert_grads.shape[-1])
    slot_dots = slot_dot.reshape(local_experts, members, capacity).transpose(1, 0, 2)
    d_gates = jnp.sum(jnp.where(picks, slot_dots[:, :, :, None], 0.0), axis=2)
    d_gates = d_gates.transpose(0, 2, 1).reshape(count, local_experts)
    ids = jnp.arange(experts_count, dtype=jnp.int32)
    d_choice = sum(
        jnp.where(ids[None, :] == own_ids[which], d_gates[:, which : which + 1], 0.0)
        for which in range(local_experts)
    )
    d_logits = router_probs * (d_choice - jnp.sum(gates * d_gates, axis=-1, keepdims=True))
    d_small = jnp.concatenate([d_logits, switch_logit], axis=1)
    d_small_high = d_small.astype(jnp.bfloat16)
    d_small_low = (d_small - d_small_high.astype(jnp.float32)).astype(jnp.bfloat16)
    d_small_both = jnp.pad(
        jnp.concatenate([d_small_high, d_small_low], axis=1),
        ((0, 0), (0, 128 - 2 * small_count)),
    )
    small_both = jnp.pad(
        jnp.concatenate([small_weight.T, small_weight.T], axis=0),
        ((0, 128 - 2 * small_count), (0, 0)),
    )
    dh_low = collect(
        places,
        after(d_in, (expert_grads, shared_sums, down_sum, block_sums)).reshape(by_block),
        dh_shared[0],
        members,
        d_small_both,
        small_both,
    )
    small_part = matmul_tn(normed_second, d_small_both)
    small_part = small_part[:, :small_count] + small_part[:, small_count : 2 * small_count]

    d_resid_own, norm2_part, d_attn_out = turnaround(
        dh_low,
        resid_mid,
        rate_second,
        cotangent,
        gain_second[None],
        members,
        2,
    )
    d_context = matmul_nt(d_attn_out, out_weight).astype(jnp.bfloat16)
    d_query_pre, d_key_pre, d_value_pre = attend_back(
        lows,
        starts,
        queries,
        keys_all,
        values_all,
        d_context,
        log_mass,
        cosine,
        sine,
        block,
    )

    dh_first_low, norm1_part, *biases = unproject(
        (d_query_pre, d_key_pre, d_value_pre),
        (query_weight, key_weight, value_weight),
        group_tokens,
        rate_first,
        block,
    )
    norm1_part = norm1_part[0]
    attn_grads = attend_grads(
        after(normed_first, dh_first_low),
        (d_query_pre, d_key_pre, d_value_pre),
        attended,
        d_attn_out,
        math.gcd(width, 512),
    )
    crossed_grads = exchange(after(expert_pieces, d_attn_out).transpose(1, 0, 2, 3))
    line_parts = jnp.concatenate([norm1_part, norm2_part, small_part.T.reshape(-1)])
    stats = jnp.concatenate([line_parts] + [bias[0] for bias in biases]).reshape(-1, 128)
    dh_first_own, stats, mixed_grads = scatter(
        after(dh_first_low, attn_grads),
        jnp.pad(stats, ((0, -stats.shape[0] % 8), (0, 0))),
        crossed_grads,
        line_parts.shape[0] // 128,
        members,
        columns,
        4,
        LONG_COST,
    )
    shared_sums, down_sum, block_low, block_sums = after(
        (shared_sums, down_sum, block_low, block_sums), dh_first_own
    )
    stats = stats.reshape(-1)
    block_out = resid_own + own_rows(block_low).astype(jnp.float32)
    for came in block_sums:
        block_out = block_out + came.astype(jnp.float32)
    block_out = block_out.astype(jnp.bfloat16)
    grad_tokens = norm_back(
        d_resid_own, dh_first_own, tokens_own_wide, own_rows(rate_first), gain_first
    )

    small_sum = stats[2 * width : (2 + small_count) * width].reshape(-1, width)
    bias_end = line_parts.shape[0] + 3 * biases[0].shape[1]
    bias_sums = stats[line_parts.shape[0] : bias_end].reshape(3, -1)

    attn_sums = after(lax.psum(attn_grads, "expert"), dh_first_own)
    expert_sums = [mixed_grads[:, kind] for kind in range(3)]

    return (
        block_out,
        grad_tokens,
        stats[:width],
        attn_sums[0].astype(jnp.float32),
        bias_sums[0],
        attn_sums[1].astype(jnp.float32),
        bias_sums[1],
        attn_sums[2].astype(jnp.float32),
        bias_sums[2],
        attn_sums[3].astype(jnp.float32),
        stats[width : 2 * width],
        small_sum[:experts_count].T,
        small_sum[experts_count],
        shared_sums[0].astype(jnp.float32),
        shared_sums[1].astype(jnp.float32),
        down_sum.astype(jnp.float32),
        expert_sums[0].reshape(1, width // members, -1).astype(jnp.float32),
        expert_sums[1].reshape(1, width // members, -1).astype(jnp.float32),
        turn(expert_sums[2])[None],
    )


def solution(mesh):
    placed = (
        P(("expert", "fsdp"), None),
        P(("expert", "fsdp"), None),
        P("expert", None),
        P(("expert", "fsdp"), None),
        P(),
        P(None, "fsdp"),
        P("fsdp"),
        P(None, "fsdp"),
        P("fsdp"),
        P(None, "fsdp"),
        P("fsdp"),
        P("fsdp", None),
        P(),
        P(),
        P(),
        P(None, "fsdp"),
        P(None, "fsdp"),
        P("fsdp", None),
        P("expert", "fsdp", None),
        P("expert", "fsdp", None),
        P("expert", None, "fsdp"),
    )
    return jax.shard_map(
        shards,
        mesh=mesh,
        in_specs=placed,
        out_specs=(
            P(("expert", "fsdp"), None),
            P(("expert", "fsdp"), None),
            P(),
            P(None, "fsdp"),
            P("fsdp"),
            P(None, "fsdp"),
            P("fsdp"),
            P(None, "fsdp"),
            P("fsdp"),
            P("fsdp", None),
            P(),
            P(),
            P(),
            P(None, "fsdp"),
            P(None, "fsdp"),
            P("fsdp", None),
            P("expert", "fsdp", None),
            P("expert", "fsdp", None),
            P("expert", None, "fsdp"),
        ),
        check_vma=False,
    )
```

```python
import functools
import math

import jax
import jax.numpy as jnp
from jax import lax
from jax.experimental import pallas as pl
from jax.experimental.pallas import tpu as pltpu
from jax.sharding import PartitionSpec as P

HEAD_DIM = 128
TOP = 4


EPSILON = 1e-06
THETA = 1000000.0
MASKED = -1e30
KERNEL_VMEM = 40 * 1024 * 1024
BIG_VMEM = 58 * 1024 * 1024
NO_COST = pl.CostEstimate(flops=0, bytes_accessed=0, transcendentals=0)
LONG_COST = pl.CostEstimate(flops=10**11, bytes_accessed=0, transcendentals=0)


def rms_rate(values):
    return lax.rsqrt(jnp.mean(values * values, axis=-1, keepdims=True) + EPSILON)


def token_layout(lengths, count):
    ends = jnp.cumsum(lengths)
    places = jnp.arange(count, dtype=jnp.int32)
    passed = (places[:, None] >= ends[None, :]).astype(jnp.int32)
    segment = jnp.sum(passed, axis=1)
    start = jnp.sum(passed * lengths[None, :], axis=1)
    return (segment, places - start)


def rotary_tables(positions, width):
    half_width = width // 2
    inverse = THETA ** (-2.0 * jnp.arange(half_width, dtype=jnp.float32) / width)
    angle = positions.astype(jnp.float32)[:, None] * inverse[None, :]
    cosine, sine = jnp.cos(angle), jnp.sin(angle)
    return (
        jnp.concatenate([cosine, cosine], axis=1),
        jnp.concatenate([-sine, sine], axis=1),
    )


def matmul(left_matrix, right_matrix):
    return jnp.dot(left_matrix, right_matrix, preferred_element_type=jnp.float32)


def matmul_tn(left_matrix, right_matrix):
    return lax.dot_general(
        left_matrix, right_matrix, (((0,), (0,)), ((), ())), preferred_element_type=jnp.float32
    )


def matmul_nt(left_matrix, right_matrix):
    return lax.dot_general(
        left_matrix, right_matrix, (((1,), (1,)), ((), ())), preferred_element_type=jnp.float32
    )


def silu_parts(pre_values):
    sigma_values = jax.nn.sigmoid(pre_values)
    return (pre_values * sigma_values, sigma_values * (1.0 + pre_values * (1.0 - sigma_values)))


def norm_back(upstream, dh_values, values, rate, gain):
    gained = dh_values * gain
    return (
        upstream
        + rate * gained
        - values * rate**3 * jnp.mean(gained * values, axis=-1, keepdims=True)
    )


def lane_turn(values):
    return pltpu.roll(values, HEAD_DIM // 2, 1)


def project_body(tokens_ref, gain_ref, weight_refs, bias_refs, cos_ref, sin_ref, outs):
    normed_ref, rate_ref, query_ref, key_ref, value_ref = outs
    wide = tokens_ref[...].astype(jnp.float32)
    rate = rms_rate(wide)
    normed = (wide * rate * gain_ref[...]).astype(jnp.bfloat16)
    normed_ref[...] = normed
    rate_ref[...] = rate
    cosine, sine = cos_ref[...], sin_ref[...]
    for place, out_ref in enumerate((query_ref, key_ref, value_ref)):
        pre = (
            jnp.dot(normed, weight_refs[place][...], preferred_element_type=jnp.float32)
            + bias_refs[place][...]
        )
        if place == 2:
            out_ref[...] = pre.astype(jnp.bfloat16)
            continue
        for head in range(pre.shape[1] // HEAD_DIM):
            part = pre[:, head * HEAD_DIM : (head + 1) * HEAD_DIM]
            turned = part * cosine + lane_turn(part) * sine
            out_ref[:, head * HEAD_DIM : (head + 1) * HEAD_DIM] = turned.astype(jnp.bfloat16)


def project(tokens, gain, weights, biases, cosine, sine, rows):
    count, width = tokens.shape
    features = weights[0].shape[1]

    def body(t, g, w0, w1, w2, b0, b1, b2, c, s, *outs):
        project_body(t, g, (w0, w1, w2), (b0, b1, b2), c, s, outs)

    def by_rows(cols):
        return pl.BlockSpec((rows, cols), lambda i: (i, 0))

    def whole(*shape):
        return pl.BlockSpec(shape, lambda i: (0, 0))

    return pl.pallas_call(
        body,
        grid=(count // rows,),
        in_specs=[by_rows(width), whole(1, width)]
        + [whole(width, features)] * 3
        + [whole(1, features)] * 3
        + [by_rows(HEAD_DIM)] * 2,
        out_specs=[by_rows(width), by_rows(1)] + [by_rows(features)] * 3,
        out_shape=[
            jax.ShapeDtypeStruct((count, width), jnp.bfloat16),
            jax.ShapeDtypeStruct((count, 1), jnp.float32),
        ]
        + [jax.ShapeDtypeStruct((count, features), jnp.bfloat16)] * 3,
        compiler_params=pltpu.CompilerParams(vmem_limit_bytes=KERNEL_VMEM),
        cost_estimate=NO_COST,
        name="project",
    )(tokens, gain, *weights, *biases, cosine, sine)


def scores_of(lows_ref, starts_ref, query, key_ref, wide, block):
    index = pl.program_id(1)
    low = lows_ref[index]
    rows = pl.ds(pl.multiple_of(low * block, block), wide * block)
    keys = key_ref[rows, :]
    scores = lax.dot_general(
        keys, query, (((1,), (1,)), ((), ())), preferred_element_type=jnp.float32
    ) * (1.0 / math.sqrt(HEAD_DIM))
    key_place = low * block + lax.broadcasted_iota(jnp.int32, scores.shape, 0)
    query_place = index * block + lax.broadcasted_iota(jnp.int32, scores.shape, 1)
    allowed = (key_place <= query_place) & (key_place >= starts_ref[...])
    return rows, keys, jnp.where(allowed, scores, MASKED)


def attend_body(lows_ref, starts_ref, query_ref, key_ref, value_ref, out_ref, mass_ref):
    block = query_ref.shape[0]
    index = pl.program_id(1)

    def run(wide):
        rows, _, scores = scores_of(lows_ref, starts_ref, query_ref[...], key_ref, wide, block)
        peak = jnp.max(scores, axis=0, keepdims=True)
        raised = jnp.exp(scores - peak)
        total = jnp.sum(raised, axis=0, keepdims=True)
        soft = (raised * (1.0 / total)).astype(jnp.bfloat16)
        mixed = lax.dot_general(
            value_ref[rows, :], soft, (((0,), (0,)), ((), ())), preferred_element_type=jnp.float32
        )
        out_ref[...] = mixed.T.astype(jnp.bfloat16)
        mass_ref[0] = peak + jnp.log(total)

    for wide in range(1, key_ref.shape[0] // block + 1):
        pl.when(index - lows_ref[index] + 1 == wide)(functools.partial(run, wide))


def attend(lows, starts, queries, keys, values, block):
    count, features = queries.shape
    heads = features // HEAD_DIM
    by_block = pl.BlockSpec((block, HEAD_DIM), lambda h, i, *_: (i, h))
    by_head = pl.BlockSpec((count, HEAD_DIM), lambda h, i, *_: (0, h))
    return pl.pallas_call(
        attend_body,
        grid_spec=pltpu.PrefetchScalarGridSpec(
            num_scalar_prefetch=1,
            grid=(heads, count // block),
            in_specs=[
                pl.BlockSpec((1, block), lambda h, i, *_: (0, i)),
                by_block,
                by_head,
                by_head,
            ],
            out_specs=[by_block, pl.BlockSpec((1, 1, block), lambda h, i, *_: (h, 0, i))],
        ),
        out_shape=[
            jax.ShapeDtypeStruct((count, features), jnp.bfloat16),
            jax.ShapeDtypeStruct((heads, 1, count), jnp.float32),
        ],
        compiler_params=pltpu.CompilerParams(vmem_limit_bytes=KERNEL_VMEM),
        cost_estimate=NO_COST,
        name="attend",
    )(lows, starts, queries, keys, values)


def attend_back_body(
    lows_ref, starts_ref, query_ref, key_ref, value_ref, grad_ref, mass_ref, *rest
):
    cos_ref, sin_ref, d_query_ref, d_key_ref, d_value_ref, key_sum, value_sum = rest
    block = query_ref.shape[0]
    index = pl.program_id(1)
    blocks = key_ref.shape[0] // block
    factor = 1.0 / math.sqrt(HEAD_DIM)

    def rope_back(values, rows):
        return (
            values * cos_ref[rows, :] + lane_turn(values) * -sin_ref[rows, :]
        ).astype(jnp.bfloat16)

    @pl.when(index == 0)
    def _():
        key_sum[...] = jnp.zeros_like(key_sum)
        value_sum[...] = jnp.zeros_like(value_sum)

    def run(wide):
        query, grad = query_ref[...], grad_ref[...]
        rows, keys, scores = scores_of(lows_ref, starts_ref, query, key_ref, wide, block)
        soft = jnp.exp(scores - mass_ref[0])
        d_soft = lax.dot_general(
            value_ref[rows, :], grad, (((1,), (1,)), ((), ())), preferred_element_type=jnp.float32
        )
        inner = jnp.sum(soft * d_soft, axis=0, keepdims=True)
        d_scores = (soft * (d_soft - inner)).astype(jnp.bfloat16)
        value_sum[rows, :] += jnp.dot(
            soft.astype(jnp.bfloat16), grad, preferred_element_type=jnp.float32
        )
        key_sum[rows, :] += jnp.dot(d_scores, query, preferred_element_type=jnp.float32) * factor
        d_query = lax.dot_general(
            keys, d_scores, (((0,), (0,)), ((), ())), preferred_element_type=jnp.float32
        ).T * factor
        here = pl.ds(pl.multiple_of(index * block, block), block)
        d_query_ref[...] = rope_back(d_query, here)

    for wide in range(1, blocks + 1):
        pl.when(index - lows_ref[index] + 1 == wide)(functools.partial(run, wide))

    @pl.when(index == blocks - 1)
    def _():
        d_key_ref[...] = rope_back(key_sum[...], slice(None))
        d_value_ref[...] = value_sum[...].astype(jnp.bfloat16)


def attend_back(lows, starts, queries, keys, values, grads, mass, cosine, sine, block):
    count, features = queries.shape
    heads = features // HEAD_DIM
    by_block = pl.BlockSpec((block, HEAD_DIM), lambda h, i, *_: (i, h))
    by_head = pl.BlockSpec((count, HEAD_DIM), lambda h, i, *_: (0, h))
    whole = pl.BlockSpec((count, HEAD_DIM), lambda h, i, *_: (0, 0))
    return pl.pallas_call(
        attend_back_body,
        grid_spec=pltpu.PrefetchScalarGridSpec(
            num_scalar_prefetch=1,
            grid=(heads, count // block),
            in_specs=[
                pl.BlockSpec((1, block), lambda h, i, *_: (0, i)),
                by_block,
                by_head,
                by_head,
                by_block,
                pl.BlockSpec((1, 1, block), lambda h, i, *_: (h, 0, i)),
                whole,
                whole,
            ],
            out_specs=[by_block, by_head, by_head],
            scratch_shapes=[pltpu.VMEM((count, HEAD_DIM), jnp.float32)] * 2,
        ),
        out_shape=[jax.ShapeDtypeStruct((count, features), jnp.bfloat16)] * 3,
        compiler_params=pltpu.CompilerParams(vmem_limit_bytes=KERNEL_VMEM),
        cost_estimate=NO_COST,
        name="attend_back",
    )(lows, starts, queries, keys, values, grads, mass, cosine, sine)


def settle_body(tokens_ref, attended_ref, weight_ref, gain_ref, small_ref, *outs):
    resid_ref, rate_ref, normed_ref, logit_ref = outs
    total = tokens_ref[...].astype(jnp.float32)
    members, _, features = attended_ref.shape
    for member in range(members):
        total = total + jnp.dot(
            attended_ref[member],
            weight_ref[member * features : (member + 1) * features, :],
            preferred_element_type=jnp.float32,
        )
    rate = rms_rate(total)
    normed = (total * rate * gain_ref[...]).astype(jnp.bfloat16)
    resid_ref[...] = total
    rate_ref[...] = rate
    normed_ref[...] = normed
    logit_ref[...] = jnp.dot(normed, small_ref[...], preferred_element_type=jnp.float32)


def settle(tokens, attended, weight, gain, small, rows):
    count, width = tokens.shape
    members, _, features = attended.shape

    def by_rows(cols):
        return pl.BlockSpec((rows, cols), lambda i: (i, 0))

    def whole(*shape):
        return pl.BlockSpec(shape, lambda i: (0,) * len(shape))

    return pl.pallas_call(
        settle_body,
        grid=(count // rows,),
        in_specs=[
            by_rows(width),
            pl.BlockSpec((members, rows, features), lambda i: (0, i, 0)),
            whole(width, width),
            whole(1, width),
            whole(*small.shape),
        ],
        out_specs=[by_rows(width), by_rows(1), by_rows(width), by_rows(small.shape[1])],
        out_shape=[
            jax.ShapeDtypeStruct((count, width), jnp.float32),
            jax.ShapeDtypeStruct((count, 1), jnp.float32),
            jax.ShapeDtypeStruct((count, width), jnp.bfloat16),
            jax.ShapeDtypeStruct((count, small.shape[1]), jnp.float32),
        ],
        compiler_params=pltpu.CompilerParams(vmem_limit_bytes=KERNEL_VMEM),
        cost_estimate=pl.CostEstimate(
            flops=2 * count * width * width, bytes_accessed=12 * count * width, transcendentals=0
        ),
        name="settle",
    )(tokens, attended, weight, gain, small)


def mixed_places(members, rows):
    for z in range(members):
        for q in range(members):
            yield (z * members + q) * rows, (q * members + z) * rows


def dispatch_body(members, places_ref, source_ref, target_ref):
    slots = target_ref.shape[2]
    quarter = source_ref.shape[1] // members // members
    for which in range(target_ref.shape[0]):
        place = places_ref[0, which : which + 1, :]
        picks = lax.broadcasted_iota(jnp.int32, (slots, place.shape[1]), 0) == place
        picks = picks.astype(jnp.float32).astype(jnp.bfloat16)
        values = jnp.dot(picks, source_ref[...], preferred_element_type=jnp.float32).astype(
            jnp.bfloat16
        )
        for plain, mixed in mixed_places(members, quarter):
            target_ref[which, 0, :, mixed : mixed + quarter] = values[:, plain : plain + quarter]


def dispatch(places, source, slots, members):
    experts, width = places.shape[1], source.shape[1]
    own = source.shape[0] // members
    return pl.pallas_call(
        functools.partial(dispatch_body, members),
        grid=(members,),
        in_specs=[
            pl.BlockSpec((1, experts, own), lambda b: (b, 0, 0)),
            pl.BlockSpec((own, width), lambda b: (b, 0)),
        ],
        out_specs=pl.BlockSpec((experts, 1, slots, width), lambda b: (0, b, 0, 0)),
        out_shape=jax.ShapeDtypeStruct((experts, members, slots, width), jnp.bfloat16),
        compiler_params=pltpu.CompilerParams(vmem_limit_bytes=KERNEL_VMEM),
        cost_estimate=NO_COST,
        name="dispatch",
    )(places, source).reshape(experts, members * slots, width)


def collect_body(members, scaled, places_ref, values_ref, extra_ref, *rest):
    *rest, out_ref = rest
    slots = values_ref.shape[2]
    total = 0.0
    for which in range(values_ref.shape[0]):
        place = places_ref[:, which : which + 1]
        picks = lax.broadcasted_iota(jnp.int32, (place.shape[0], slots), 1) == place
        total = total + jnp.dot(
            picks.astype(jnp.float32).astype(jnp.bfloat16),
            values_ref[which, 0],
            preferred_element_type=jnp.float32,
        )
    extra = extra_ref[...]
    if scaled:
        extra = extra * rest[0][...]
    else:
        extra = extra + jnp.dot(rest[0][...], rest[1][...], preferred_element_type=jnp.float32)
    quarter = extra.shape[1] // members // members
    for plain, mixed in mixed_places(members, quarter):
        out_ref[:, plain : plain + quarter] = (
            extra[:, plain : plain + quarter] + total[:, mixed : mixed + quarter]
        ).astype(out_ref.dtype)


def collect(places, values, extra, members, left, right=None):
    experts, _, slots, width = values.shape
    own = extra.shape[0] // members
    by_block = pl.BlockSpec((own, width), lambda b: (b, 0))
    operands = [places, values, extra]
    in_specs = [
        pl.BlockSpec((own, experts), lambda b: (b, 0)),
        pl.BlockSpec((experts, 1, slots, width), lambda b: (0, b, 0, 0)),
        by_block,
    ]
    operands.append(left)
    in_specs.append(pl.BlockSpec((own, left.shape[1]), lambda b: (b, 0)))
    if right is not None:
        operands.append(right)
        in_specs.append(pl.BlockSpec(right.shape, lambda b: (0, 0)))
    return pl.pallas_call(
        functools.partial(collect_body, members, right is None),
        grid=(members,),
        in_specs=in_specs,
        out_specs=by_block,
        out_shape=jax.ShapeDtypeStruct(extra.shape, jnp.bfloat16),
        compiler_params=pltpu.CompilerParams(vmem_limit_bytes=KERNEL_VMEM),
        cost_estimate=NO_COST,
        name="collect",
    )(*operands)


def expert_specs(experts, count, width, features, rows):
    def by_rows(cols):
        return pl.BlockSpec((1, rows, cols), lambda e, i: (e, i, 0))

    def whole(array):
        return pl.BlockSpec(
            (1,) + array.shape[1:], lambda e, i: (e, 0, 0), pipeline_mode=pl.Buffered(1)
        )

    def out(cols, kind):
        return jax.ShapeDtypeStruct((experts, count, cols), kind)

    return by_rows, whole, out


def expert_body(turned, values_ref, scale_ref, gate_ref, up_ref, down_ref, *outs):
    result_ref, mid_ref, silu_ref, up_slope_ref, *scaled_ref = outs
    values = values_ref[0]
    gate_pre = jnp.dot(values, gate_ref[0], preferred_element_type=jnp.float32)
    up_pre = jnp.dot(values, up_ref[0], preferred_element_type=jnp.float32)
    silu, slope = silu_parts(gate_pre)
    mid = (silu * up_pre).astype(jnp.bfloat16)
    mid_ref[0] = mid
    silu_ref[0] = silu
    up_slope_ref[0] = up_pre * slope
    if turned:
        result = matmul_nt(mid, down_ref[0]).astype(jnp.bfloat16)
        scaled_ref[0][0] = (scale_ref[0] * result.astype(jnp.float32)).astype(jnp.bfloat16)
    else:
        result = matmul(mid, down_ref[0])
    result_ref[0] = result


def expert(values, scales, gate, up, down, turned, rows):
    experts, count, width = values.shape
    features = gate.shape[2]
    by_rows, whole, out = expert_specs(experts, count, width, features, rows)
    low, wide = jnp.bfloat16, jnp.float32
    cols = (width, features, features, features) + (width,) * turned
    kinds = (low if turned else wide, low, wide, wide) + (low,) * turned
    return pl.pallas_call(
        functools.partial(expert_body, turned),
        grid=(experts, count // rows),
        in_specs=[by_rows(width), by_rows(1), whole(gate), whole(up), whole(down)],
        out_specs=[by_rows(c) for c in cols],
        out_shape=[out(c, kind) for c, kind in zip(cols, kinds)],
        compiler_params=pltpu.CompilerParams(vmem_limit_bytes=BIG_VMEM),
        cost_estimate=NO_COST if turned else None,
        name="expert",
    )(values, scales, gate, up, down)


def expert_back_body(turned, grad_ref, result_ref, scale_ref, silu_ref, up_slope_ref, *rest):
    gate_ref, up_ref, down_ref, dot_ref, d_out_ref, d_gate_ref, d_up_ref, d_in_ref = rest
    grad = grad_ref[0].astype(jnp.float32)
    dot_ref[0] = jnp.sum(grad * result_ref[0].astype(jnp.float32), axis=1, keepdims=True)
    d_out = (scale_ref[0] * grad).astype(jnp.bfloat16)
    d_out_ref[0] = d_out
    d_mid = (matmul if turned else matmul_nt)(d_out, down_ref[0])
    d_gate = (d_mid * up_slope_ref[0]).astype(jnp.bfloat16)
    d_up = (d_mid * silu_ref[0]).astype(jnp.bfloat16)
    d_gate_ref[0] = d_gate
    d_up_ref[0] = d_up
    d_in_ref[0] = (matmul_nt(d_gate, gate_ref[0]) + matmul_nt(d_up, up_ref[0])).astype(
        d_in_ref.dtype
    )


def expert_back(grads, results, scales, silu, up_slope, gate, up, down, turned, rows):
    experts, count, width = grads.shape
    features = gate.shape[2]
    by_rows, whole, out = expert_specs(experts, count, width, features, rows)
    low = jnp.bfloat16
    return pl.pallas_call(
        functools.partial(expert_back_body, turned),
        grid=(experts, count // rows),
        in_specs=[by_rows(width), by_rows(width), by_rows(1), by_rows(features), by_rows(features)]
        + [whole(gate), whole(up), whole(down)],
        out_specs=[by_rows(c) for c in (1, width, features, features, width)],
        out_shape=[
            out(1, jnp.float32),
            out(width, low),
            out(features, low),
            out(features, low),
            out(width, results.dtype),
        ],
        compiler_params=pltpu.CompilerParams(vmem_limit_bytes=BIG_VMEM),
        cost_estimate=NO_COST,
        name="expert_back",
    )(grads, results, scales, silu, up_slope, gate, up, down)


def weight_grads_body(rows_ref, d_out_ref, d_gate_ref, d_up_ref, mid_ref, out_ref):
    rows = rows_ref[0].T
    out_ref[0, 0, 0] = matmul(rows, d_gate_ref[0]).astype(jnp.bfloat16)
    out_ref[0, 0, 1] = matmul(rows, d_up_ref[0]).astype(jnp.bfloat16)
    out_ref[0, 0, 2] = matmul(d_out_ref[0].T, mid_ref[0]).astype(jnp.bfloat16)


def weight_grads(rows, d_out, d_gate, d_up, mid, members):
    experts, count, width = rows.shape
    features = mid.shape[2]
    cut = width // members
    by_cols = pl.BlockSpec((1, count, cut), lambda e, i: (e, 0, i))
    whole = pl.BlockSpec((1, count, features), lambda e, i: (e, 0, 0))
    return pl.pallas_call(
        weight_grads_body,
        grid=(experts, members),
        in_specs=[by_cols, by_cols, whole, whole, whole],
        out_specs=pl.BlockSpec((1, 1, 3, cut, features), lambda e, i: (e, i, 0, 0, 0)),
        out_shape=jax.ShapeDtypeStruct((experts, members, 3, cut, features), jnp.bfloat16),
        compiler_params=pltpu.CompilerParams(vmem_limit_bytes=KERNEL_VMEM),
        cost_estimate=NO_COST,
        name="weight_grads",
    )(rows, d_out, d_gate, d_up, mid)


def pair_grads_body(rows_ref, first_ref, second_ref, first_out, second_out):
    rows = rows_ref[...].T
    first_out[...] = matmul(rows, first_ref[...]).astype(jnp.bfloat16)
    second_out[...] = matmul(rows, second_ref[...]).astype(jnp.bfloat16)


def pair_grads(rows, first, second, cut):
    count, width = rows.shape
    features = first.shape[1]
    whole = pl.BlockSpec((count, features), lambda i: (0, 0))
    out = jax.ShapeDtypeStruct((width, features), jnp.bfloat16)
    return pl.pallas_call(
        pair_grads_body,
        grid=(width // cut,),
        in_specs=[pl.BlockSpec((count, cut), lambda i: (0, i)), whole, whole],
        out_specs=[pl.BlockSpec((cut, features), lambda i: (i, 0))] * 2,
        out_shape=[out, out],
        compiler_params=pltpu.CompilerParams(vmem_limit_bytes=KERNEL_VMEM),
        cost_estimate=NO_COST,
        name="pair_grads",
    )(rows, first, second)


MESH = pl.DeviceIdType.MESH


class Line:
    def __init__(self, source, out, send_sems, recv_sems, pieces):
        self.source, self.out = source, out
        self.send_sems, self.recv_sems = send_sems, recv_sems
        self.members, self.rows, self.pieces = out.shape[0], out.shape[1] // pieces, pieces
        self.member = lax.axis_index("fsdp")

    def origin(self, step, way):
        return self.member - step if way == 0 else self.member + step

    def inside(self, place):
        return (place >= 0) & (place < self.members)

    def target(self, way):
        return self.member + 1 if way == 0 else self.member - 1

    def sends(self, step, way):
        return self.inside(self.origin(step - 1, way)) & self.inside(self.target(way))

    def copy(self, origin, step, way, piece, first):
        rows = pl.ds(piece * self.rows, self.rows)
        return pltpu.make_async_remote_copy(
            src_ref=self.source.at[rows] if first else self.out.at[origin, rows],
            dst_ref=self.out.at[origin, rows],
            send_sem=self.send_sems.at[way, step - 1, piece],
            recv_sem=self.recv_sems.at[way, step - 1, piece],
            device_id={"fsdp": self.target(way)},
            device_id_type=MESH,
        )

    def send(self, step, way, piece):
        copy = self.copy(self.origin(step - 1, way), step, way, piece, step == 1)
        pl.when(self.sends(step, way))(copy.start)

    def start(self):
        for piece in range(self.pieces):
            for way in range(2):
                self.send(1, way, piece)

    def hand_on(self, step):
        for piece in range(self.pieces):
            self.hand_on_piece(step, piece)

    def hand_on_piece(self, step, piece):
        for way in range(2):
            origin = self.origin(step, way)
            came = self.copy(origin, step, way, piece, False)
            pl.when(self.inside(origin))(came.wait_recv)
            if step < self.members - 1:
                self.send(step + 1, way, piece)

    def finish(self):
        for step in range(1, self.members):
            for piece in range(self.pieces):
                for way in range(2):
                    copy = self.copy(self.origin(step - 1, way), step, way, piece, step == 1)
                    pl.when(self.sends(step, way))(copy.wait_send)


def arrive_body(members, local_experts, pieces, *refs):
    tokens_ref, routes_ref, *refs = refs
    chunk_refs, refs = refs[:3], refs[3:]
    group_ref, routes_out, *refs = refs
    mixed_refs, crossed_refs, refs = refs[:3], refs[3:6], refs[6:]
    line_send, line_recv, routes_send, routes_recv, mix_send, mix_recv, refs = *refs[:6], refs[6:]
    cross_send, cross_recv, own_sems = refs
    columns = members * local_experts
    column, member = lax.axis_index("expert"), lax.axis_index("fsdp")
    plane, j = column // local_experts, column % local_experts
    rows = chunk_refs[0].shape[0] // members

    barrier = pltpu.get_barrier_semaphore()
    for other in range(1, columns):
        pl.semaphore_signal(
            barrier, inc=1, device_id={"expert": (column + other) % columns}, device_id_type=MESH
        )
    for other in range(1, members):
        pl.semaphore_signal(
            barrier, inc=1, device_id={"fsdp": (member + other) % members}, device_id_type=MESH
        )
    pl.semaphore_wait(barrier, columns + members - 2)

    line = Line(tokens_ref, group_ref, line_send, line_recv, pieces)
    line.start()
    own_copies = [
        pltpu.make_async_copy(tokens_ref, group_ref.at[member], own_sems.at[0]),
        pltpu.make_async_copy(routes_ref, routes_out.at[member], own_sems.at[1]),
    ]
    for copy in own_copies:
        copy.start()

    def mix(turn, kind):
        part = (plane + turn) % members
        target = j * members + part
        source = chunk_refs[kind].at[pl.ds(pl.multiple_of(part * rows, rows), rows)]
        remote = pltpu.make_async_remote_copy(
            src_ref=source,
            dst_ref=mixed_refs[kind].at[plane],
            send_sem=mix_send.at[turn, kind],
            recv_sem=mix_recv.at[turn, kind],
            device_id={"expert": target},
            device_id_type=MESH,
        )
        local = pltpu.make_async_copy(
            source, mixed_refs[kind].at[plane], mix_send.at[turn, kind]
        )
        return target == column, remote, local

    turns = [(turn, kind) for turn in range(members) for kind in range(3)]
    for turn, kind in turns:
        here, remote, local = mix(turn, kind)
        pl.when(here)(local.start)
        pl.when(jnp.logical_not(here))(remote.start)

    def route(other):
        return pltpu.make_async_remote_copy(
            src_ref=routes_ref,
            dst_ref=routes_out.at[member],
            send_sem=routes_send.at[other - 1],
            recv_sem=routes_recv.at[other - 1],
            device_id={"fsdp": (member + other) % members},
            device_id_type=MESH,
        )

    for other in range(1, members):
        route(other).start()
    for step in range(1, members - 1):
        line.hand_on(step)
    for turn, kind in turns:
        here, remote, local = mix(turn, kind)
        pl.when(here)(local.wait)
        pl.when(jnp.logical_not(here))(remote.wait)

    def cross(other, kind):
        target = (member + other) % members
        return pltpu.make_async_remote_copy(
            src_ref=mixed_refs[kind].at[target],
            dst_ref=crossed_refs[kind].at[member],
            send_sem=cross_send.at[other - 1, kind],
            recv_sem=cross_recv.at[other - 1, kind],
            device_id={"fsdp": target},
            device_id_type=MESH,
        )

    for kind in range(3):
        own_copies.append(
            pltpu.make_async_copy(
                mixed_refs[kind].at[member], crossed_refs[kind].at[member], own_sems.at[2 + kind]
            )
        )
        own_copies[-1].start()
        for other in range(1, members):
            cross(other, kind).start()
    line.hand_on(members - 1)
    line.finish()
    for other in range(1, members):
        route(other).wait()
        for kind in range(3):
            cross(other, kind).wait()
    for copy in own_copies:
        copy.wait()


def arrive(tokens, routes, chunks, members, local_experts):
    own, width = tokens.shape
    pieces = 3 if own % 48 == 0 else 1
    rows, cols = chunks[0].shape
    piece = jax.ShapeDtypeStruct((members, rows // members, cols), jnp.bfloat16)
    anywhere = pl.BlockSpec(memory_space=pl.ANY)
    sems = pltpu.SemaphoreType.DMA
    out_shape = [
        jax.ShapeDtypeStruct((members, own, width), jnp.bfloat16),
        jax.ShapeDtypeStruct((members,) + routes.shape, jnp.int32),
    ] + [piece] * 6
    group, group_routes, *rest = pl.pallas_call(
        functools.partial(arrive_body, members, local_experts, pieces),
        in_specs=[anywhere] * 5,
        out_specs=[anywhere] * len(out_shape),
        out_shape=out_shape,
        scratch_shapes=[sems((2, members - 1, pieces))] * 2
        + [sems((members - 1,))] * 2
        + [sems((members, 3))] * 2
        + [sems((members - 1, 3))] * 2
        + [sems((5,))],
        compiler_params=pltpu.CompilerParams(collective_id=0, has_side_effects=True),
        name="arrive",
    )(tokens, routes, *chunks)
    return group.reshape(members * own, width), group_routes, rest[3:]


def greet(members):
    member = lax.axis_index("fsdp")
    barrier = pltpu.get_barrier_semaphore()
    for other in range(1, members):
        pl.semaphore_signal(
            barrier, inc=1, device_id={"fsdp": (member + other) % members}, device_id_type=MESH
        )
    pl.semaphore_wait(barrier, members - 1)


def gather_body(pieces, block_ref, out_ref, send_sems, recv_sems, own_sem):
    members = out_ref.shape[0]
    member = lax.axis_index("fsdp")
    greet(members)
    line = Line(block_ref, out_ref, send_sems, recv_sems, pieces)
    line.start()
    own = pltpu.make_async_copy(block_ref, out_ref.at[member], own_sem)
    own.start()
    for step in range(1, members):
        line.hand_on(step)
    line.finish()
    own.wait()


def gather(block, members, pieces, collective_id):
    sems = pltpu.SemaphoreType.DMA
    return pl.pallas_call(
        functools.partial(gather_body, pieces),
        in_specs=[pl.BlockSpec(memory_space=pl.ANY)],
        out_specs=pl.BlockSpec(memory_space=pl.ANY),
        out_shape=jax.ShapeDtypeStruct((members,) + block.shape, block.dtype),
        scratch_shapes=[sems((2, members - 1, pieces))] * 2 + [sems],
        compiler_params=pltpu.CompilerParams(collective_id=collective_id, has_side_effects=True),
        name="gather",
    )(block)


class Sums:
    def __init__(self, parts, came, send_sems, recv_sems, pieces):
        self.parts, self.came = parts, came
        self.send_sems, self.recv_sems = send_sems, recv_sems
        self.members, self.rows = parts.shape[0], parts.shape[1] // pieces
        self.member = lax.axis_index("fsdp")

    def clear(self):
        for way, end in ((0, 0), (1, self.members - 1)):

            @pl.when(self.member == end)
            def _():
                self.came[way, end] = jnp.zeros_like(self.came[way, end])

    def copy(self, way, block, piece, first):
        here = pl.ds(piece * self.rows, self.rows)
        source = self.parts.at[block, here] if first else self.came.at[way, block, here]
        return pltpu.make_async_remote_copy(
            src_ref=source,
            dst_ref=self.came.at[way, block, here],
            send_sem=self.send_sems.at[way, block, piece],
            recv_sem=self.recv_sems.at[way, block, piece],
            device_id={"fsdp": self.member + 1 if way == 0 else self.member - 1},
            device_id_type=MESH,
        )

    def passes(self, way, block):
        member, last = self.member, self.members - 1
        if way == 0:
            starts = (member == 0) & (block > 0)
            return starts, (member > 0) & (block > member), (member > 0) & (block == member)
        starts = (member == last) & (block < last)
        return starts, (member < last) & (block < member), (member < last) & (block == member)

    def turns(self):
        for turn in range(self.members):
            for way in range(2):
                yield way, self.members - 1 - turn if way == 0 else turn

    def hand_on(self, piece):
        here = pl.ds(piece * self.rows, self.rows)
        for way, block in self.turns():
            starts, hands_on, _ = self.passes(way, block)
            pl.when(starts)(self.copy(way, block, piece, True).start)

            @pl.when(hands_on)
            def _():
                self.copy(way, block, piece, False).wait_recv()
                self.came[way, block, here] = (
                    self.came[way, block, here].astype(jnp.float32)
                    + self.parts[block, here].astype(jnp.float32)
                ).astype(self.came.dtype)
                self.copy(way, block, piece, False).start()

    def total(self, piece):
        for way, block in self.turns():
            pl.when(self.passes(way, block)[2])(self.copy(way, block, piece, False).wait_recv)
        here = pl.ds(piece * self.rows, self.rows)
        return (
            self.parts[self.member, here].astype(jnp.float32)
            + self.came[0, self.member, here].astype(jnp.float32)
            + self.came[1, self.member, here].astype(jnp.float32)
        )

    def finish(self, piece):
        for way, block in self.turns():
            starts, hands_on, _ = self.passes(way, block)
            pl.when(starts)(self.copy(way, block, piece, True).wait_send)
            pl.when(hands_on)(self.copy(way, block, piece, False).wait_send)


def pair_stages(members, columns):
    for size, axis in ((members, "fsdp"), (columns, "expert")):
        for bit in range(size.bit_length() - 1):
            yield axis, 1 << bit


def scatter_body(pieces, columns, line_rows, parts_ref, stats_ref, crossed_ref, *refs):
    out_ref, stats_out, mixed_ref, came, levels, stats_came, send_sems, recv_sems, *refs = refs
    stats_send, stats_recv, mix_send, mix_recv = refs
    members = parts_ref.shape[0]
    stages = list(pair_stages(members, columns))
    member, column = lax.axis_index("fsdp"), lax.axis_index("expert")
    barrier = pltpu.get_barrier_semaphore()
    for other in range(1, members):
        pl.semaphore_signal(
            barrier, inc=1, device_id={"fsdp": (member + other) % members}, device_id_type=MESH
        )
    for other in range(1, columns):
        pl.semaphore_signal(
            barrier, inc=1, device_id={"expert": (column + other) % columns}, device_id_type=MESH
        )
    pl.semaphore_wait(barrier, members + columns - 2)

    def exchange(stage):
        axis, distance = stages[stage]
        place = member if axis == "fsdp" else column
        partner = place + distance - 2 * distance * ((place // distance) % 2)
        return pltpu.make_async_remote_copy(
            src_ref=levels.at[stage],
            dst_ref=stats_came.at[stage],
            send_sem=stats_send.at[stage],
            recv_sem=stats_recv.at[stage],
            device_id={axis: partner},
            device_id_type=MESH,
        )

    def settle_stage(stage):
        exchange(stage).wait_recv()
        value = levels[stage] + stats_came[stage]
        if stages[stage][0] == "fsdp":
            rows = lax.broadcasted_iota(jnp.int32, value.shape, 0)
            value = jnp.where(rows < line_rows, value, levels[stage])
        if stage + 1 < len(stages):
            levels[stage + 1] = value
            exchange(stage + 1).start()
        else:
            stats_out[...] = value

    def mix(turn):
        quarter, j = column % members, column // members
        plane = (quarter - turn + members) % members
        target = plane * (columns // members) + j
        remote = pltpu.make_async_remote_copy(
            src_ref=crossed_ref.at[plane],
            dst_ref=mixed_ref.at[quarter],
            send_sem=mix_send.at[turn],
            recv_sem=mix_recv.at[turn],
            device_id={"expert": target},
            device_id_type=MESH,
        )
        local = pltpu.make_async_copy(
            crossed_ref.at[plane], mixed_ref.at[quarter], mix_send.at[turn]
        )
        return target == column, remote, local

    for turn in range(members):
        here, remote, local = mix(turn)
        pl.when(here)(local.start)
        pl.when(jnp.logical_not(here))(remote.start)
    sums = Sums(parts_ref, came, send_sems, recv_sems, pieces)
    sums.clear()
    levels[0] = stats_ref[...]
    exchange(0).start()
    for piece in range(pieces):
        sums.hand_on(piece)
        if piece < len(stages):
            settle_stage(piece)
    for stage in range(pieces, len(stages)):
        settle_stage(stage)
    for piece in range(pieces):
        out_ref[piece * sums.rows : (piece + 1) * sums.rows, :] = sums.total(piece)
    for piece in range(pieces):
        sums.finish(piece)
    for stage in range(len(stages)):
        exchange(stage).wait_send()
    for turn in range(members):
        here, remote, local = mix(turn)
        pl.when(here)(local.wait)
        pl.when(jnp.logical_not(here))(remote.wait)


def scatter(parts, stats, crossed, line_rows, members, columns, collective_id, cost):
    count, width = parts.shape
    own = count // members
    pieces = 6 if own % 96 == 0 else 1
    stages = len(list(pair_stages(members, columns)))
    sems = pltpu.SemaphoreType.DMA
    in_vmem = pl.BlockSpec(memory_space=pltpu.VMEM)
    anywhere = pl.BlockSpec(memory_space=pl.ANY)
    return pl.pallas_call(
        functools.partial(scatter_body, pieces, columns, line_rows),
        in_specs=[in_vmem, in_vmem, anywhere],
        out_specs=[in_vmem, in_vmem, anywhere],
        out_shape=[
            jax.ShapeDtypeStruct((own, width), jnp.float32),
            jax.ShapeDtypeStruct(stats.shape, jnp.float32),
            jax.ShapeDtypeStruct(crossed.shape, crossed.dtype),
        ],
        scratch_shapes=[
            pltpu.VMEM((2, members, own, width), parts.dtype),
            pltpu.VMEM((stages,) + stats.shape, jnp.float32),
            pltpu.VMEM((stages,) + stats.shape, jnp.float32),
        ]
        + [sems((2, members, pieces))] * 2
        + [sems((stages,))] * 2
        + [sems((members,))] * 2,
        compiler_params=pltpu.CompilerParams(
            collective_id=collective_id, has_side_effects=True, vmem_limit_bytes=KERNEL_VMEM
        ),
        cost_estimate=cost,
        name="scatter",
    )(parts.reshape(members, own, width), stats, crossed)


def turnaround_body(pieces, *refs):
    parts_ref, resid_all, rate_all, grad_ref, gain_ref, d_resid_ref, sum_ref, out_ref, *refs = refs
    came, resid_ref, rate_ref, low, send_sems, recv_sems, line_send, line_recv, own_sems = refs
    members, own_rows = parts_ref.shape[:2]
    greet(members)
    here = pl.ds(pl.multiple_of(lax.axis_index("fsdp") * own_rows, own_rows), own_rows)
    reads = [
        pltpu.make_async_copy(resid_all.at[here], resid_ref, own_sems.at[1]),
        pltpu.make_async_copy(rate_all.at[here], rate_ref, own_sems.at[2]),
    ]
    for read in reads:
        read.start()
    sums = Sums(parts_ref, came, send_sems, recv_sems, pieces)
    sums.clear()
    line = Line(low, out_ref, line_send, line_recv, pieces)
    sum_ref[...] = jnp.zeros_like(sum_ref)
    for read in reads:
        read.wait()
    for phase in range(pieces + members - 1 + 1):
        if phase < pieces:
            sums.hand_on(phase)
        ready = phase - 1
        if 0 <= ready < pieces:
            here = slice(ready * sums.rows, (ready + 1) * sums.rows)
            dh = sums.total(ready)
            resid, rate = resid_ref[here, :], rate_ref[here, :]
            sum_ref[...] += jnp.sum(dh * resid * rate, axis=0, keepdims=True)
            d_resid = norm_back(
                grad_ref[here, :].astype(jnp.float32), dh, resid, rate, gain_ref[...]
            )
            d_resid_ref[here, :] = d_resid
            low[here, :] = d_resid.astype(low.dtype)
            for way in range(2):
                line.send(1, way, ready)
        for step in range(1, members):
            if 0 <= ready - step < pieces:
                line.hand_on_piece(step, ready - step)
    own = pltpu.make_async_copy(low, out_ref.at[line.member], own_sems.at[0])
    own.start()
    line.finish()
    for piece in range(pieces):
        sums.finish(piece)
    own.wait()


def turnaround(parts, resid, rate, grad, gain, members, collective_id):
    count, width = parts.shape
    own = count // members
    pieces = 12 if own % 192 == 0 else 1
    sems = pltpu.SemaphoreType.DMA
    in_vmem = pl.BlockSpec(memory_space=pltpu.VMEM)
    anywhere = pl.BlockSpec(memory_space=pl.ANY)
    d_resid, gain_part, d_attn = pl.pallas_call(
        functools.partial(turnaround_body, pieces),
        in_specs=[in_vmem, anywhere, anywhere, in_vmem, in_vmem],
        out_specs=[in_vmem, in_vmem, anywhere],
        out_shape=[
            jax.ShapeDtypeStruct((own, width), jnp.float32),
            jax.ShapeDtypeStruct((1, width), jnp.float32),
            jax.ShapeDtypeStruct((members, own, width), jnp.bfloat16),
        ],
        scratch_shapes=[
            pltpu.VMEM((2, members, own, width), parts.dtype),
            pltpu.VMEM((own, width), jnp.float32),
            pltpu.VMEM((own, 1), jnp.float32),
            pltpu.VMEM((own, width), jnp.bfloat16),
        ]
        + [sems((2, members, pieces))] * 2
        + [sems((2, members - 1, pieces))] * 2
        + [sems((3,))],
        compiler_params=pltpu.CompilerParams(
            collective_id=collective_id, has_side_effects=True, vmem_limit_bytes=KERNEL_VMEM
        ),
        name="turnaround",
    )(parts.reshape(members, own, width), resid, rate, grad, gain)
    return d_resid, gain_part[0], d_attn.reshape(count, width)


def unproject_body(*refs):
    grad_refs, weight_refs, refs = refs[:3], refs[3:6], refs[6:]
    tokens_ref, rate_ref, out_ref, sum_ref, *bias_refs = refs
    total = 0.0
    for grad_ref, weight_ref in zip(grad_refs, weight_refs):
        total = total + matmul_nt(grad_ref[...], weight_ref[...])
    out_ref[...] = total.astype(jnp.bfloat16)
    part = total * (tokens_ref[...].astype(jnp.float32) * rate_ref[...])

    @pl.when(pl.program_id(0) == 0)
    def _():
        for ref in (sum_ref, *bias_refs):
            ref[...] = jnp.zeros_like(ref)

    sum_ref[...] += jnp.sum(part, axis=0, keepdims=True)
    for grad_ref, bias_ref in zip(grad_refs, bias_refs):
        bias_ref[...] += jnp.sum(grad_ref[...].astype(jnp.float32), axis=0, keepdims=True)


def unproject(grads, weights, tokens, rates, rows):
    count, width = tokens.shape
    features = grads[0].shape[1]

    def by_rows(cols):
        return pl.BlockSpec((rows, cols), lambda i: (i, 0))

    def whole(*shape):
        return pl.BlockSpec(shape, lambda i: (0, 0))

    return pl.pallas_call(
        unproject_body,
        grid=(count // rows,),
        in_specs=[by_rows(features)] * 3
        + [whole(width, features)] * 3
        + [by_rows(width), by_rows(1)],
        out_specs=[by_rows(width), whole(1, width)] + [whole(1, features)] * 3,
        out_shape=[
            jax.ShapeDtypeStruct((count, width), jnp.bfloat16),
            jax.ShapeDtypeStruct((1, width), jnp.float32),
        ]
        + [jax.ShapeDtypeStruct((1, features), jnp.float32)] * 3,
        compiler_params=pltpu.CompilerParams(vmem_limit_bytes=KERNEL_VMEM),
        cost_estimate=NO_COST,
        name="unproject",
    )(*grads, *weights, tokens, rates)


def attend_grads_body(rows_ref, d_query, d_key, d_value, *outs):
    rows = rows_ref[...].T
    for d_ref, out in zip((d_query, d_key, d_value), outs):
        out[...] = matmul(rows, d_ref[...]).astype(jnp.bfloat16)


def attend_grads(rows, d_pres, cut):
    count, width = rows.shape
    features = d_pres[0].shape[1]
    whole = pl.BlockSpec((count, features), lambda i: (0, 0))
    tall = pl.BlockSpec((cut, features), lambda i: (i, 0))
    return pl.pallas_call(
        attend_grads_body,
        grid=(width // cut,),
        in_specs=[pl.BlockSpec((count, cut), lambda i: (0, i))] + [whole] * 3,
        out_specs=[tall] * 3,
        out_shape=[jax.ShapeDtypeStruct((width, features), jnp.bfloat16)] * 3,
        compiler_params=pltpu.CompilerParams(vmem_limit_bytes=KERNEL_VMEM),
        cost_estimate=NO_COST,
        name="attend_grads",
    )(rows, *d_pres)


def turn_body(piece_ref, out_ref):
    out_ref[...] = piece_ref[0].astype(jnp.float32).T


def turn(pieces):
    members, rows, features = pieces.shape
    if rows % 128:
        return pieces.reshape(members * rows, features).astype(jnp.float32).T
    return pl.pallas_call(
        turn_body,
        grid=(members,),
        in_specs=[pl.BlockSpec((1, rows, features), lambda i: (i, 0, 0))],
        out_specs=pl.BlockSpec((features, rows), lambda i: (0, i)),
        out_shape=jax.ShapeDtypeStruct((features, members * rows), jnp.float32),
        compiler_params=pltpu.CompilerParams(vmem_limit_bytes=KERNEL_VMEM),
        name="turn",
    )(pieces)


def shards(
    tokens,
    routes,
    seq_lengths,
    cotangent,
    norm1_gain,
    query_weight,
    query_bias,
    key_weight,
    key_bias,
    value_weight,
    value_bias,
    out_weight,
    norm2_gain,
    router_weight,
    shared_switch,
    shared_gate,
    shared_up,
    shared_down,
    expert_gate,
    expert_up,
    expert_down,
):
    own_count = tokens.shape[0]
    width = tokens.shape[1]
    members = lax.axis_size("fsdp")
    columns = lax.axis_size("expert")
    member = lax.axis_index("fsdp")
    own_start = member * own_count
    count = own_count * members
    experts_count = router_weight.shape[1]
    local_experts = experts_count // members
    capacity = 4 * own_count * TOP // (3 * experts_count)

    def own_rows(values):
        return lax.dynamic_slice_in_dim(values, own_start, own_count, 0)

    def take(pieces, place):
        return lax.dynamic_index_in_dim(pieces, place, 0, keepdims=False)

    def put(pieces, piece, place):
        return lax.dynamic_update_index_in_dim(pieces, piece, place, 0)

    def after(value, other):
        return lax.optimization_barrier((value, other))[0]

    def one_hop(low, high, step):
        upward = [(m, m + 1) for m in range(step - 1, members - 1)]
        downward = [(members - 1 - m, members - 2 - m) for m in range(step - 1, members - 1)]
        return lax.ppermute(low, "fsdp", upward), lax.ppermute(high, "fsdp", downward)

    def line_gather(block, first, ties, last):
        from_low, from_high = [block, first[0]], [block, first[1]]
        for step in range(2, members):
            from_low[-1], from_high[-1] = after(
                (from_low[-1], from_high[-1]), ties[min(step - 2, len(ties) - 1)]
            )
            low, high = one_hop(from_low[-1], from_high[-1], step)
            from_low.append(low)
            from_high.append(high)
        from_low[-1], from_high[-1] = after((from_low[-1], from_high[-1]), last)
        window = jnp.concatenate(from_low[:0:-1] + [block] + from_high[1:], axis=0)
        size = block.shape[0]
        return lax.dynamic_slice_in_dim(window, (members - 1 - member) * size, members * size, 0)

    def relay(parts, step, sums=None):
        blocks = parts.reshape((members, -1) + parts.shape[1:])
        up_block = take(blocks, jnp.minimum(members - step + member, members - 1))
        down_block = take(blocks, jnp.maximum(member - (members - step), 0))
        if sums is not None:
            up_block, down_block = (
                (block.astype(jnp.float32) + came.astype(jnp.float32)).astype(parts.dtype)
                for block, came in zip((up_block, down_block), sums)
            )
        up_pairs = [(m, m + 1) for m in range(step)]
        down_pairs = [(members - 1 - m, members - 2 - m) for m in range(step)]
        return (
            lax.ppermute(up_block, "fsdp", up_pairs),
            lax.ppermute(down_block, "fsdp", down_pairs),
        )

    column = lax.axis_index("expert")

    def weights_whole(piece):
        gathered = lax.all_gather(piece, "expert", axis=0, tiled=False)
        return gathered.reshape(local_experts, width, -1)

    group_tokens, group_routes, crossed = arrive(
        tokens,
        routes.T,
        (expert_gate[0], expert_up[0], expert_down[0].T),
        members,
        local_experts,
    )
    out_piece_rows = out_weight.shape[0] // columns
    out_piece = lax.dynamic_slice_in_dim(out_weight, column * out_piece_rows, out_piece_rows, 0)
    out_full = lax.all_gather(out_piece, ("fsdp", "expert"), axis=0, tiled=True)
    gate_mats, up_mats, down_mats = (weights_whole(piece) for piece in crossed)

    segment, positions = token_layout(seq_lengths[0], count)
    block = math.gcd(count, 256)
    starts = jnp.arange(count, dtype=jnp.int32) - positions
    lows = starts[::block] // block
    starts = starts[None]
    cosine, sine = rotary_tables(positions, HEAD_DIM)
    tokens_own_wide = tokens.astype(jnp.float32)
    gain_first = norm1_gain.astype(jnp.float32)
    normed_first, rate_first, queries, keys_all, values_all = project(
        group_tokens,
        gain_first[None],
        (query_weight, key_weight, value_weight),
        [bias.astype(jnp.float32)[None] for bias in (query_bias, key_bias, value_bias)],
        cosine,
        sine,
        block,
    )
    attended, log_mass = attend(lows, starts, queries, keys_all, values_all, block)
    cot_tied = after(cotangent, group_tokens)
    attended, cot_hop = lax.optimization_barrier((attended, one_hop(cot_tied, cot_tied, 1)))
    attended_by_member = gather(attended, members, math.gcd(count // 16, 4), 1)
    tokens_wide = group_tokens.astype(jnp.float32)
    gain_second = norm2_gain.astype(jnp.float32)
    small_count = experts_count + 1
    small_weight = jnp.concatenate([router_weight, shared_switch[:, None]], axis=1)
    small_wide = jnp.pad(small_weight, ((0, 0), (0, 128 - small_count)))
    resid_mid, rate_second, normed_second, small_pre = settle(
        group_tokens, attended_by_member, out_full, gain_second[None], small_wide, block
    )
    resid_own = own_rows(resid_mid)

    router_probs = jax.nn.softmax(small_pre[:, :experts_count], axis=-1)
    switch_all = jax.nn.sigmoid(small_pre[:, experts_count:small_count])
    own_ids = member * local_experts + jnp.arange(local_experts, dtype=jnp.int32)
    gates = lax.dynamic_slice_in_dim(router_probs, member * local_experts, local_experts, 1)
    hot = jnp.sum(
        (group_routes[:, :, None, :] == own_ids[None, None, :, None]).astype(jnp.float32), axis=1
    )
    order = jnp.arange(own_count, dtype=jnp.int32)
    before = (order[:, None] > order[None, :]).astype(jnp.bfloat16)
    ranks = jnp.einsum(
        "ut,bjt->bju", before, hot.astype(jnp.bfloat16), preferred_element_type=jnp.float32
    ).astype(jnp.int32)
    places_turned = jnp.where(hot > 0.0, ranks, -1)
    places = places_turned.transpose(0, 2, 1)
    slots = jnp.arange(capacity, dtype=jnp.int32)
    picks = places_turned[:, :, None, :] == slots[None, None, :, None]
    gates_turned = gates.reshape(members, own_count, local_experts).transpose(0, 2, 1)
    slot_gates = jnp.sum(jnp.where(picks, gates_turned[:, :, None, :], 0.0), axis=-1)
    slot_gates = slot_gates.transpose(1, 0, 2).reshape(local_experts, members * capacity, 1)
    places = places.reshape(count, local_experts)

    shared_weights = (shared_gate[None], shared_up[None], shared_down[None])
    shared_out, shared_mid, shared_silu, shared_slope = expert(
        normed_second[None], switch_all[None], *shared_weights, False, block
    )
    group_cot = line_gather(
        cotangent, cot_hop, (attended_by_member, normed_second), shared_mid
    )
    row_count = members * capacity
    row_block = math.gcd(row_count, 256)
    rows = dispatch(places_turned, after(normed_second, shared_mid), capacity, members)

    grad_wide = group_cot.astype(jnp.float32)
    down_grad = matmul_tn(shared_mid[0], (switch_all * grad_wide).astype(jnp.bfloat16)).astype(
        jnp.bfloat16
    )
    down_sum = lax.psum(down_grad, "expert")
    switch_dot, _, d_shared_gate, d_shared_up, dh_shared = expert_back(
        after(group_cot, down_grad)[None],
        shared_out,
        switch_all[None],
        shared_silu,
        shared_slope,
        *shared_weights,
        False,
        block,
    )
    switch_logit = switch_dot[0] * switch_all * (1.0 - switch_all)
    shared_grads = tuple(
        pair_grads(normed_second, d_shared_gate[0], d_shared_up[0], math.gcd(width, 512))
    )
    shared_sums = lax.psum(shared_grads, "expert")

    result, expert_mid, expert_silu, expert_slope, scaled = expert(
        after(rows, shared_grads), slot_gates, gate_mats, up_mats, down_mats, True, row_block
    )
    by_block = (local_experts, members, capacity, width)
    block_low = collect(places, scaled.reshape(by_block), shared_out[0], members, switch_all)
    slot_dot, d_rows, d_expert_gate, d_expert_up, d_in = expert_back(
        dispatch(places_turned, after(group_cot, block_low), capacity, members),
        result,
        slot_gates,
        expert_silu,
        expert_slope,
        gate_mats,
        up_mats,
        down_mats,
        True,
        row_block,
    )
    block_sums = relay(block_low, 1)
    expert_grads = weight_grads(
        after(rows, block_sums), d_rows, d_expert_gate, d_expert_up, expert_mid, members
    )
    block_sums = relay(block_low, 2, after(block_sums, d_in))
    slot_dot, block_sums, expert_grads = lax.optimization_barrier(
        (slot_dot, block_sums, expert_grads)
    )
    for step in range(3, members):
        block_sums = relay(block_low, step, block_sums)
    expert_pieces = lax.psum_scatter(
        expert_grads.reshape((columns, 3) + expert_grads.shape[3:]),
        "expert",
        scatter_dimension=0,
        tiled=True,
    ).reshape(3, members, -1, expert_grads.shape[-1])
    slot_dots = slot_dot.reshape(local_experts, members, capacity).transpose(1, 0, 2)
    d_gates = jnp.sum(jnp.where(picks, slot_dots[:, :, :, None], 0.0), axis=2)
    d_gates = d_gates.transpose(0, 2, 1).reshape(count, local_experts)
    ids = jnp.arange(experts_count, dtype=jnp.int32)
    d_choice = sum(
        jnp.where(ids[None, :] == own_ids[which], d_gates[:, which : which + 1], 0.0)
        for which in range(local_experts)
    )
    d_logits = router_probs * (d_choice - jnp.sum(gates * d_gates, axis=-1, keepdims=True))
    d_small = jnp.concatenate([d_logits, switch_logit], axis=1)
    d_small_high = d_small.astype(jnp.bfloat16)
    d_small_low = (d_small - d_small_high.astype(jnp.float32)).astype(jnp.bfloat16)
    d_small_both = jnp.pad(
        jnp.concatenate([d_small_high, d_small_low], axis=1),
        ((0, 0), (0, 128 - 2 * small_count)),
    )
    small_both = jnp.pad(
        jnp.concatenate([small_weight.T, small_weight.T], axis=0),
        ((0, 128 - 2 * small_count), (0, 0)),
    )
    dh_low = collect(
        places,
        after(d_in, (expert_grads, shared_sums, down_sum)).reshape(by_block),
        dh_shared[0],
        members,
        d_small_both,
        small_both,
    )
    small_part = matmul_tn(normed_second, d_small_both)
    small_part = small_part[:, :small_count] + small_part[:, small_count : 2 * small_count]

    d_resid_own, norm2_part, d_attn_out = turnaround(
        dh_low,
        resid_mid,
        rate_second,
        cotangent,
        gain_second[None],
        members,
        2,
    )
    d_attn_out, block_sums = lax.optimization_barrier((d_attn_out, block_sums))
    d_context = matmul_nt(d_attn_out, out_weight).astype(jnp.bfloat16)
    out_sum = lax.psum(matmul_tn(attended, d_attn_out).astype(jnp.bfloat16), "expert")
    d_query_pre, d_key_pre, d_value_pre = attend_back(
        lows,
        starts,
        queries,
        keys_all,
        values_all,
        d_context,
        log_mass,
        cosine,
        sine,
        block,
    )

    expert_pieces = expert_pieces.transpose(1, 0, 2, 3)

    def cross(step, tie):
        return lax.ppermute(
            after(take(expert_pieces, (member + step) % members), tie),
            "fsdp",
            [(m, (m + step) % members) for m in range(members)],
        )

    arrived = [cross(step, d_attn_out) for step in range(1, members - 1)]
    d_query_pre, arrived[0] = lax.optimization_barrier((d_query_pre, arrived[0]))
    attn_grads = attend_grads(
        normed_first, (d_query_pre, d_key_pre, d_value_pre), math.gcd(width, 512)
    )
    attn_grads, out_sum = lax.optimization_barrier((attn_grads, out_sum))
    arrived.append(cross(members - 1, d_query_pre))
    d_pres, arrived[1:-1] = after(
        ((d_query_pre, d_key_pre, d_value_pre), arrived[1:-1]), attn_grads
    )
    dh_first_low, norm1_part, *biases = unproject(
        d_pres, (query_weight, key_weight, value_weight), group_tokens, rate_first, block
    )
    norm1_part = norm1_part[0]
    crossed_grads = expert_pieces
    for step, piece in enumerate(arrived, 1):
        crossed_grads = put(crossed_grads, piece, (member - step) % members)

    shared_sums, down_sum = after((shared_sums, down_sum), dh_first_low)
    shared_out_grads = [
        grad.astype(jnp.float32) for grad in (shared_sums[0], shared_sums[1], down_sum)
    ]
    line_parts = jnp.concatenate([norm1_part, norm2_part, small_part.T.reshape(-1)])
    stats = jnp.concatenate([line_parts] + [bias[0] for bias in biases]).reshape(-1, 128)
    dh_first_own, stats, mixed_grads = scatter(
        after(dh_first_low, (attn_grads, shared_out_grads)),
        jnp.pad(stats, ((0, -stats.shape[0] % 8), (0, 0))),
        crossed_grads,
        line_parts.shape[0] // 128,
        members,
        columns,
        4,
        LONG_COST,
    )
    block_low, block_sums = after((block_low, block_sums), dh_first_own)
    stats = stats.reshape(-1)
    block_out = resid_own + own_rows(block_low).astype(jnp.float32)
    for came in block_sums:
        block_out = block_out + came.astype(jnp.float32)
    block_out = block_out.astype(jnp.bfloat16)
    grad_tokens = norm_back(
        d_resid_own, dh_first_own, tokens_own_wide, own_rows(rate_first), gain_first
    )

    small_sum = stats[2 * width : (2 + small_count) * width].reshape(-1, width)
    bias_end = line_parts.shape[0] + 3 * biases[0].shape[1]
    bias_sums = stats[line_parts.shape[0] : bias_end].reshape(3, -1)

    attn_sums = (*after(lax.psum(attn_grads, "expert"), dh_first_own), after(out_sum, dh_first_own))
    expert_sums = [mixed_grads[:, kind] for kind in range(3)]

    return (
        block_out,
        grad_tokens,
        stats[:width],
        attn_sums[0].astype(jnp.float32),
        bias_sums[0],
        attn_sums[1].astype(jnp.float32),
        bias_sums[1],
        attn_sums[2].astype(jnp.float32),
        bias_sums[2],
        attn_sums[3].astype(jnp.float32),
        stats[width : 2 * width],
        small_sum[:experts_count].T,
        small_sum[experts_count],
        shared_out_grads[0],
        shared_out_grads[1],
        shared_out_grads[2],
        expert_sums[0].reshape(1, width // members, -1).astype(jnp.float32),
        expert_sums[1].reshape(1, width // members, -1).astype(jnp.float32),
        turn(expert_sums[2])[None],
    )


def solution(mesh):
    placed = (
        P(("expert", "fsdp"), None),
        P(("expert", "fsdp"), None),
        P("expert", None),
        P(("expert", "fsdp"), None),
        P(),
        P(None, "fsdp"),
        P("fsdp"),
        P(None, "fsdp"),
        P("fsdp"),
        P(None, "fsdp"),
        P("fsdp"),
        P("fsdp", None),
        P(),
        P(),
        P(),
        P(None, "fsdp"),
        P(None, "fsdp"),
        P("fsdp", None),
        P("expert", "fsdp", None),
        P("expert", "fsdp", None),
        P("expert", None, "fsdp"),
    )
    return jax.shard_map(
        shards,
        mesh=mesh,
        in_specs=placed,
        out_specs=(
            P(("expert", "fsdp"), None),
            P(("expert", "fsdp"), None),
            P(),
            P(None, "fsdp"),
            P("fsdp"),
            P(None, "fsdp"),
            P("fsdp"),
            P(None, "fsdp"),
            P("fsdp"),
            P("fsdp", None),
            P(),
            P(),
            P(),
            P(None, "fsdp"),
            P(None, "fsdp"),
            P("fsdp", None),
            P("expert", "fsdp", None),
            P("expert", "fsdp", None),
            P("expert", None, "fsdp"),
        ),
        check_vma=False,
    )
```

```python
import functools
import math

import jax
import jax.numpy as jnp
from jax import lax
from jax.experimental import pallas as pl
from jax.experimental.pallas import tpu as pltpu
from jax.sharding import PartitionSpec as P

HEAD_DIM = 128
TOP = 4


EPSILON = 1e-06
THETA = 1000000.0
MASKED = -1e30
KERNEL_VMEM = 40 * 1024 * 1024
BIG_VMEM = 58 * 1024 * 1024
NO_COST = pl.CostEstimate(flops=0, bytes_accessed=0, transcendentals=0)
LONG_COST = pl.CostEstimate(flops=10**11, bytes_accessed=0, transcendentals=0)


def rms_rate(values):
    return lax.rsqrt(jnp.mean(values * values, axis=-1, keepdims=True) + EPSILON)


def token_layout(lengths, count):
    ends = jnp.cumsum(lengths)
    places = jnp.arange(count, dtype=jnp.int32)
    passed = (places[:, None] >= ends[None, :]).astype(jnp.int32)
    segment = jnp.sum(passed, axis=1)
    start = jnp.sum(passed * lengths[None, :], axis=1)
    return (segment, places - start)


def rotary_tables(positions, width):
    half_width = width // 2
    inverse = THETA ** (-2.0 * jnp.arange(half_width, dtype=jnp.float32) / width)
    angle = positions.astype(jnp.float32)[:, None] * inverse[None, :]
    cosine, sine = jnp.cos(angle), jnp.sin(angle)
    return (
        jnp.concatenate([cosine, cosine], axis=1),
        jnp.concatenate([-sine, sine], axis=1),
    )


def matmul(left_matrix, right_matrix):
    return jnp.dot(left_matrix, right_matrix, preferred_element_type=jnp.float32)


def matmul_tn(left_matrix, right_matrix):
    return lax.dot_general(
        left_matrix, right_matrix, (((0,), (0,)), ((), ())), preferred_element_type=jnp.float32
    )


def matmul_nt(left_matrix, right_matrix):
    return lax.dot_general(
        left_matrix, right_matrix, (((1,), (1,)), ((), ())), preferred_element_type=jnp.float32
    )


def silu_parts(pre_values):
    sigma_values = jax.nn.sigmoid(pre_values)
    return (pre_values * sigma_values, sigma_values * (1.0 + pre_values * (1.0 - sigma_values)))


def norm_back(upstream, dh_values, values, rate, gain):
    gained = dh_values * gain
    return (
        upstream
        + rate * gained
        - values * rate**3 * jnp.mean(gained * values, axis=-1, keepdims=True)
    )


def lane_turn(values):
    return pltpu.roll(values, HEAD_DIM // 2, 1)


def project_body(tokens_ref, gain_ref, weight_refs, bias_refs, cos_ref, sin_ref, outs):
    normed_ref, rate_ref, query_ref, key_ref, value_ref = outs
    wide = tokens_ref[...].astype(jnp.float32)
    rate = rms_rate(wide)
    normed = (wide * rate * gain_ref[...]).astype(jnp.bfloat16)
    normed_ref[...] = normed
    rate_ref[...] = rate
    cosine, sine = cos_ref[...], sin_ref[...]
    for place, out_ref in enumerate((query_ref, key_ref, value_ref)):
        pre = (
            jnp.dot(normed, weight_refs[place][...], preferred_element_type=jnp.float32)
            + bias_refs[place][...]
        )
        if place == 2:
            out_ref[...] = pre.astype(jnp.bfloat16)
            continue
        for head in range(pre.shape[1] // HEAD_DIM):
            part = pre[:, head * HEAD_DIM : (head + 1) * HEAD_DIM]
            turned = part * cosine + lane_turn(part) * sine
            out_ref[:, head * HEAD_DIM : (head + 1) * HEAD_DIM] = turned.astype(jnp.bfloat16)


def project(tokens, gain, weights, biases, cosine, sine, rows):
    count, width = tokens.shape
    features = weights[0].shape[1]

    def body(t, g, w0, w1, w2, b0, b1, b2, c, s, *outs):
        project_body(t, g, (w0, w1, w2), (b0, b1, b2), c, s, outs)

    def by_rows(cols):
        return pl.BlockSpec((rows, cols), lambda i: (i, 0))

    def whole(*shape):
        return pl.BlockSpec(shape, lambda i: (0, 0))

    return pl.pallas_call(
        body,
        grid=(count // rows,),
        in_specs=[by_rows(width), whole(1, width)]
        + [whole(width, features)] * 3
        + [whole(1, features)] * 3
        + [by_rows(HEAD_DIM)] * 2,
        out_specs=[by_rows(width), by_rows(1)] + [by_rows(features)] * 3,
        out_shape=[
            jax.ShapeDtypeStruct((count, width), jnp.bfloat16),
            jax.ShapeDtypeStruct((count, 1), jnp.float32),
        ]
        + [jax.ShapeDtypeStruct((count, features), jnp.bfloat16)] * 3,
        compiler_params=pltpu.CompilerParams(vmem_limit_bytes=KERNEL_VMEM),
        cost_estimate=NO_COST,
        name="project",
    )(tokens, gain, *weights, *biases, cosine, sine)


def scores_of(lows_ref, starts_ref, query, key_ref, wide, block):
    index = pl.program_id(1)
    low = lows_ref[index]
    rows = pl.ds(pl.multiple_of(low * block, block), wide * block)
    keys = key_ref[rows, :]
    scores = lax.dot_general(
        keys, query, (((1,), (1,)), ((), ())), preferred_element_type=jnp.float32
    ) * (1.0 / math.sqrt(HEAD_DIM))
    key_place = low * block + lax.broadcasted_iota(jnp.int32, scores.shape, 0)
    query_place = index * block + lax.broadcasted_iota(jnp.int32, scores.shape, 1)
    allowed = (key_place <= query_place) & (key_place >= starts_ref[...])
    return rows, keys, jnp.where(allowed, scores, MASKED)


def attend_body(lows_ref, starts_ref, query_ref, key_ref, value_ref, out_ref, mass_ref):
    block = query_ref.shape[0]
    index = pl.program_id(1)

    def run(wide):
        rows, _, scores = scores_of(lows_ref, starts_ref, query_ref[...], key_ref, wide, block)
        peak = jnp.max(scores, axis=0, keepdims=True)
        raised = jnp.exp(scores - peak)
        total = jnp.sum(raised, axis=0, keepdims=True)
        soft = (raised * (1.0 / total)).astype(jnp.bfloat16)
        mixed = lax.dot_general(
            value_ref[rows, :], soft, (((0,), (0,)), ((), ())), preferred_element_type=jnp.float32
        )
        out_ref[...] = mixed.T.astype(jnp.bfloat16)
        mass_ref[0] = peak + jnp.log(total)

    for wide in range(1, key_ref.shape[0] // block + 1):
        pl.when(index - lows_ref[index] + 1 == wide)(functools.partial(run, wide))


def attend(lows, starts, queries, keys, values, block):
    count, features = queries.shape
    heads = features // HEAD_DIM
    by_block = pl.BlockSpec((block, HEAD_DIM), lambda h, i, *_: (i, h))
    by_head = pl.BlockSpec((count, HEAD_DIM), lambda h, i, *_: (0, h))
    return pl.pallas_call(
        attend_body,
        grid_spec=pltpu.PrefetchScalarGridSpec(
            num_scalar_prefetch=1,
            grid=(heads, count // block),
            in_specs=[
                pl.BlockSpec((1, block), lambda h, i, *_: (0, i)),
                by_block,
                by_head,
                by_head,
            ],
            out_specs=[by_block, pl.BlockSpec((1, 1, block), lambda h, i, *_: (h, 0, i))],
        ),
        out_shape=[
            jax.ShapeDtypeStruct((count, features), jnp.bfloat16),
            jax.ShapeDtypeStruct((heads, 1, count), jnp.float32),
        ],
        compiler_params=pltpu.CompilerParams(vmem_limit_bytes=KERNEL_VMEM),
        cost_estimate=NO_COST,
        name="attend",
    )(lows, starts, queries, keys, values)


def attend_back_body(
    lows_ref, starts_ref, query_ref, key_ref, value_ref, grad_ref, mass_ref, *rest
):
    cos_ref, sin_ref, d_query_ref, d_key_ref, d_value_ref, key_sum, value_sum = rest
    block = query_ref.shape[0]
    index = pl.program_id(1)
    blocks = key_ref.shape[0] // block
    factor = 1.0 / math.sqrt(HEAD_DIM)

    def rope_back(values, rows):
        return (
            values * cos_ref[rows, :] + lane_turn(values) * -sin_ref[rows, :]
        ).astype(jnp.bfloat16)

    @pl.when(index == 0)
    def _():
        key_sum[...] = jnp.zeros_like(key_sum)
        value_sum[...] = jnp.zeros_like(value_sum)

    def run(wide):
        query, grad = query_ref[...], grad_ref[...]
        rows, keys, scores = scores_of(lows_ref, starts_ref, query, key_ref, wide, block)
        soft = jnp.exp(scores - mass_ref[0])
        d_soft = lax.dot_general(
            value_ref[rows, :], grad, (((1,), (1,)), ((), ())), preferred_element_type=jnp.float32
        )
        inner = jnp.sum(soft * d_soft, axis=0, keepdims=True)
        d_scores = (soft * (d_soft - inner)).astype(jnp.bfloat16)
        value_sum[rows, :] += jnp.dot(
            soft.astype(jnp.bfloat16), grad, preferred_element_type=jnp.float32
        )
        key_sum[rows, :] += jnp.dot(d_scores, query, preferred_element_type=jnp.float32) * factor
        d_query = lax.dot_general(
            keys, d_scores, (((0,), (0,)), ((), ())), preferred_element_type=jnp.float32
        ).T * factor
        here = pl.ds(pl.multiple_of(index * block, block), block)
        d_query_ref[...] = rope_back(d_query, here)

    for wide in range(1, blocks + 1):
        pl.when(index - lows_ref[index] + 1 == wide)(functools.partial(run, wide))

    @pl.when(index == blocks - 1)
    def _():
        d_key_ref[...] = rope_back(key_sum[...], slice(None))
        d_value_ref[...] = value_sum[...].astype(jnp.bfloat16)


def attend_back(lows, starts, queries, keys, values, grads, mass, cosine, sine, block):
    count, features = queries.shape
    heads = features // HEAD_DIM
    by_block = pl.BlockSpec((block, HEAD_DIM), lambda h, i, *_: (i, h))
    by_head = pl.BlockSpec((count, HEAD_DIM), lambda h, i, *_: (0, h))
    whole = pl.BlockSpec((count, HEAD_DIM), lambda h, i, *_: (0, 0))
    return pl.pallas_call(
        attend_back_body,
        grid_spec=pltpu.PrefetchScalarGridSpec(
            num_scalar_prefetch=1,
            grid=(heads, count // block),
            in_specs=[
                pl.BlockSpec((1, block), lambda h, i, *_: (0, i)),
                by_block,
                by_head,
                by_head,
                by_block,
                pl.BlockSpec((1, 1, block), lambda h, i, *_: (h, 0, i)),
                whole,
                whole,
            ],
            out_specs=[by_block, by_head, by_head],
            scratch_shapes=[pltpu.VMEM((count, HEAD_DIM), jnp.float32)] * 2,
        ),
        out_shape=[jax.ShapeDtypeStruct((count, features), jnp.bfloat16)] * 3,
        compiler_params=pltpu.CompilerParams(vmem_limit_bytes=KERNEL_VMEM),
        cost_estimate=NO_COST,
        name="attend_back",
    )(lows, starts, queries, keys, values, grads, mass, cosine, sine)


def settle_body(tokens_ref, attended_ref, weight_ref, gain_ref, small_ref, *outs):
    resid_ref, rate_ref, normed_ref, logit_ref = outs
    total = tokens_ref[...].astype(jnp.float32)
    members, _, features = attended_ref.shape
    for member in range(members):
        total = total + jnp.dot(
            attended_ref[member],
            weight_ref[member * features : (member + 1) * features, :],
            preferred_element_type=jnp.float32,
        )
    rate = rms_rate(total)
    normed = (total * rate * gain_ref[...]).astype(jnp.bfloat16)
    resid_ref[...] = total
    rate_ref[...] = rate
    normed_ref[...] = normed
    logit_ref[...] = jnp.dot(normed, small_ref[...], preferred_element_type=jnp.float32)


def settle(tokens, attended, weight, gain, small, rows):
    count, width = tokens.shape
    members, _, features = attended.shape

    def by_rows(cols):
        return pl.BlockSpec((rows, cols), lambda i: (i, 0))

    def whole(*shape):
        return pl.BlockSpec(shape, lambda i: (0,) * len(shape))

    return pl.pallas_call(
        settle_body,
        grid=(count // rows,),
        in_specs=[
            by_rows(width),
            pl.BlockSpec((members, rows, features), lambda i: (0, i, 0)),
            whole(width, width),
            whole(1, width),
            whole(*small.shape),
        ],
        out_specs=[by_rows(width), by_rows(1), by_rows(width), by_rows(small.shape[1])],
        out_shape=[
            jax.ShapeDtypeStruct((count, width), jnp.float32),
            jax.ShapeDtypeStruct((count, 1), jnp.float32),
            jax.ShapeDtypeStruct((count, width), jnp.bfloat16),
            jax.ShapeDtypeStruct((count, small.shape[1]), jnp.float32),
        ],
        compiler_params=pltpu.CompilerParams(vmem_limit_bytes=KERNEL_VMEM),
        cost_estimate=pl.CostEstimate(
            flops=2 * count * width * width, bytes_accessed=12 * count * width, transcendentals=0
        ),
        name="settle",
    )(tokens, attended, weight, gain, small)


def mixed_places(members, rows):
    for z in range(members):
        for q in range(members):
            yield (z * members + q) * rows, (q * members + z) * rows


def dispatch_body(members, places_ref, source_ref, target_ref):
    slots = target_ref.shape[2]
    quarter = source_ref.shape[1] // members // members
    for which in range(target_ref.shape[0]):
        place = places_ref[0, which : which + 1, :]
        picks = lax.broadcasted_iota(jnp.int32, (slots, place.shape[1]), 0) == place
        picks = picks.astype(jnp.float32).astype(jnp.bfloat16)
        values = jnp.dot(picks, source_ref[...], preferred_element_type=jnp.float32).astype(
            jnp.bfloat16
        )
        for plain, mixed in mixed_places(members, quarter):
            target_ref[which, 0, :, mixed : mixed + quarter] = values[:, plain : plain + quarter]


def dispatch(places, source, slots, members):
    experts, width = places.shape[1], source.shape[1]
    own = source.shape[0] // members
    return pl.pallas_call(
        functools.partial(dispatch_body, members),
        grid=(members,),
        in_specs=[
            pl.BlockSpec((1, experts, own), lambda b: (b, 0, 0)),
            pl.BlockSpec((own, width), lambda b: (b, 0)),
        ],
        out_specs=pl.BlockSpec((experts, 1, slots, width), lambda b: (0, b, 0, 0)),
        out_shape=jax.ShapeDtypeStruct((experts, members, slots, width), jnp.bfloat16),
        compiler_params=pltpu.CompilerParams(vmem_limit_bytes=KERNEL_VMEM),
        cost_estimate=NO_COST,
        name="dispatch",
    )(places, source).reshape(experts, members * slots, width)


def collect_body(members, scaled, places_ref, values_ref, extra_ref, *rest):
    *rest, out_ref = rest
    slots = values_ref.shape[2]
    total = 0.0
    for which in range(values_ref.shape[0]):
        place = places_ref[:, which : which + 1]
        picks = lax.broadcasted_iota(jnp.int32, (place.shape[0], slots), 1) == place
        total = total + jnp.dot(
            picks.astype(jnp.float32).astype(jnp.bfloat16),
            values_ref[which, 0],
            preferred_element_type=jnp.float32,
        )
    extra = extra_ref[...]
    if scaled:
        extra = extra * rest[0][...]
    else:
        extra = extra + jnp.dot(rest[0][...], rest[1][...], preferred_element_type=jnp.float32)
    quarter = extra.shape[1] // members // members
    for plain, mixed in mixed_places(members, quarter):
        out_ref[:, plain : plain + quarter] = (
            extra[:, plain : plain + quarter] + total[:, mixed : mixed + quarter]
        ).astype(out_ref.dtype)


def collect(places, values, extra, members, left, right=None):
    experts, _, slots, width = values.shape
    own = extra.shape[0] // members
    by_block = pl.BlockSpec((own, width), lambda b: (b, 0))
    operands = [places, values, extra]
    in_specs = [
        pl.BlockSpec((own, experts), lambda b: (b, 0)),
        pl.BlockSpec((experts, 1, slots, width), lambda b: (0, b, 0, 0)),
        by_block,
    ]
    operands.append(left)
    in_specs.append(pl.BlockSpec((own, left.shape[1]), lambda b: (b, 0)))
    if right is not None:
        operands.append(right)
        in_specs.append(pl.BlockSpec(right.shape, lambda b: (0, 0)))
    return pl.pallas_call(
        functools.partial(collect_body, members, right is None),
        grid=(members,),
        in_specs=in_specs,
        out_specs=by_block,
        out_shape=jax.ShapeDtypeStruct(extra.shape, jnp.bfloat16),
        compiler_params=pltpu.CompilerParams(vmem_limit_bytes=KERNEL_VMEM),
        cost_estimate=NO_COST,
        name="collect",
    )(*operands)


def expert_specs(experts, count, width, features, rows):
    def by_rows(cols):
        return pl.BlockSpec((1, rows, cols), lambda e, i: (e, i, 0))

    def whole(array):
        return pl.BlockSpec(
            (1,) + array.shape[1:], lambda e, i: (e, 0, 0), pipeline_mode=pl.Buffered(1)
        )

    def out(cols, kind):
        return jax.ShapeDtypeStruct((experts, count, cols), kind)

    return by_rows, whole, out


def expert_body(turned, values_ref, scale_ref, gate_ref, up_ref, down_ref, *outs):
    result_ref, mid_ref, silu_ref, up_slope_ref, *scaled_ref = outs
    values = values_ref[0]
    gate_pre = jnp.dot(values, gate_ref[0], preferred_element_type=jnp.float32)
    up_pre = jnp.dot(values, up_ref[0], preferred_element_type=jnp.float32)
    silu, slope = silu_parts(gate_pre)
    mid = (silu * up_pre).astype(jnp.bfloat16)
    mid_ref[0] = mid
    silu_ref[0] = silu
    up_slope_ref[0] = up_pre * slope
    if turned:
        result = matmul_nt(mid, down_ref[0]).astype(jnp.bfloat16)
        scaled_ref[0][0] = (scale_ref[0] * result.astype(jnp.float32)).astype(jnp.bfloat16)
    else:
        result = matmul(mid, down_ref[0])
    result_ref[0] = result


def expert(values, scales, gate, up, down, turned, rows):
    experts, count, width = values.shape
    features = gate.shape[2]
    by_rows, whole, out = expert_specs(experts, count, width, features, rows)
    low, wide = jnp.bfloat16, jnp.float32
    cols = (width, features, features, features) + (width,) * turned
    kinds = (low if turned else wide, low, wide, wide) + (low,) * turned
    return pl.pallas_call(
        functools.partial(expert_body, turned),
        grid=(experts, count // rows),
        in_specs=[by_rows(width), by_rows(1), whole(gate), whole(up), whole(down)],
        out_specs=[by_rows(c) for c in cols],
        out_shape=[out(c, kind) for c, kind in zip(cols, kinds)],
        compiler_params=pltpu.CompilerParams(vmem_limit_bytes=BIG_VMEM),
        cost_estimate=NO_COST if turned else None,
        name="expert",
    )(values, scales, gate, up, down)


def expert_back_body(turned, grad_ref, result_ref, scale_ref, silu_ref, up_slope_ref, *rest):
    gate_ref, up_ref, down_ref, dot_ref, d_out_ref, d_gate_ref, d_up_ref, d_in_ref = rest
    grad = grad_ref[0].astype(jnp.float32)
    dot_ref[0] = jnp.sum(grad * result_ref[0].astype(jnp.float32), axis=1, keepdims=True)
    d_out = (scale_ref[0] * grad).astype(jnp.bfloat16)
    d_out_ref[0] = d_out
    d_mid = (matmul if turned else matmul_nt)(d_out, down_ref[0])
    d_gate = (d_mid * up_slope_ref[0]).astype(jnp.bfloat16)
    d_up = (d_mid * silu_ref[0]).astype(jnp.bfloat16)
    d_gate_ref[0] = d_gate
    d_up_ref[0] = d_up
    d_in_ref[0] = (matmul_nt(d_gate, gate_ref[0]) + matmul_nt(d_up, up_ref[0])).astype(
        d_in_ref.dtype
    )


def expert_back(grads, results, scales, silu, up_slope, gate, up, down, turned, rows):
    experts, count, width = grads.shape
    features = gate.shape[2]
    by_rows, whole, out = expert_specs(experts, count, width, features, rows)
    low = jnp.bfloat16
    return pl.pallas_call(
        functools.partial(expert_back_body, turned),
        grid=(experts, count // rows),
        in_specs=[by_rows(width), by_rows(width), by_rows(1), by_rows(features), by_rows(features)]
        + [whole(gate), whole(up), whole(down)],
        out_specs=[by_rows(c) for c in (1, width, features, features, width)],
        out_shape=[
            out(1, jnp.float32),
            out(width, low),
            out(features, low),
            out(features, low),
            out(width, results.dtype),
        ],
        compiler_params=pltpu.CompilerParams(vmem_limit_bytes=BIG_VMEM),
        cost_estimate=NO_COST,
        name="expert_back",
    )(grads, results, scales, silu, up_slope, gate, up, down)


def weight_grads_body(rows_ref, d_out_ref, d_gate_ref, d_up_ref, mid_ref, out_ref):
    rows = rows_ref[0].T
    out_ref[0, 0, 0] = matmul(rows, d_gate_ref[0]).astype(jnp.bfloat16)
    out_ref[0, 0, 1] = matmul(rows, d_up_ref[0]).astype(jnp.bfloat16)
    out_ref[0, 0, 2] = matmul(d_out_ref[0].T, mid_ref[0]).astype(jnp.bfloat16)


def weight_grads(rows, d_out, d_gate, d_up, mid, members):
    experts, count, width = rows.shape
    features = mid.shape[2]
    cut = width // members
    by_cols = pl.BlockSpec((1, count, cut), lambda e, i: (e, 0, i))
    whole = pl.BlockSpec((1, count, features), lambda e, i: (e, 0, 0))
    return pl.pallas_call(
        weight_grads_body,
        grid=(experts, members),
        in_specs=[by_cols, by_cols, whole, whole, whole],
        out_specs=pl.BlockSpec((1, 1, 3, cut, features), lambda e, i: (e, i, 0, 0, 0)),
        out_shape=jax.ShapeDtypeStruct((experts, members, 3, cut, features), jnp.bfloat16),
        compiler_params=pltpu.CompilerParams(vmem_limit_bytes=KERNEL_VMEM),
        cost_estimate=NO_COST,
        name="weight_grads",
    )(rows, d_out, d_gate, d_up, mid)


def pair_grads_body(rows_ref, first_ref, second_ref, first_out, second_out):
    rows = rows_ref[...].T
    first_out[...] = matmul(rows, first_ref[...]).astype(jnp.bfloat16)
    second_out[...] = matmul(rows, second_ref[...]).astype(jnp.bfloat16)


def pair_grads(rows, first, second, cut):
    count, width = rows.shape
    features = first.shape[1]
    whole = pl.BlockSpec((count, features), lambda i: (0, 0))
    out = jax.ShapeDtypeStruct((width, features), jnp.bfloat16)
    return pl.pallas_call(
        pair_grads_body,
        grid=(width // cut,),
        in_specs=[pl.BlockSpec((count, cut), lambda i: (0, i)), whole, whole],
        out_specs=[pl.BlockSpec((cut, features), lambda i: (i, 0))] * 2,
        out_shape=[out, out],
        compiler_params=pltpu.CompilerParams(vmem_limit_bytes=KERNEL_VMEM),
        cost_estimate=NO_COST,
        name="pair_grads",
    )(rows, first, second)


MESH = pl.DeviceIdType.MESH


class Line:
    def __init__(self, source, out, send_sems, recv_sems, pieces):
        self.source, self.out = source, out
        self.send_sems, self.recv_sems = send_sems, recv_sems
        self.members, self.rows, self.pieces = out.shape[0], out.shape[1] // pieces, pieces
        self.member = lax.axis_index("fsdp")

    def origin(self, step, way):
        return self.member - step if way == 0 else self.member + step

    def inside(self, place):
        return (place >= 0) & (place < self.members)

    def target(self, way):
        return self.member + 1 if way == 0 else self.member - 1

    def sends(self, step, way):
        return self.inside(self.origin(step - 1, way)) & self.inside(self.target(way))

    def copy(self, origin, step, way, piece, first):
        rows = pl.ds(piece * self.rows, self.rows)
        return pltpu.make_async_remote_copy(
            src_ref=self.source.at[rows] if first else self.out.at[origin, rows],
            dst_ref=self.out.at[origin, rows],
            send_sem=self.send_sems.at[way, step - 1, piece],
            recv_sem=self.recv_sems.at[way, step - 1, piece],
            device_id={"fsdp": self.target(way)},
            device_id_type=MESH,
        )

    def send(self, step, way, piece):
        copy = self.copy(self.origin(step - 1, way), step, way, piece, step == 1)
        pl.when(self.sends(step, way))(copy.start)

    def start(self):
        for piece in range(self.pieces):
            for way in range(2):
                self.send(1, way, piece)

    def hand_on(self, step):
        for piece in range(self.pieces):
            self.hand_on_piece(step, piece)

    def hand_on_piece(self, step, piece):
        for way in range(2):
            origin = self.origin(step, way)
            came = self.copy(origin, step, way, piece, False)
            pl.when(self.inside(origin))(came.wait_recv)
            if step < self.members - 1:
                self.send(step + 1, way, piece)

    def finish(self):
        for step in range(1, self.members):
            for piece in range(self.pieces):
                for way in range(2):
                    copy = self.copy(self.origin(step - 1, way), step, way, piece, step == 1)
                    pl.when(self.sends(step, way))(copy.wait_send)


def arrive_body(members, local_experts, pieces, *refs):
    tokens_ref, routes_ref, *refs = refs
    chunk_refs, refs = refs[:3], refs[3:]
    group_ref, routes_out, *refs = refs
    mixed_refs, crossed_refs, refs = refs[:3], refs[3:6], refs[6:]
    line_send, line_recv, routes_send, routes_recv, mix_send, mix_recv, refs = *refs[:6], refs[6:]
    cross_send, cross_recv, own_sems = refs
    columns = members * local_experts
    column, member = lax.axis_index("expert"), lax.axis_index("fsdp")
    plane, j = column // local_experts, column % local_experts
    rows = chunk_refs[0].shape[0] // members

    barrier = pltpu.get_barrier_semaphore()
    for other in range(1, columns):
        pl.semaphore_signal(
            barrier, inc=1, device_id={"expert": (column + other) % columns}, device_id_type=MESH
        )
    for other in range(1, members):
        pl.semaphore_signal(
            barrier, inc=1, device_id={"fsdp": (member + other) % members}, device_id_type=MESH
        )
    pl.semaphore_wait(barrier, columns + members - 2)

    line = Line(tokens_ref, group_ref, line_send, line_recv, pieces)
    line.start()
    own_copies = [
        pltpu.make_async_copy(tokens_ref, group_ref.at[member], own_sems.at[0]),
        pltpu.make_async_copy(routes_ref, routes_out.at[member], own_sems.at[1]),
    ]
    for copy in own_copies:
        copy.start()

    def mix(turn, kind):
        part = (plane + turn) % members
        target = j * members + part
        source = chunk_refs[kind].at[pl.ds(pl.multiple_of(part * rows, rows), rows)]
        remote = pltpu.make_async_remote_copy(
            src_ref=source,
            dst_ref=mixed_refs[kind].at[plane],
            send_sem=mix_send.at[turn, kind],
            recv_sem=mix_recv.at[turn, kind],
            device_id={"expert": target},
            device_id_type=MESH,
        )
        local = pltpu.make_async_copy(
            source, mixed_refs[kind].at[plane], mix_send.at[turn, kind]
        )
        return target == column, remote, local

    turns = [(turn, kind) for turn in range(members) for kind in range(3)]
    for turn, kind in turns:
        here, remote, local = mix(turn, kind)
        pl.when(here)(local.start)
        pl.when(jnp.logical_not(here))(remote.start)

    def route(other):
        return pltpu.make_async_remote_copy(
            src_ref=routes_ref,
            dst_ref=routes_out.at[member],
            send_sem=routes_send.at[other - 1],
            recv_sem=routes_recv.at[other - 1],
            device_id={"fsdp": (member + other) % members},
            device_id_type=MESH,
        )

    for other in range(1, members):
        route(other).start()
    for step in range(1, members - 1):
        line.hand_on(step)
    for turn, kind in turns:
        here, remote, local = mix(turn, kind)
        pl.when(here)(local.wait)
        pl.when(jnp.logical_not(here))(remote.wait)

    def cross(other, kind):
        target = (member + other) % members
        return pltpu.make_async_remote_copy(
            src_ref=mixed_refs[kind].at[target],
            dst_ref=crossed_refs[kind].at[member],
            send_sem=cross_send.at[other - 1, kind],
            recv_sem=cross_recv.at[other - 1, kind],
            device_id={"fsdp": target},
            device_id_type=MESH,
        )

    for kind in range(3):
        own_copies.append(
            pltpu.make_async_copy(
                mixed_refs[kind].at[member], crossed_refs[kind].at[member], own_sems.at[2 + kind]
            )
        )
        own_copies[-1].start()
        for other in range(1, members):
            cross(other, kind).start()
    line.hand_on(members - 1)
    line.finish()
    for other in range(1, members):
        route(other).wait()
        for kind in range(3):
            cross(other, kind).wait()
    for copy in own_copies:
        copy.wait()


def arrive(tokens, routes, chunks, members, local_experts):
    own, width = tokens.shape
    pieces = 3 if own % 48 == 0 else 1
    rows, cols = chunks[0].shape
    piece = jax.ShapeDtypeStruct((members, rows // members, cols), jnp.bfloat16)
    anywhere = pl.BlockSpec(memory_space=pl.ANY)
    sems = pltpu.SemaphoreType.DMA
    out_shape = [
        jax.ShapeDtypeStruct((members, own, width), jnp.bfloat16),
        jax.ShapeDtypeStruct((members,) + routes.shape, jnp.int32),
    ] + [piece] * 6
    group, group_routes, *rest = pl.pallas_call(
        functools.partial(arrive_body, members, local_experts, pieces),
        in_specs=[anywhere] * 5,
        out_specs=[anywhere] * len(out_shape),
        out_shape=out_shape,
        scratch_shapes=[sems((2, members - 1, pieces))] * 2
        + [sems((members - 1,))] * 2
        + [sems((members, 3))] * 2
        + [sems((members - 1, 3))] * 2
        + [sems((5,))],
        compiler_params=pltpu.CompilerParams(collective_id=0, has_side_effects=True),
        name="arrive",
    )(tokens, routes, *chunks)
    return group.reshape(members * own, width), group_routes, rest[3:]


def greet(members):
    member = lax.axis_index("fsdp")
    barrier = pltpu.get_barrier_semaphore()
    for other in range(1, members):
        pl.semaphore_signal(
            barrier, inc=1, device_id={"fsdp": (member + other) % members}, device_id_type=MESH
        )
    pl.semaphore_wait(barrier, members - 1)


def gather_body(pieces, block_ref, out_ref, send_sems, recv_sems, own_sem):
    members = out_ref.shape[0]
    member = lax.axis_index("fsdp")
    greet(members)
    line = Line(block_ref, out_ref, send_sems, recv_sems, pieces)
    line.start()
    own = pltpu.make_async_copy(block_ref, out_ref.at[member], own_sem)
    own.start()
    for step in range(1, members):
        line.hand_on(step)
    line.finish()
    own.wait()


def gather(block, members, pieces, collective_id):
    sems = pltpu.SemaphoreType.DMA
    return pl.pallas_call(
        functools.partial(gather_body, pieces),
        in_specs=[pl.BlockSpec(memory_space=pl.ANY)],
        out_specs=pl.BlockSpec(memory_space=pl.ANY),
        out_shape=jax.ShapeDtypeStruct((members,) + block.shape, block.dtype),
        scratch_shapes=[sems((2, members - 1, pieces))] * 2 + [sems],
        compiler_params=pltpu.CompilerParams(collective_id=collective_id, has_side_effects=True),
        name="gather",
    )(block)


class Sums:
    def __init__(self, parts, came, send_sems, recv_sems, pieces):
        self.parts, self.came = parts, came
        self.send_sems, self.recv_sems = send_sems, recv_sems
        self.members, self.rows = parts.shape[0], parts.shape[1] // pieces
        self.member = lax.axis_index("fsdp")

    def clear(self):
        for way, end in ((0, 0), (1, self.members - 1)):

            @pl.when(self.member == end)
            def _():
                self.came[way, end] = jnp.zeros_like(self.came[way, end])

    def copy(self, way, block, piece, first):
        here = pl.ds(piece * self.rows, self.rows)
        source = self.parts.at[block, here] if first else self.came.at[way, block, here]
        return pltpu.make_async_remote_copy(
            src_ref=source,
            dst_ref=self.came.at[way, block, here],
            send_sem=self.send_sems.at[way, block, piece],
            recv_sem=self.recv_sems.at[way, block, piece],
            device_id={"fsdp": self.member + 1 if way == 0 else self.member - 1},
            device_id_type=MESH,
        )

    def passes(self, way, block):
        member, last = self.member, self.members - 1
        if way == 0:
            starts = (member == 0) & (block > 0)
            return starts, (member > 0) & (block > member), (member > 0) & (block == member)
        starts = (member == last) & (block < last)
        return starts, (member < last) & (block < member), (member < last) & (block == member)

    def turns(self):
        for turn in range(self.members):
            for way in range(2):
                yield way, self.members - 1 - turn if way == 0 else turn

    def hand_on(self, piece):
        here = pl.ds(piece * self.rows, self.rows)
        for way, block in self.turns():
            starts, hands_on, _ = self.passes(way, block)
            pl.when(starts)(self.copy(way, block, piece, True).start)

            @pl.when(hands_on)
            def _():
                self.copy(way, block, piece, False).wait_recv()
                self.came[way, block, here] = (
                    self.came[way, block, here].astype(jnp.float32)
                    + self.parts[block, here].astype(jnp.float32)
                ).astype(self.came.dtype)
                self.copy(way, block, piece, False).start()

    def total(self, piece):
        for way, block in self.turns():
            pl.when(self.passes(way, block)[2])(self.copy(way, block, piece, False).wait_recv)
        here = pl.ds(piece * self.rows, self.rows)
        return (
            self.parts[self.member, here].astype(jnp.float32)
            + self.came[0, self.member, here].astype(jnp.float32)
            + self.came[1, self.member, here].astype(jnp.float32)
        )

    def finish(self, piece):
        for way, block in self.turns():
            starts, hands_on, _ = self.passes(way, block)
            pl.when(starts)(self.copy(way, block, piece, True).wait_send)
            pl.when(hands_on)(self.copy(way, block, piece, False).wait_send)


def pair_stages(members, columns):
    for size, axis in ((members, "fsdp"), (columns, "expert")):
        for bit in range(size.bit_length() - 1):
            yield axis, 1 << bit


def scatter_body(pieces, columns, line_rows, parts_ref, stats_ref, crossed_ref, *refs):
    out_ref, stats_out, mixed_ref, came, levels, stats_came, send_sems, recv_sems, *refs = refs
    stats_send, stats_recv, mix_send, mix_recv = refs
    members = parts_ref.shape[0]
    stages = list(pair_stages(members, columns))
    member, column = lax.axis_index("fsdp"), lax.axis_index("expert")
    barrier = pltpu.get_barrier_semaphore()
    for other in range(1, members):
        pl.semaphore_signal(
            barrier, inc=1, device_id={"fsdp": (member + other) % members}, device_id_type=MESH
        )
    for other in range(1, columns):
        pl.semaphore_signal(
            barrier, inc=1, device_id={"expert": (column + other) % columns}, device_id_type=MESH
        )
    pl.semaphore_wait(barrier, members + columns - 2)

    def exchange(stage):
        axis, distance = stages[stage]
        place = member if axis == "fsdp" else column
        partner = place + distance - 2 * distance * ((place // distance) % 2)
        return pltpu.make_async_remote_copy(
            src_ref=levels.at[stage],
            dst_ref=stats_came.at[stage],
            send_sem=stats_send.at[stage],
            recv_sem=stats_recv.at[stage],
            device_id={axis: partner},
            device_id_type=MESH,
        )

    def settle_stage(stage):
        exchange(stage).wait_recv()
        value = levels[stage] + stats_came[stage]
        if stages[stage][0] == "fsdp":
            rows = lax.broadcasted_iota(jnp.int32, value.shape, 0)
            value = jnp.where(rows < line_rows, value, levels[stage])
        if stage + 1 < len(stages):
            levels[stage + 1] = value
            exchange(stage + 1).start()
        else:
            stats_out[...] = value

    def mix(turn):
        quarter, j = column % members, column // members
        plane = (quarter - turn + members) % members
        target = plane * (columns // members) + j
        remote = pltpu.make_async_remote_copy(
            src_ref=crossed_ref.at[plane],
            dst_ref=mixed_ref.at[quarter],
            send_sem=mix_send.at[turn],
            recv_sem=mix_recv.at[turn],
            device_id={"expert": target},
            device_id_type=MESH,
        )
        local = pltpu.make_async_copy(
            crossed_ref.at[plane], mixed_ref.at[quarter], mix_send.at[turn]
        )
        return target == column, remote, local

    for turn in range(members):
        here, remote, local = mix(turn)
        pl.when(here)(local.start)
        pl.when(jnp.logical_not(here))(remote.start)
    sums = Sums(parts_ref, came, send_sems, recv_sems, pieces)
    sums.clear()
    levels[0] = stats_ref[...]
    exchange(0).start()
    for piece in range(pieces):
        sums.hand_on(piece)
        if piece < len(stages):
            settle_stage(piece)
    for stage in range(pieces, len(stages)):
        settle_stage(stage)
    for piece in range(pieces):
        out_ref[piece * sums.rows : (piece + 1) * sums.rows, :] = sums.total(piece)
    for piece in range(pieces):
        sums.finish(piece)
    for stage in range(len(stages)):
        exchange(stage).wait_send()
    for turn in range(members):
        here, remote, local = mix(turn)
        pl.when(here)(local.wait)
        pl.when(jnp.logical_not(here))(remote.wait)


def scatter(parts, stats, crossed, line_rows, members, columns, collective_id, cost):
    count, width = parts.shape
    own = count // members
    pieces = 6 if own % 96 == 0 else 1
    stages = len(list(pair_stages(members, columns)))
    sems = pltpu.SemaphoreType.DMA
    in_vmem = pl.BlockSpec(memory_space=pltpu.VMEM)
    anywhere = pl.BlockSpec(memory_space=pl.ANY)
    return pl.pallas_call(
        functools.partial(scatter_body, pieces, columns, line_rows),
        in_specs=[in_vmem, in_vmem, anywhere],
        out_specs=[in_vmem, in_vmem, anywhere],
        out_shape=[
            jax.ShapeDtypeStruct((own, width), jnp.float32),
            jax.ShapeDtypeStruct(stats.shape, jnp.float32),
            jax.ShapeDtypeStruct(crossed.shape, crossed.dtype),
        ],
        scratch_shapes=[
            pltpu.VMEM((2, members, own, width), parts.dtype),
            pltpu.VMEM((stages,) + stats.shape, jnp.float32),
            pltpu.VMEM((stages,) + stats.shape, jnp.float32),
        ]
        + [sems((2, members, pieces))] * 2
        + [sems((stages,))] * 2
        + [sems((members,))] * 2,
        compiler_params=pltpu.CompilerParams(
            collective_id=collective_id, has_side_effects=True, vmem_limit_bytes=KERNEL_VMEM
        ),
        cost_estimate=cost,
        name="scatter",
    )(parts.reshape(members, own, width), stats, crossed)


def turnaround_body(pieces, *refs):
    parts_ref, resid_all, rate_all, grad_ref, gain_ref, d_resid_ref, sum_ref, out_ref, *refs = refs
    came, resid_ref, rate_ref, low, send_sems, recv_sems, line_send, line_recv, own_sems = refs
    members, own_rows = parts_ref.shape[:2]
    greet(members)
    here = pl.ds(pl.multiple_of(lax.axis_index("fsdp") * own_rows, own_rows), own_rows)
    reads = [
        pltpu.make_async_copy(resid_all.at[here], resid_ref, own_sems.at[1]),
        pltpu.make_async_copy(rate_all.at[here], rate_ref, own_sems.at[2]),
    ]
    for read in reads:
        read.start()
    sums = Sums(parts_ref, came, send_sems, recv_sems, pieces)
    sums.clear()
    line = Line(low, out_ref, line_send, line_recv, pieces)
    sum_ref[...] = jnp.zeros_like(sum_ref)
    for read in reads:
        read.wait()
    for phase in range(pieces + members - 1 + 1):
        if phase < pieces:
            sums.hand_on(phase)
        ready = phase - 1
        if 0 <= ready < pieces:
            here = slice(ready * sums.rows, (ready + 1) * sums.rows)
            dh = sums.total(ready)
            resid, rate = resid_ref[here, :], rate_ref[here, :]
            sum_ref[...] += jnp.sum(dh * resid * rate, axis=0, keepdims=True)
            d_resid = norm_back(
                grad_ref[here, :].astype(jnp.float32), dh, resid, rate, gain_ref[...]
            )
            d_resid_ref[here, :] = d_resid
            low[here, :] = d_resid.astype(low.dtype)
            for way in range(2):
                line.send(1, way, ready)
        for step in range(1, members):
            if 0 <= ready - step < pieces:
                line.hand_on_piece(step, ready - step)
    own = pltpu.make_async_copy(low, out_ref.at[line.member], own_sems.at[0])
    own.start()
    line.finish()
    for piece in range(pieces):
        sums.finish(piece)
    own.wait()


def turnaround(parts, resid, rate, grad, gain, members, collective_id):
    count, width = parts.shape
    own = count // members
    pieces = 12 if own % 192 == 0 else 1
    sems = pltpu.SemaphoreType.DMA
    in_vmem = pl.BlockSpec(memory_space=pltpu.VMEM)
    anywhere = pl.BlockSpec(memory_space=pl.ANY)
    d_resid, gain_part, d_attn = pl.pallas_call(
        functools.partial(turnaround_body, pieces),
        in_specs=[in_vmem, anywhere, anywhere, in_vmem, in_vmem],
        out_specs=[in_vmem, in_vmem, anywhere],
        out_shape=[
            jax.ShapeDtypeStruct((own, width), jnp.float32),
            jax.ShapeDtypeStruct((1, width), jnp.float32),
            jax.ShapeDtypeStruct((members, own, width), jnp.bfloat16),
        ],
        scratch_shapes=[
            pltpu.VMEM((2, members, own, width), parts.dtype),
            pltpu.VMEM((own, width), jnp.float32),
            pltpu.VMEM((own, 1), jnp.float32),
            pltpu.VMEM((own, width), jnp.bfloat16),
        ]
        + [sems((2, members, pieces))] * 2
        + [sems((2, members - 1, pieces))] * 2
        + [sems((3,))],
        compiler_params=pltpu.CompilerParams(
            collective_id=collective_id, has_side_effects=True, vmem_limit_bytes=KERNEL_VMEM
        ),
        name="turnaround",
    )(parts.reshape(members, own, width), resid, rate, grad, gain)
    return d_resid, gain_part[0], d_attn.reshape(count, width)


def unproject_body(*refs):
    grad_refs, weight_refs, refs = refs[:3], refs[3:6], refs[6:]
    tokens_ref, rate_ref, out_ref, sum_ref, *bias_refs = refs
    total = 0.0
    for grad_ref, weight_ref in zip(grad_refs, weight_refs):
        total = total + matmul_nt(grad_ref[...], weight_ref[...])
    out_ref[...] = total.astype(jnp.bfloat16)
    part = total * (tokens_ref[...].astype(jnp.float32) * rate_ref[...])

    @pl.when(pl.program_id(0) == 0)
    def _():
        for ref in (sum_ref, *bias_refs):
            ref[...] = jnp.zeros_like(ref)

    sum_ref[...] += jnp.sum(part, axis=0, keepdims=True)
    for grad_ref, bias_ref in zip(grad_refs, bias_refs):
        bias_ref[...] += jnp.sum(grad_ref[...].astype(jnp.float32), axis=0, keepdims=True)


def unproject(grads, weights, tokens, rates, rows):
    count, width = tokens.shape
    features = grads[0].shape[1]

    def by_rows(cols):
        return pl.BlockSpec((rows, cols), lambda i: (i, 0))

    def whole(*shape):
        return pl.BlockSpec(shape, lambda i: (0, 0))

    return pl.pallas_call(
        unproject_body,
        grid=(count // rows,),
        in_specs=[by_rows(features)] * 3
        + [whole(width, features)] * 3
        + [by_rows(width), by_rows(1)],
        out_specs=[by_rows(width), whole(1, width)] + [whole(1, features)] * 3,
        out_shape=[
            jax.ShapeDtypeStruct((count, width), jnp.bfloat16),
            jax.ShapeDtypeStruct((1, width), jnp.float32),
        ]
        + [jax.ShapeDtypeStruct((1, features), jnp.float32)] * 3,
        compiler_params=pltpu.CompilerParams(vmem_limit_bytes=KERNEL_VMEM),
        cost_estimate=NO_COST,
        name="unproject",
    )(*grads, *weights, tokens, rates)


def attend_grads_body(rows_ref, d_query, d_key, d_value, *outs):
    rows = rows_ref[...].T
    for d_ref, out in zip((d_query, d_key, d_value), outs):
        out[...] = matmul(rows, d_ref[...]).astype(jnp.bfloat16)


def attend_grads(rows, d_pres, cut):
    count, width = rows.shape
    features = d_pres[0].shape[1]
    whole = pl.BlockSpec((count, features), lambda i: (0, 0))
    tall = pl.BlockSpec((cut, features), lambda i: (i, 0))
    return pl.pallas_call(
        attend_grads_body,
        grid=(width // cut,),
        in_specs=[pl.BlockSpec((count, cut), lambda i: (0, i))] + [whole] * 3,
        out_specs=[tall] * 3,
        out_shape=[jax.ShapeDtypeStruct((width, features), jnp.bfloat16)] * 3,
        compiler_params=pltpu.CompilerParams(vmem_limit_bytes=KERNEL_VMEM),
        cost_estimate=NO_COST,
        name="attend_grads",
    )(rows, *d_pres)


def turn_body(piece_ref, out_ref):
    out_ref[...] = piece_ref[0].astype(jnp.float32).T


def turn(pieces):
    members, rows, features = pieces.shape
    if rows % 128:
        return pieces.reshape(members * rows, features).astype(jnp.float32).T
    return pl.pallas_call(
        turn_body,
        grid=(members,),
        in_specs=[pl.BlockSpec((1, rows, features), lambda i: (i, 0, 0))],
        out_specs=pl.BlockSpec((features, rows), lambda i: (0, i)),
        out_shape=jax.ShapeDtypeStruct((features, members * rows), jnp.float32),
        compiler_params=pltpu.CompilerParams(vmem_limit_bytes=KERNEL_VMEM),
        name="turn",
    )(pieces)


def shards(
    tokens,
    routes,
    seq_lengths,
    cotangent,
    norm1_gain,
    query_weight,
    query_bias,
    key_weight,
    key_bias,
    value_weight,
    value_bias,
    out_weight,
    norm2_gain,
    router_weight,
    shared_switch,
    shared_gate,
    shared_up,
    shared_down,
    expert_gate,
    expert_up,
    expert_down,
):
    own_count = tokens.shape[0]
    width = tokens.shape[1]
    members = lax.axis_size("fsdp")
    columns = lax.axis_size("expert")
    member = lax.axis_index("fsdp")
    own_start = member * own_count
    count = own_count * members
    experts_count = router_weight.shape[1]
    local_experts = experts_count // members
    capacity = 4 * own_count * TOP // (3 * experts_count)

    def own_rows(values):
        return lax.dynamic_slice_in_dim(values, own_start, own_count, 0)

    def take(pieces, place):
        return lax.dynamic_index_in_dim(pieces, place, 0, keepdims=False)

    def put(pieces, piece, place):
        return lax.dynamic_update_index_in_dim(pieces, piece, place, 0)

    def after(value, other):
        return lax.optimization_barrier((value, other))[0]

    def one_hop(low, high, step):
        upward = [(m, m + 1) for m in range(step - 1, members - 1)]
        downward = [(members - 1 - m, members - 2 - m) for m in range(step - 1, members - 1)]
        return lax.ppermute(low, "fsdp", upward), lax.ppermute(high, "fsdp", downward)

    def line_gather(block, first, ties, last):
        from_low, from_high = [block, first[0]], [block, first[1]]
        for step in range(2, members):
            from_low[-1], from_high[-1] = after(
                (from_low[-1], from_high[-1]), ties[min(step - 2, len(ties) - 1)]
            )
            low, high = one_hop(from_low[-1], from_high[-1], step)
            from_low.append(low)
            from_high.append(high)
        from_low[-1], from_high[-1] = after((from_low[-1], from_high[-1]), last)
        window = jnp.concatenate(from_low[:0:-1] + [block] + from_high[1:], axis=0)
        size = block.shape[0]
        return lax.dynamic_slice_in_dim(window, (members - 1 - member) * size, members * size, 0)

    def relay(parts, step, sums=None):
        blocks = parts.reshape((members, -1) + parts.shape[1:])
        up_block = take(blocks, jnp.minimum(members - step + member, members - 1))
        down_block = take(blocks, jnp.maximum(member - (members - step), 0))
        if sums is not None:
            up_block, down_block = (
                (block.astype(jnp.float32) + came.astype(jnp.float32)).astype(parts.dtype)
                for block, came in zip((up_block, down_block), sums)
            )
        up_pairs = [(m, m + 1) for m in range(step)]
        down_pairs = [(members - 1 - m, members - 2 - m) for m in range(step)]
        return (
            lax.ppermute(up_block, "fsdp", up_pairs),
            lax.ppermute(down_block, "fsdp", down_pairs),
        )

    column = lax.axis_index("expert")

    def weights_whole(piece):
        gathered = lax.all_gather(piece, "expert", axis=0, tiled=False)
        return gathered.reshape(local_experts, width, -1)

    group_tokens, group_routes, crossed = arrive(
        tokens,
        routes.T,
        (expert_gate[0], expert_up[0], expert_down[0].T),
        members,
        local_experts,
    )
    out_piece_rows = out_weight.shape[0] // columns
    out_piece = lax.dynamic_slice_in_dim(out_weight, column * out_piece_rows, out_piece_rows, 0)
    out_full = lax.all_gather(out_piece, ("fsdp", "expert"), axis=0, tiled=True)
    gate_mats, up_mats, down_mats = (weights_whole(piece) for piece in crossed)

    segment, positions = token_layout(seq_lengths[0], count)
    block = math.gcd(count, 256)
    starts = jnp.arange(count, dtype=jnp.int32) - positions
    lows = starts[::block] // block
    starts = starts[None]
    cosine, sine = rotary_tables(positions, HEAD_DIM)
    tokens_own_wide = tokens.astype(jnp.float32)
    gain_first = norm1_gain.astype(jnp.float32)
    normed_first, rate_first, queries, keys_all, values_all = project(
        group_tokens,
        gain_first[None],
        (query_weight, key_weight, value_weight),
        [bias.astype(jnp.float32)[None] for bias in (query_bias, key_bias, value_bias)],
        cosine,
        sine,
        block,
    )
    attended, log_mass = attend(lows, starts, queries, keys_all, values_all, block)
    cot_tied = after(cotangent, group_tokens)
    attended, cot_hop = lax.optimization_barrier((attended, one_hop(cot_tied, cot_tied, 1)))
    attended_by_member = gather(attended, members, math.gcd(count // 16, 4), 1)
    tokens_wide = group_tokens.astype(jnp.float32)
    gain_second = norm2_gain.astype(jnp.float32)
    small_count = experts_count + 1
    small_weight = jnp.concatenate([router_weight, shared_switch[:, None]], axis=1)
    small_wide = jnp.pad(small_weight, ((0, 0), (0, 128 - small_count)))
    resid_mid, rate_second, normed_second, small_pre = settle(
        group_tokens, attended_by_member, out_full, gain_second[None], small_wide, block
    )
    resid_own = own_rows(resid_mid)

    router_probs = jax.nn.softmax(small_pre[:, :experts_count], axis=-1)
    switch_all = jax.nn.sigmoid(small_pre[:, experts_count:small_count])
    own_ids = member * local_experts + jnp.arange(local_experts, dtype=jnp.int32)
    gates = lax.dynamic_slice_in_dim(router_probs, member * local_experts, local_experts, 1)
    hot = jnp.sum(
        (group_routes[:, :, None, :] == own_ids[None, None, :, None]).astype(jnp.float32), axis=1
    )
    order = jnp.arange(own_count, dtype=jnp.int32)
    before = (order[:, None] > order[None, :]).astype(jnp.bfloat16)
    ranks = jnp.einsum(
        "ut,bjt->bju", before, hot.astype(jnp.bfloat16), preferred_element_type=jnp.float32
    ).astype(jnp.int32)
    places_turned = jnp.where(hot > 0.0, ranks, -1)
    places = places_turned.transpose(0, 2, 1)
    slots = jnp.arange(capacity, dtype=jnp.int32)
    picks = places_turned[:, :, None, :] == slots[None, None, :, None]
    gates_turned = gates.reshape(members, own_count, local_experts).transpose(0, 2, 1)
    slot_gates = jnp.sum(jnp.where(picks, gates_turned[:, :, None, :], 0.0), axis=-1)
    slot_gates = slot_gates.transpose(1, 0, 2).reshape(local_experts, members * capacity, 1)
    places = places.reshape(count, local_experts)

    shared_weights = (shared_gate[None], shared_up[None], shared_down[None])
    shared_out, shared_mid, shared_silu, shared_slope = expert(
        normed_second[None], switch_all[None], *shared_weights, False, block
    )
    group_cot = line_gather(
        cotangent, cot_hop, (attended_by_member, normed_second), shared_mid
    )
    row_count = members * capacity
    row_block = math.gcd(row_count, 256)
    rows = dispatch(places_turned, after(normed_second, shared_mid), capacity, members)

    grad_wide = group_cot.astype(jnp.float32)
    down_grad = matmul_tn(shared_mid[0], (switch_all * grad_wide).astype(jnp.bfloat16)).astype(
        jnp.bfloat16
    )
    down_sum = lax.psum(down_grad, "expert")
    switch_dot, _, d_shared_gate, d_shared_up, dh_shared = expert_back(
        after(group_cot, down_grad)[None],
        shared_out,
        switch_all[None],
        shared_silu,
        shared_slope,
        *shared_weights,
        False,
        block,
    )
    switch_logit = switch_dot[0] * switch_all * (1.0 - switch_all)
    shared_grads = tuple(
        pair_grads(normed_second, d_shared_gate[0], d_shared_up[0], math.gcd(width, 512))
    )
    shared_sums = lax.psum(shared_grads, "expert")

    result, expert_mid, expert_silu, expert_slope, scaled = expert(
        after(rows, shared_grads), slot_gates, gate_mats, up_mats, down_mats, True, row_block
    )
    by_block = (local_experts, members, capacity, width)
    block_low = collect(places, scaled.reshape(by_block), shared_out[0], members, switch_all)
    slot_dot, d_rows, d_expert_gate, d_expert_up, d_in = expert_back(
        dispatch(places_turned, after(group_cot, block_low), capacity, members),
        result,
        slot_gates,
        expert_silu,
        expert_slope,
        gate_mats,
        up_mats,
        down_mats,
        True,
        row_block,
    )
    block_sums = relay(block_low, 1)
    expert_grads = weight_grads(
        after(rows, block_sums), d_rows, d_expert_gate, d_expert_up, expert_mid, members
    )
    block_sums = relay(block_low, 2, after(block_sums, d_in))
    slot_dot, block_sums, expert_grads = lax.optimization_barrier(
        (slot_dot, block_sums, expert_grads)
    )
    for step in range(3, members):
        block_sums = relay(block_low, step, block_sums)
    expert_pieces = lax.psum_scatter(
        expert_grads.reshape((columns, 3) + expert_grads.shape[3:]),
        "expert",
        scatter_dimension=0,
        tiled=True,
    ).reshape(3, members, -1, expert_grads.shape[-1])
    slot_dots = slot_dot.reshape(local_experts, members, capacity).transpose(1, 0, 2)
    d_gates = jnp.sum(jnp.where(picks, slot_dots[:, :, :, None], 0.0), axis=2)
    d_gates = d_gates.transpose(0, 2, 1).reshape(count, local_experts)
    ids = jnp.arange(experts_count, dtype=jnp.int32)
    d_choice = sum(
        jnp.where(ids[None, :] == own_ids[which], d_gates[:, which : which + 1], 0.0)
        for which in range(local_experts)
    )
    d_logits = router_probs * (d_choice - jnp.sum(gates * d_gates, axis=-1, keepdims=True))
    d_small = jnp.concatenate([d_logits, switch_logit], axis=1)
    d_small_high = d_small.astype(jnp.bfloat16)
    d_small_low = (d_small - d_small_high.astype(jnp.float32)).astype(jnp.bfloat16)
    d_small_both = jnp.pad(
        jnp.concatenate([d_small_high, d_small_low], axis=1),
        ((0, 0), (0, 128 - 2 * small_count)),
    )
    small_both = jnp.pad(
        jnp.concatenate([small_weight.T, small_weight.T], axis=0),
        ((0, 128 - 2 * small_count), (0, 0)),
    )
    dh_low = collect(
        places,
        after(d_in, (expert_grads, shared_sums, down_sum)).reshape(by_block),
        dh_shared[0],
        members,
        d_small_both,
        small_both,
    )
    small_part = matmul_tn(normed_second, d_small_both)
    small_part = small_part[:, :small_count] + small_part[:, small_count : 2 * small_count]

    d_resid_own, norm2_part, d_attn_out = turnaround(
        dh_low,
        resid_mid,
        rate_second,
        cotangent,
        gain_second[None],
        members,
        2,
    )
    d_attn_out, block_sums = lax.optimization_barrier((d_attn_out, block_sums))
    d_context = matmul_nt(d_attn_out, out_weight).astype(jnp.bfloat16)
    out_sum = lax.psum(matmul_tn(attended, d_attn_out).astype(jnp.bfloat16), "expert")
    d_query_pre, d_key_pre, d_value_pre = attend_back(
        lows,
        starts,
        queries,
        keys_all,
        values_all,
        d_context,
        log_mass,
        cosine,
        sine,
        block,
    )

    expert_pieces = expert_pieces.transpose(1, 0, 2, 3)

    def cross(step, tie):
        return lax.ppermute(
            after(take(expert_pieces, (member + step) % members), tie),
            "fsdp",
            [(m, (m + step) % members) for m in range(members)],
        )

    arrived = [cross(step, d_attn_out) for step in range(1, members - 1)]
    d_query_pre, arrived[0] = lax.optimization_barrier((d_query_pre, arrived[0]))
    attn_grads = attend_grads(
        normed_first, (d_query_pre, d_key_pre, d_value_pre), math.gcd(width, 512)
    )
    attn_grads, out_sum = lax.optimization_barrier((attn_grads, out_sum))
    arrived.append(cross(members - 1, d_query_pre))
    d_pres, arrived[1:-1] = after(
        ((d_query_pre, d_key_pre, d_value_pre), arrived[1:-1]), attn_grads
    )
    dh_first_low, norm1_part, *biases = unproject(
        d_pres, (query_weight, key_weight, value_weight), group_tokens, rate_first, block
    )
    norm1_part = norm1_part[0]
    crossed_grads = expert_pieces
    for step, piece in enumerate(arrived, 1):
        crossed_grads = put(crossed_grads, piece, (member - step) % members)

    shared_sums, down_sum, out_sum, block_low, block_sums = after(
        (shared_sums, down_sum, out_sum, block_low, block_sums), dh_first_low
    )
    out_grad = out_sum.astype(jnp.float32)
    block_out = resid_own + own_rows(block_low).astype(jnp.float32)
    for came in block_sums:
        block_out = block_out + came.astype(jnp.float32)
    block_out = block_out.astype(jnp.bfloat16)
    shared_out_grads = [
        grad.astype(jnp.float32) for grad in (shared_sums[0], shared_sums[1], down_sum)
    ]
    line_parts = jnp.concatenate([norm1_part, norm2_part, small_part.T.reshape(-1)])
    stats = jnp.concatenate([line_parts] + [bias[0] for bias in biases]).reshape(-1, 128)
    dh_first_own, stats, mixed_grads = scatter(
        after(dh_first_low, (attn_grads, shared_out_grads, out_grad, block_out)),
        jnp.pad(stats, ((0, -stats.shape[0] % 8), (0, 0))),
        crossed_grads,
        line_parts.shape[0] // 128,
        members,
        columns,
        4,
        LONG_COST,
    )
    stats = stats.reshape(-1)
    grad_tokens = norm_back(
        d_resid_own, dh_first_own, tokens_own_wide, own_rows(rate_first), gain_first
    )

    small_sum = stats[2 * width : (2 + small_count) * width].reshape(-1, width)
    bias_end = line_parts.shape[0] + 3 * biases[0].shape[1]
    bias_sums = stats[line_parts.shape[0] : bias_end].reshape(3, -1)

    attn_sums = after(lax.psum(attn_grads, "expert"), dh_first_own)
    expert_sums = [mixed_grads[:, kind] for kind in range(3)]

    return (
        block_out,
        grad_tokens,
        stats[:width],
        attn_sums[0].astype(jnp.float32),
        bias_sums[0],
        attn_sums[1].astype(jnp.float32),
        bias_sums[1],
        attn_sums[2].astype(jnp.float32),
        bias_sums[2],
        out_grad,
        stats[width : 2 * width],
        small_sum[:experts_count].T,
        small_sum[experts_count],
        shared_out_grads[0],
        shared_out_grads[1],
        shared_out_grads[2],
        expert_sums[0].reshape(1, width // members, -1).astype(jnp.float32),
        expert_sums[1].reshape(1, width // members, -1).astype(jnp.float32),
        turn(expert_sums[2])[None],
    )


def solution(mesh):
    placed = (
        P(("expert", "fsdp"), None),
        P(("expert", "fsdp"), None),
        P("expert", None),
        P(("expert", "fsdp"), None),
        P(),
        P(None, "fsdp"),
        P("fsdp"),
        P(None, "fsdp"),
        P("fsdp"),
        P(None, "fsdp"),
        P("fsdp"),
        P("fsdp", None),
        P(),
        P(),
        P(),
        P(None, "fsdp"),
        P(None, "fsdp"),
        P("fsdp", None),
        P("expert", "fsdp", None),
        P("expert", "fsdp", None),
        P("expert", None, "fsdp"),
    )
    return jax.shard_map(
        shards,
        mesh=mesh,
        in_specs=placed,
        out_specs=(
            P(("expert", "fsdp"), None),
            P(("expert", "fsdp"), None),
            P(),
            P(None, "fsdp"),
            P("fsdp"),
            P(None, "fsdp"),
            P("fsdp"),
            P(None, "fsdp"),
            P("fsdp"),
            P("fsdp", None),
            P(),
            P(),
            P(),
            P(None, "fsdp"),
            P(None, "fsdp"),
            P("fsdp", None),
            P("expert", "fsdp", None),
            P("expert", "fsdp", None),
            P("expert", None, "fsdp"),
        ),
        check_vma=False,
    )
```
